256 devices in a mesh: section: 16 (over z, core), dp: 16 (over x, y).
Axes of the slice: x: 4, y: 4, z: 8, core: 2. Of those that a mesh axis runs over, the one named last changes fastest.
Arguments:
- tokens: bfloat16 [16, 192, 4096], P('dp'), may hold values from -6 to 6
- upstream: bfloat16 [16, 192, 4096], P('dp'), may hold values from -6 to 6
- gains: bfloat16 [16, 4096], P('section'), may hold values from 0.5 to 1.5
- w_kv: bfloat16 [16, 4096, 1024], P('section'), may hold values from -0.09375 to 0.09375
- doc_lengths: int32 [16, 4], P('dp'), may hold values from 1 to 96, 192 in all within a row
- seg_lengths: int32 [16, 4], P('dp'), may hold values from 1 to 60, 192 in all within a row
- block_mask: int32 [16, 12, 12], P('dp'), may hold values 0 or 1
Outputs:
- grad_kv: float32 [16, 4096, 1024], P('section', 'dp')
- grad_gain: float32 [16, 4096], P('section', 'dp')
The draws below stay inside these ranges and needn't reach their ends.
Inputs may be any that keep to these rules, and one draw needn't show every extreme that they name: `doc_lengths`: each row sums to 192. `seg_lengths`: each row sums to 192.
All inputs are finite; a program needn't handle non-finite values. No bound on the sum of `block_mask` on one device may be relied on, other than what follows from the above.
Results may differ from the reference program's by a relative error of at most 0.035.
Values may be sent and summed in bfloat16 or wider, within the bound.
A program may use at most 128 MiB of HBM per device.

```python
import math
import jax
import jax.numpy as jnp
import numpy as np
from jax import lax

KV_HEADS = 4
HEAD_DIM = 128
SEGS = 4
BLK = 16
DOCS = 4
SEQ = 192
D = 4096
GROUP = 8
KV = 512
SEGMAX = 60
DOCMAX = 96
NB = 12
SEQS = 16
N_SECTION = 16


def place_ends(values, stream_key, low, high):
    longest = values.shape.index(max(values.shape))
    spots = []
    for shift in (0, 1):
        where = [jax.random.randint(jax.random.fold_in(stream_key, axis), (), 0, length) for axis, length in enumerate(values.shape)]
        where[longest] = (where[longest] + shift) % values.shape[longest]
        spots.append(tuple(where))
    return values.at[spots[0]].set(low).at[spots[1]].set(high)


def raised(entries, key, source, target, parts, factor):
    owner, partner = [(jnp.arange(entries.shape[axis_at]) // (entries.shape[axis_at] // parts)).reshape([-1 if axis == axis_at else 1 for axis in range(entries.ndim)]) for axis_at in (source, target)]
    chosen = jax.random.permutation(key, parts)[partner]
    strong = (owner == chosen) | (owner == (partner + parts // 2) % parts)
    return jnp.where(strong, factor * entries, entries)


def shard_levels(stream_key, shape, split, smallest, top_value):
    def one(axis_at, shards_of):
        heights = jax.random.uniform(jax.random.fold_in(jax.random.fold_in(stream_key, 6), axis_at), (shards_of,), jnp.float32, smallest / len(split), top_value / len(split))
        return jnp.repeat(jnp.exp(heights), shape[axis_at] // shards_of).reshape((-1,) + (1,) * (len(shape) - axis_at - 1))

    level = one(*split[0])
    for cut in split[1:]:
        level = level * one(*cut)
    return level


def split_up(count, total, bound, slope):
    weights = [(1 << 20) // math.isqrt(standing ** slope) + 1 for standing in range(2, count + 1)]
    surplus, holding = total - bound - (count - 1), [1] * (count - 1)
    while surplus > 0:
        free = [i for i in range(count - 1) if holding[i] < bound]
        mass, left = sum([weights[i] for i in free]), surplus
        for i in free:
            extra = min(bound - holding[i], max(1, left * weights[i] // mass), surplus)
            holding[i] = holding[i] + extra
            surplus = surplus - extra
    return np.array([bound] + holding)


def uneven_parts(stream_key, amount, total, limit, lean):
    if amount == 2:
        one = jax.random.randint(stream_key, (), max(1, total - limit), min(limit, total - 1) + 1)
        return jnp.stack([one, total - one])
    sizes = jnp.asarray(split_up(amount, total, limit, lean), jnp.int32)
    couples = (amount - 1) // 2
    giver, receiver = sizes[1:1 + 2 * couples:2], sizes[2:2 + 2 * couples:2]
    slack = jnp.minimum(giver - 1, limit - receiver)
    moved = jax.random.randint(jax.random.fold_in(stream_key, 1), (couples,), 0, 1 << 20) % (slack + 1)
    sizes = sizes.at[1:1 + 2 * couples:2].set(giver - moved).at[2:2 + 2 * couples:2].set(receiver + moved)
    return sizes[jax.random.permutation(jax.random.fold_in(stream_key, 2), amount)]


def normal_values(rng, shape, width, most, cuts=(), held_as=jnp.bfloat16):
    array = jax.random.normal(rng, shape, jnp.float32) * width
    if len(cuts) > 0:
        array = shard_levels(rng, shape, cuts, -0.22, 0.18) * array
    return jnp.clip(array, min=-most, max=most).astype(held_as)


def bell_draw_with(stream_key, shape, spread, limit, split, heavy, kind=jnp.bfloat16):
    array = spread * jax.random.normal(stream_key, shape, jnp.float32)
    if split:
        array = array * shard_levels(stream_key, shape, split, -0.22, 0.18)
    return jnp.clip(raised(array, jax.random.fold_in(stream_key, 3), *heavy), -limit, limit).astype(kind)


def setup_inputs(seed: int = 0) -> dict:
    streams_of = jax.random.split(jax.random.key(seed), 8)
    tokens = bell_draw_with(streams_of[0], (SEQS, SEQ, D), 1.0, 6.0, ((0, 16),), (0, 2, 16, 2.0))
    upstream = normal_values(streams_of[1], (SEQS, SEQ, D), 1.0, 6.0, ((0, 16),))
    gains = jnp.clip(1.0 + 0.1 * jax.random.normal(streams_of[2], (N_SECTION, D), jnp.float32), 0.5, 1.5).astype(jnp.bfloat16)
    w_kv = normal_values(streams_of[3], (N_SECTION, D, 2 * KV), D ** -0.5, 0.09375, ((0, 16),))
    doc_lengths = jax.vmap(lambda own: uneven_parts(own, DOCS, SEQ, DOCMAX, 1))(jax.random.split(streams_of[4], SEQS)).reshape((SEQS, DOCS)).astype(jnp.int32)
    seg_lengths = jax.vmap(lambda own: uneven_parts(own, SEGS, SEQ, SEGMAX, 1))(jax.random.split(streams_of[5], SEQS)).reshape((SEQS, SEGS)).astype(jnp.int32)
    block_mask = place_ends((jax.random.randint(streams_of[6], (SEQS, NB, NB), 0, 4) < 3).astype(jnp.int32), jax.random.fold_in(streams_of[6], 1), 0, 1)
    return {"tokens": tokens, "upstream": upstream, "gains": gains, "w_kv": w_kv, "doc_lengths": doc_lengths, "seg_lengths": seg_lengths, "block_mask": block_mask}


EPSILON = 1e-06

def rounded(values):
    return lax.optimization_barrier(values.astype(jnp.bfloat16))

def allowed_mask(doc_row, block_table):
    positions = jnp.arange(SEQ, dtype=jnp.int32)
    doc_ends = jnp.cumsum(doc_row)
    doc_ids = lax.optimization_barrier(jnp.sum((positions[:, None] >= doc_ends[None, :]).astype(jnp.int32), 1))
    block_ids = positions // BLK
    block_open = block_table[block_ids][:, block_ids] == 1
    same_block = block_ids[:, None] == block_ids[None, :]
    causal = positions[None, :] <= positions[:, None]
    return causal & (doc_ids[:, None] == doc_ids[None, :]) & (block_open | same_block)

def normalize(inputs):
    values = inputs.astype(jnp.float32)
    inverse = lax.rsqrt(lax.optimization_barrier(jnp.mean(values * values, -1, keepdims=True)) + EPSILON)
    return (values, inverse, values * inverse)

def attention_probs(hidden, key_values, allowed):
    scale = HEAD_DIM ** (-0.5)
    query = hidden.astype(jnp.float32).reshape(SEQ, KV_HEADS, GROUP, HEAD_DIM)
    key_part = key_values[:, :KV].astype(jnp.float32).reshape(SEQ, KV_HEADS, HEAD_DIM)
    value_part = key_values[:, KV:].astype(jnp.float32).reshape(SEQ, KV_HEADS, HEAD_DIM)
    scores = jnp.einsum('ikgd,jkd->kgij', query, key_part) * scale
    raw_probs = jnp.where(allowed[None, None], jnp.exp(scores), 0.0)
    probs = raw_probs / lax.optimization_barrier(jnp.sum(raw_probs, -1, keepdims=True))
    return (query, key_part, value_part, probs, rounded(probs))

def layer_pieces(inputs, gain_row, weight, allowed):
    values, inverse, normed = normalize(inputs)
    hidden = rounded(normed * gain_row.astype(jnp.float32))
    key_values = rounded(jnp.dot(hidden, weight, preferred_element_type=jnp.float32))
    return (values, inverse, normed, hidden, key_values)

def forward_one(inputs, gain_row, weight, allowed):
    values, inverse, normed, hidden, key_values = layer_pieces(inputs, gain_row, weight, allowed)
    query, key_part, value_part, probs, probs_low = attention_probs(hidden, key_values, allowed)
    mixed = jnp.einsum('kgij,jkd->ikgd', probs_low.astype(jnp.float32), value_part).reshape(SEQ, D)
    return (values + mixed).astype(jnp.bfloat16)

def backward_one(inputs, grads_in, gain_row, weight, allowed):
    scale = HEAD_DIM ** (-0.5)
    values, inverse, normed, hidden, key_values = layer_pieces(inputs, gain_row, weight, allowed)
    query, key_part, value_part, probs, probs_low = attention_probs(hidden, key_values, allowed)
    grad_out = grads_in.astype(jnp.float32).reshape(SEQ, KV_HEADS, GROUP, HEAD_DIM)
    d_probs = jnp.einsum('ikgd,jkd->kgij', grad_out, value_part)
    d_scores = probs * (d_probs - lax.optimization_barrier(jnp.sum(probs * d_probs, -1, keepdims=True)))
    d_low = rounded(d_scores * scale).astype(jnp.float32)
    d_query = jnp.einsum('kgij,jkd->ikgd', d_low, key_part).reshape(SEQ, D)
    d_keys = jnp.einsum('kgij,ikgd->jkd', d_low, query).reshape(SEQ, KV)
    d_values = jnp.einsum('kgij,ikgd->jkd', probs_low.astype(jnp.float32), grad_out).reshape(SEQ, KV)
    d_kv = rounded(jnp.concatenate([d_keys, d_values], 1))
    d_hidden = d_query + jnp.dot(d_kv, weight.T, preferred_element_type=jnp.float32)
    weight_part = rounded(jnp.dot(hidden.T, d_kv, preferred_element_type=jnp.float32))
    gain_part = rounded(lax.optimization_barrier(jnp.sum(d_hidden * normed, 0)))
    d_normed = d_hidden * gain_row.astype(jnp.float32)
    d_inputs = inverse * (d_normed - normed * lax.optimization_barrier(jnp.mean(d_normed * normed, -1, keepdims=True)))
    grads_out = (grads_in.astype(jnp.float32) + d_inputs).astype(jnp.bfloat16)
    return (grads_out, weight_part, gain_part)

def first_grads(upstream_row, seg_row):
    positions = jnp.arange(SEQ, dtype=jnp.int32)
    seg_ends = jnp.cumsum(seg_row)
    seg_ids = lax.optimization_barrier(jnp.sum((positions[:, None] >= seg_ends[None, :]).astype(jnp.int32), 1))
    seg_sizes = seg_row[seg_ids].astype(jnp.float32)
    factor = SEQ / (SEGS * seg_sizes)
    return (upstream_row.astype(jnp.float32) * factor[:, None]).astype(jnp.bfloat16)

def reference(tokens, upstream, gains, w_kv, doc_lengths, seg_lengths, block_mask):
    allowed = jax.vmap(allowed_mask)(doc_lengths, block_mask)

    def forward_section(current, params):
        gain_row, weight = params
        produced = jax.vmap(lambda rows, mask_rows: forward_one(rows, gain_row, weight, mask_rows))(current, allowed)
        return (produced, current)
    unused, section_inputs = lax.scan(forward_section, tokens, (gains, w_kv))
    start_grads = jax.vmap(first_grads)(upstream, seg_lengths)

    def backward_section(grads_in, params):
        gain_row, weight, inputs = params
        grads_out, weight_parts, gain_parts = jax.vmap(lambda rows, grad_rows, mask_rows: backward_one(rows, grad_rows, gain_row, weight, mask_rows))(inputs, grads_in, allowed)
        return (grads_out, (lax.optimization_barrier(jnp.sum(weight_parts.astype(jnp.float32), 0)), lax.optimization_barrier(jnp.sum(gain_parts.astype(jnp.float32), 0))))
    unused_grads, (grad_kv, grad_gain) = lax.scan(backward_section, start_grads, (gains, w_kv, section_inputs), reverse=True)
    return (grad_kv, grad_gain)
```

```python
import functools
import math

import jax
import jax.numpy as jnp
from jax import lax
from jax.experimental import pallas as pl
from jax.experimental.pallas import tpu as pltpu
from jax.sharding import PartitionSpec as P

HEADS = 32
KV_HEADS = 4
GROUP = 8
HEAD_DIM = 128
SEGS = 4
BLK = 16
EPSILON = 1e-06

T = 32
WINDOW = 128
PAD = WINDOW - T
CHUNK = GROUP * HEAD_DIM
MESH = pl.DeviceIdType.MESH
F32 = jnp.float32
BF16 = jnp.bfloat16
EXP_SCALE = HEAD_DIM**-0.5 * math.log2(math.e)
SCALE = HEAD_DIM**-0.5


def to_rows(block):
    return jnp.concatenate(
        [block[:, HEAD_DIM * g : HEAD_DIM * (g + 1)] for g in range(GROUP)], axis=0
    )


def to_lanes(block):
    return jnp.concatenate([block[T * g : T * (g + 1)] for g in range(GROUP)], axis=1)


def fold_lanes(block):
    total = block[:, :128]
    for g in range(1, block.shape[1] // 128):
        total = total + block[:, 128 * g : 128 * (g + 1)]
    return total


def dot_t(a, b):
    return lax.dot_general(a, b, (((1,), (1,)), ((), ())), preferred_element_type=F32)


def t_dot(a, b):
    return lax.dot_general(a, b, (((0,), (0,)), ((), ())), preferred_element_type=F32)


def dot(a, b):
    return jnp.dot(a, b, preferred_element_type=F32)


def kernel(
    n_sec,
    n_dp,
    tok,
    ups,
    gain,
    w,
    bias,
    fac,
    out_w,
    out_g,
    xb,
    hb,
    gb,
    xo,
    go,
    wb,
    kvb,
    dacc,
    pb,
    dqb,
    rb,
    gf,
    gsum,
    gs,
    hg,
    dg,
    gg,
    w_sem,
    in_sem,
    f_send,
    f_recv,
    g_send,
    g_recv,
    h_send,
    h_recv,
    d_send,
    d_recv,
    s_send,
    s_recv,
):
    sec = lax.axis_index("section")
    me = lax.axis_index("dp")
    seq_len = xb.shape[1]
    pieces = seq_len // T
    width = KV_HEADS * CHUNK
    kv_width = KV_HEADS * HEAD_DIM
    block = width // n_dp
    first = sec == 0
    last = sec == n_sec - 1

    w_copies = [
        pltpu.make_async_copy(w.at[0, pl.ds(k * CHUNK, CHUNK)], wb.at[k], w_sem.at[k])
        for k in range(KV_HEADS)
    ]
    tok_copies = [
        pltpu.make_async_copy(tok.at[0, :, pl.ds(k * CHUNK, CHUNK)], xb.at[k], in_sem.at[k])
        for k in range(KV_HEADS)
    ]
    ups_copies = [
        pltpu.make_async_copy(ups.at[0, :, pl.ds(k * CHUNK, CHUNK)], xo.at[k], in_sem.at[k])
        for k in range(KV_HEADS)
    ]

    @pl.when(first)
    def _():
        for copy in tok_copies:
            copy.start()

    for copy in w_copies:
        copy.start()

    @pl.when(last)
    def _():
        for copy in ups_copies:
            copy.start()

    barrier = pltpu.get_barrier_semaphore()

    for neighbour in ((sec + 1) % n_sec, (sec + n_sec - 1) % n_sec):
        pl.semaphore_signal(
            barrier, inc=1, device_id={"section": neighbour}, device_id_type=MESH
        )
    for j in range(1, n_dp):
        pl.semaphore_signal(
            barrier, inc=1, device_id={"dp": (me + j) % n_dp}, device_id_type=MESH
        )

    kvb[pl.ds(0, PAD), :] = jnp.zeros((PAD, 2 * kv_width), BF16)
    dacc[...] = jnp.zeros_like(dacc)
    gsum[...] = jnp.zeros_like(gsum)
    for k in range(KV_HEADS):
        gf[k] = jnp.broadcast_to(
            gain[:, pl.ds(k * CHUNK, CHUNK)].astype(F32), (8, CHUNK)
        )

    @pl.when(last)
    def _():
        for copy in ups_copies:
            copy.wait()

        def scale_piece(p, carry):
            rows = pl.ds(pl.multiple_of(p * T, T), T)
            factor = fac[rows, :][:, :1]
            for k in range(KV_HEADS):
                gb[k, rows, :] = (xo[k, rows, :].astype(F32) * factor).astype(BF16)
            return carry

        lax.fori_loop(0, pieces, scale_piece, 0)

    for copy in w_copies:
        copy.wait()

    @pl.when(first)
    def _():
        for copy in tok_copies:
            copy.wait()

    pl.semaphore_wait(barrier, n_dp + 1)

    def forward(p, carry):
        start = pl.multiple_of(p * T, T)
        rows = pl.ds(start, T)
        acc = jnp.zeros((T, 2 * kv_width), F32)
        squares = jnp.zeros((T, 128), F32)
        for k in range(KV_HEADS):
            arrival = pltpu.make_async_remote_copy(
                src_ref=xb.at[k, rows],
                dst_ref=xb.at[k, rows],
                send_sem=f_send,
                recv_sem=f_recv.at[p, k],
                device_id={"section": sec},
                device_id_type=MESH,
            )

            @pl.when(sec > 0)
            def _():
                arrival.wait_recv()

            values = xb[k, rows, :].astype(F32)
            squares = squares + fold_lanes(values * values)
            acc = acc + dot((values * gf[k, 0:1, :]).astype(BF16), wb[k])
        inverse = lax.rsqrt(jnp.sum(squares, -1, keepdims=True) / width + EPSILON)
        rb[rows, :] = jnp.broadcast_to(inverse, (T, 128))
        kvb[pl.ds(pl.multiple_of(start + PAD, T), T), :] = (acc * inverse).astype(BF16)
        window = pl.ds(start, WINDOW)
        bias_rows = jnp.concatenate([bias[p]] * GROUP, axis=0)
        for k in range(KV_HEADS):
            values = xb[k, rows, :].astype(F32)
            hidden = (values * inverse * gf[k, 0:1, :]).astype(BF16)
            hb[k, rows, :] = hidden
            keys = kvb[window, pl.ds(k * HEAD_DIM, HEAD_DIM)]
            vals = kvb[window, pl.ds(kv_width + k * HEAD_DIM, HEAD_DIM)]
            scores = dot_t(to_rows(hidden), keys)
            raw = jnp.exp2(scores * EXP_SCALE + bias_rows)
            share = 1.0 / jnp.sum(raw, -1, keepdims=True)
            mixed = dot(raw.astype(BF16), vals) * share
            xo_rows = (values + to_lanes(mixed)).astype(BF16)

            @pl.when(sec < n_sec - 1)
            def _():
                xo[k, rows, :] = xo_rows
                pltpu.make_async_remote_copy(
                    src_ref=xo.at[k, rows],
                    dst_ref=xb.at[k, rows],
                    send_sem=f_send,
                    recv_sem=f_recv.at[p, k],
                    device_id={"section": sec + 1},
                    device_id_type=MESH,
                ).start()

            pb[p, k] = raw * share
        return carry

    lax.fori_loop(0, pieces, forward, 0)

    def to_peer(j, src, dst, send_sem, recv_sem):
        return pltpu.make_async_remote_copy(
            src_ref=src,
            dst_ref=dst,
            send_sem=send_sem,
            recv_sem=recv_sem,
            device_id={"dp": (me + j) % n_dp},
            device_id_type=MESH,
        )

    def block_of(ref, j):
        column = ((me + j) % n_dp) * block
        return ref.at[
            column // CHUNK, :, pl.ds(pl.multiple_of(column % CHUNK, block), block)
        ]

    own_block = pltpu.make_async_copy(block_of(hb, 0), hg.at[0], in_sem.at[0])
    own_block.start()
    for j in range(1, n_dp):
        to_peer(j, block_of(hb, j), hg.at[j], h_send, h_recv).start()

    def backward(step, carry):
        p = pieces - 1 - step
        start = pl.multiple_of(p * T, T)
        rows = pl.ds(start, T)
        window = pl.ds(start, WINDOW)
        own = pl.ds(pl.multiple_of(start + PAD, T), T)
        inner = jnp.zeros((T, 128), F32)
        for k in range(KV_HEADS):
            arrival = pltpu.make_async_remote_copy(
                src_ref=gb.at[k, rows],
                dst_ref=gb.at[k, rows],
                send_sem=g_send,
                recv_sem=g_recv.at[p, k],
                device_id={"section": sec},
                device_id_type=MESH,
            )

            @pl.when(sec < n_sec - 1)
            def _():
                arrival.wait_recv()

            grads = to_rows(gb[k, rows, :])
            hidden = hb[k, rows, :]
            query = to_rows(hidden)
            keys = kvb[window, pl.ds(k * HEAD_DIM, HEAD_DIM)]
            vals = kvb[window, pl.ds(kv_width + k * HEAD_DIM, HEAD_DIM)]
            probs = pb[p, k]
            product = probs * dot_t(grads, vals)
            total = jnp.sum(product, -1, keepdims=True)
            d_low = ((product - probs * total) * SCALE).astype(BF16)
            d_query = to_lanes(dot(d_low, keys))
            dqb[k] = d_query
            inner = inner + fold_lanes(d_query * hidden.astype(F32))
            dacc[k, window, :] += t_dot(d_low, query)
            dacc[KV_HEADS + k, window, :] += t_dot(probs.astype(BF16), grads)
        d_kv = jnp.concatenate([dacc[i, own, :] for i in range(2 * KV_HEADS)], axis=1).astype(
            BF16
        )
        dg[p, 0] = d_kv
        inner = inner + fold_lanes(d_kv.astype(F32) * kvb[own, :].astype(F32))
        mean = jnp.sum(inner, -1, keepdims=True) / width
        inverse = rb[rows, :][:, :1]
        for k in range(KV_HEADS):
            d_hidden = dqb[k] + dot_t(d_kv, wb[k])
            normed = xb[k, rows, :].astype(F32) * inverse
            moment = d_hidden * normed
            gsum[k] += moment[0:8] + moment[8:16] + moment[16:24] + moment[24:32]

            @pl.when(sec > 0)
            def _():
                d_inputs = inverse * (d_hidden * gf[k, 0:1, :] - normed * mean)
                go[k, rows, :] = (gb[k, rows, :].astype(F32) + d_inputs).astype(BF16)
                pltpu.make_async_remote_copy(
                    src_ref=go.at[k, rows],
                    dst_ref=gb.at[k, rows],
                    send_sem=g_send,
                    recv_sem=g_recv.at[p, k],
                    device_id={"section": sec - 1},
                    device_id_type=MESH,
                ).start()

        for j in range(1, n_dp):
            to_peer(j, dg.at[p, 0], dg.at[p, j], d_send, d_recv.at[p]).start()
        return carry

    lax.fori_loop(0, pieces, backward, 0)

    for k in range(KV_HEADS):
        row = jnp.sum(gsum[k], 0, keepdims=True).astype(BF16).astype(F32)
        gs[k] = jnp.broadcast_to(row, (8, CHUNK))
    own_gain = pltpu.make_async_copy(block_of(gs, 0), gg.at[0], in_sem.at[1])
    own_gain.start()
    for j in range(1, n_dp):
        to_peer(j, block_of(gs, j), gg.at[j], s_send, s_recv).start()

    def wait_for(ref, sem):
        pltpu.make_async_copy(ref, ref, sem).wait()

    others = pl.ds(1, n_dp - 1)
    own_block.wait()
    wait_for(hg.at[others], h_recv)

    def multiply(step, carry):
        p = pieces - 1 - step
        rows = pl.ds(pl.multiple_of(p * T, T), T)
        wait_for(dg.at[p, others], d_recv.at[p])
        hidden = hg[:, rows, :].reshape(n_dp * T, block)
        d_kv = dg[p].reshape(n_dp * T, 2 * kv_width)
        product = t_dot(hidden, d_kv)

        @pl.when(step == 0)
        def _():
            out_w[...] = product

        @pl.when(step > 0)
        def _():
            out_w[...] += product

        return carry

    lax.fori_loop(0, pieces, multiply, 0)
    own_gain.wait()
    wait_for(gg.at[others], s_recv)
    gain_total = gg[0]
    for j in range(1, n_dp):
        gain_total = gain_total + gg[j]
    out_g[...] = gain_total[0:1]

    wait_for(hg.at[others], h_send)
    wait_for(dg.at[:, others], d_send)
    wait_for(gg.at[others], s_send)

    @pl.when(sec < n_sec - 1)
    def _():
        wait_for(xo, f_send)

    @pl.when(sec > 0)
    def _():
        wait_for(go, g_send)


def attention_bias(doc_lengths, block_mask, seq_len):
    positions = jnp.arange(seq_len, dtype=jnp.int32)
    doc_ends = jnp.cumsum(doc_lengths)
    doc_ids = jnp.sum((positions[:, None] >= doc_ends[None, :]).astype(jnp.int32), 1)
    blocks = positions // BLK
    opened = jnp.repeat(jnp.repeat(block_mask == 1, BLK, 0), BLK, 1)
    allowed = (
        (positions[None, :] <= positions[:, None])
        & (doc_ids[:, None] == doc_ids[None, :])
        & (opened | (blocks[:, None] == blocks[None, :]))
    )
    full = jnp.pad(jnp.where(allowed, 0.0, -1e30), ((0, 0), (PAD, 0)), constant_values=-1e30)
    return jnp.stack(
        [full[s : s + T, s : s + WINDOW] for s in range(0, seq_len, T)]
    ).astype(F32)


def row_factor(seg_lengths, seq_len):
    positions = jnp.arange(seq_len, dtype=jnp.int32)
    seg_ends = jnp.cumsum(seg_lengths)
    seg_ids = jnp.sum((positions[:, None] >= seg_ends[None, :]).astype(jnp.int32), 1)
    sizes = jnp.sum(
        jnp.where(seg_ids[:, None] == jnp.arange(SEGS)[None, :], seg_lengths[None, :], 0), 1
    )
    factor = seq_len / (SEGS * sizes.astype(F32))
    return jnp.broadcast_to(factor[:, None], (seq_len, 128))


def local(n_sec, n_dp, tokens, upstream, gains, w_kv, doc_lengths, seg_lengths, block_mask):
    seq_len, width = tokens.shape[1:]
    pieces = seq_len // T
    kv2 = w_kv.shape[2]
    block = width // n_dp
    bias = attention_bias(doc_lengths[0], block_mask[0], seq_len)
    factor = row_factor(seg_lengths[0], seq_len)
    any_spec = pl.BlockSpec(memory_space=pl.ANY)
    vmem = pl.BlockSpec(memory_space=pltpu.VMEM)
    features = (KV_HEADS, seq_len, CHUNK)
    dma = pltpu.SemaphoreType.DMA
    grad_weight, grad_gain = pl.pallas_call(
        functools.partial(kernel, n_sec, n_dp),
        out_shape=(
            jax.ShapeDtypeStruct((block, kv2), F32),
            jax.ShapeDtypeStruct((1, block), F32),
        ),
        in_specs=[any_spec, any_spec, vmem, any_spec, vmem, vmem],
        out_specs=(vmem, vmem),
        scratch_shapes=[
            pltpu.VMEM(features, BF16),
            pltpu.VMEM(features, BF16),
            pltpu.VMEM(features, BF16),
            pltpu.VMEM(features, BF16),
            pltpu.VMEM(features, BF16),
            pltpu.VMEM((KV_HEADS, CHUNK, kv2), BF16),
            pltpu.VMEM((PAD + seq_len, kv2), BF16),
            pltpu.VMEM((2 * KV_HEADS, PAD + seq_len, HEAD_DIM), F32),
            pltpu.VMEM((pieces, KV_HEADS, GROUP * T, WINDOW), F32),
            pltpu.VMEM((KV_HEADS, T, CHUNK), F32),
            pltpu.VMEM((seq_len, 128), F32),
            pltpu.VMEM((KV_HEADS, 8, CHUNK), F32),
            pltpu.VMEM((KV_HEADS, 8, CHUNK), F32),
            pltpu.VMEM((KV_HEADS, 8, CHUNK), F32),
            pltpu.VMEM((n_dp, seq_len, block), BF16),
            pltpu.VMEM((pieces, n_dp, T, kv2), BF16),
            pltpu.VMEM((n_dp, 8, block), F32),
            dma((KV_HEADS,)),
            dma((KV_HEADS,)),
            dma,
            dma((pieces, KV_HEADS)),
            dma,
            dma((pieces, KV_HEADS)),
            dma,
            dma,
            dma,
            dma((pieces,)),
            dma,
            dma,
        ],
        compiler_params=pltpu.CompilerParams(
            collective_id=0, has_side_effects=True, vmem_limit_bytes=52 * 1024 * 1024
        ),
        cost_estimate=pl.CostEstimate(
            flops=7 * 10**9, bytes_accessed=12 * 2**20, transcendentals=10**6
        ),
        name="relay",
    )(tokens, upstream, gains, w_kv, bias, factor)
    return grad_weight[None], grad_gain


def solution(mesh):
    placed = (
        P("dp", None, None),
        P("dp", None, None),
        P("section", None),
        P("section", None, None),
        P("dp", None),
        P("dp", None),
        P("dp", None, None),
    )
    return jax.shard_map(
        functools.partial(local, mesh.shape["section"], mesh.shape["dp"]),
        mesh=mesh,
        in_specs=placed,
        out_specs=(P("section", "dp", None), P("section", "dp")),
        check_vma=False,
    )
```

```python
import functools
import math

import jax
import jax.numpy as jnp
from jax import lax
from jax.experimental import pallas as pl
from jax.experimental.pallas import tpu as pltpu
from jax.sharding import PartitionSpec as P

HEADS = 32
KV_HEADS = 4
GROUP = 8
HEAD_DIM = 128
SEGS = 4
BLK = 16
EPSILON = 1e-06

T = 32
WINDOW = 128
PAD = WINDOW - T
CHUNK = GROUP * HEAD_DIM
MESH = pl.DeviceIdType.MESH
F32 = jnp.float32
BF16 = jnp.bfloat16
EXP_SCALE = HEAD_DIM**-0.5 * math.log2(math.e)
SCALE = HEAD_DIM**-0.5


def to_rows(block):
    return jnp.concatenate(
        [block[:, HEAD_DIM * g : HEAD_DIM * (g + 1)] for g in range(GROUP)], axis=0
    )


def to_lanes(block):
    return jnp.concatenate([block[T * g : T * (g + 1)] for g in range(GROUP)], axis=1)


def fold_lanes(block):
    total = block[:, :128]
    for g in range(1, block.shape[1] // 128):
        total = total + block[:, 128 * g : 128 * (g + 1)]
    return total


def dot_t(a, b):
    return lax.dot_general(a, b, (((1,), (1,)), ((), ())), preferred_element_type=F32)


def t_dot(a, b):
    return lax.dot_general(a, b, (((0,), (0,)), ((), ())), preferred_element_type=F32)


def dot(a, b):
    return jnp.dot(a, b, preferred_element_type=F32)


def kernel(
    n_sec,
    n_dp,
    tok,
    ups,
    gain,
    w,
    docs,
    segs,
    table,
    out_w,
    out_g,
    xb,
    hb,
    gb,
    xo,
    go,
    wb,
    wt,
    kvb,
    dacc,
    pb,
    pt,
    dqb,
    rb,
    bias,
    gf,
    gsum,
    gs,
    hg,
    ht,
    do,
    dg,
    wacc,
    eo,
    eg,
    gg,
    w_sem,
    in_sem,
    f_send,
    f_recv,
    g_send,
    g_recv,
    h_send,
    h_recv,
    d_send,
    d_recv,
    e_send,
    e_recv,
    s_send,
    s_recv,
):
    sec = lax.axis_index("section")
    me = lax.axis_index("dp")
    seq_len = xb.shape[1]
    pieces = seq_len // T
    width = KV_HEADS * CHUNK
    kv_width = KV_HEADS * HEAD_DIM
    block = width // n_dp
    grid_y = n_dp // KV_HEADS
    cols = 2 * kv_width // grid_y
    x, y = me // grid_y, me % grid_y
    first = sec == 0
    last = sec == n_sec - 1
    early = sec < (n_sec + 3) // 4

    w_copies = [
        pltpu.make_async_copy(w.at[0, pl.ds(k * CHUNK, CHUNK)], wb.at[k], w_sem.at[k])
        for k in range(KV_HEADS)
    ]
    tok_copies = [
        pltpu.make_async_copy(tok.at[0, :, pl.ds(k * CHUNK, CHUNK)], xb.at[k], in_sem.at[k])
        for k in range(KV_HEADS)
    ]
    ups_copies = [
        pltpu.make_async_copy(ups.at[0, :, pl.ds(k * CHUNK, CHUNK)], xo.at[k], in_sem.at[k])
        for k in range(KV_HEADS)
    ]

    @pl.when(first)
    def _():
        for copy in tok_copies:
            copy.start()

    for copy in w_copies:
        copy.start()

    @pl.when(last)
    def _():
        for copy in ups_copies:
            copy.start()

    barrier = pltpu.get_barrier_semaphore()
    for neighbour in ((sec + 1) % n_sec, (sec + n_sec - 1) % n_sec):
        pl.semaphore_signal(
            barrier, inc=1, device_id={"section": neighbour}, device_id_type=MESH
        )
    for j in range(1, n_dp):
        pl.semaphore_signal(
            barrier, inc=1, device_id={"dp": (me + j) % n_dp}, device_id_type=MESH
        )

    kvb[pl.ds(0, PAD), :] = jnp.zeros((PAD, 2 * kv_width), BF16)
    dacc[...] = jnp.zeros_like(dacc)
    gsum[...] = jnp.zeros_like(gsum)
    for k in range(KV_HEADS):
        gf[k] = jnp.broadcast_to(
            gain[:, pl.ds(k * CHUNK, CHUNK)].astype(F32), (8, CHUNK)
        )

    doc_ends = [docs[0, 0]]
    for d in range(1, docs.shape[1] - 1):
        doc_ends.append(doc_ends[-1] + docs[0, d])

    def doc_of(positions):
        total = jnp.zeros_like(positions)
        for end in doc_ends:
            total = total + jnp.where(positions >= end, 1, 0)
        return total

    row = lax.broadcasted_iota(jnp.int32, (T, WINDOW), 0)
    column = lax.broadcasted_iota(jnp.int32, (T, WINDOW), 1)

    def mask_piece(p, carry):
        queries = row + p * T
        keys = column + (p * T - PAD)
        first_block = p * (T // BLK)
        opened = jnp.zeros((T, WINDOW), jnp.int32)
        for a in range(T // BLK):
            line = jnp.zeros((T, WINDOW), jnp.int32)
            for c in range(WINDOW // BLK):
                key_block = first_block + c - PAD // BLK
                value = table[0, first_block + a, jnp.maximum(key_block, 0)]
                line = jnp.where(column // BLK == c, value, line)
            opened = jnp.where(row // BLK == a, line, opened)
        same = row // BLK + PAD // BLK == column // BLK
        allowed = (
            (keys >= 0)
            & (keys <= queries)
            & (doc_of(keys) == doc_of(queries))
            & (same | (opened == 1))
        )
        bias[p] = jnp.where(allowed, 0.0, -1e30)
        return carry

    lax.fori_loop(0, pieces, mask_piece, 0)

    @pl.when(last)
    def _():
        for copy in ups_copies:
            copy.wait()
        sizes = [segs[0, i] for i in range(SEGS)]

        def scale_piece(p, carry):
            rows = pl.ds(pl.multiple_of(p * T, T), T)
            positions = row + p * T
            count = jnp.zeros((T, WINDOW), jnp.int32) + sizes[0]
            end = sizes[0]
            for i in range(1, SEGS):
                count = jnp.where(positions >= end, sizes[i], count)
                end = end + sizes[i]
            factor = seq_len / (SEGS * count.astype(F32))
            factor = jnp.concatenate([factor] * (CHUNK // WINDOW), axis=1)
            for k in range(KV_HEADS):
                gb[k, rows, :] = (xo[k, rows, :].astype(F32) * factor).astype(BF16)
            return carry

        lax.fori_loop(0, pieces, scale_piece, 0)

    for copy in w_copies:
        copy.wait()

    @pl.when(first)
    def _():
        for copy in tok_copies:
            copy.wait()

    def transpose_w():
        def part(i, carry):
            k, c = i // 4, i % 4
            source = pl.ds(pl.multiple_of(c * 256, 256), 256)
            for n in range(2 * kv_width // 256):
                wt[k, pl.ds(n * 256, 256), source] = wb[k, source, pl.ds(n * 256, 256)].T
            return carry

        lax.fori_loop(0, KV_HEADS * (CHUNK // 256), part, 0)

    @pl.when(jnp.logical_not(early))
    def _():
        transpose_w()

    pl.semaphore_wait(barrier, n_dp + 1)

    def forward(p, carry):
        start = pl.multiple_of(p * T, T)
        rows = pl.ds(start, T)
        acc = jnp.zeros((T, 2 * kv_width), F32)
        squares = jnp.zeros((T, 128), F32)
        for k in range(KV_HEADS):
            arrival = pltpu.make_async_remote_copy(
                src_ref=xb.at[k, rows],
                dst_ref=xb.at[k, rows],
                send_sem=f_send,
                recv_sem=f_recv.at[p, k],
                device_id={"section": sec},
                device_id_type=MESH,
            )

            @pl.when(sec > 0)
            def _():
                arrival.wait_recv()

            values = xb[k, rows, :].astype(F32)
            squares = squares + fold_lanes(values * values)
            acc = acc + dot((values * gf[k, 0:1, :]).astype(BF16), wb[k])
        inverse = lax.rsqrt(jnp.sum(squares, -1, keepdims=True) / width + EPSILON)
        rb[rows, :] = jnp.broadcast_to(inverse, (T, 128))
        kvb[pl.ds(pl.multiple_of(start + PAD, T), T), :] = (acc * inverse).astype(BF16)
        window = pl.ds(start, WINDOW)
        bias_rows = jnp.concatenate([bias[p]] * GROUP, axis=0)
        for k in range(KV_HEADS):
            values = xb[k, rows, :].astype(F32)
            hidden = (values * inverse * gf[k, 0:1, :]).astype(BF16)
            hb[k, rows, :] = hidden
            keys = kvb[window, pl.ds(k * HEAD_DIM, HEAD_DIM)]
            vals = kvb[window, pl.ds(kv_width + k * HEAD_DIM, HEAD_DIM)]
            scores = dot_t(to_rows(hidden), keys)
            raw = jnp.exp2(scores * EXP_SCALE + bias_rows)
            share = 1.0 / jnp.sum(raw, -1, keepdims=True)
            mixed = dot(raw.astype(BF16), vals) * share
            xo[k, rows, :] = (values + to_lanes(mixed)).astype(BF16)
            probs = raw * share
            pb[p, k] = probs
            pt[p, k] = probs.T

        @pl.when(sec < n_sec - 1)
        def _():
            for k in range(KV_HEADS):
                pltpu.make_async_remote_copy(
                    src_ref=xo.at[k, rows],
                    dst_ref=xb.at[k, rows],
                    send_sem=f_send,
                    recv_sem=f_recv.at[p, k],
                    device_id={"section": sec + 1},
                    device_id_type=MESH,
                ).start()

        return carry

    lax.fori_loop(0, pieces, forward, 0)

    def to_peer(dp, src, dst, send_sem, recv_sem):
        return pltpu.make_async_remote_copy(
            src_ref=src,
            dst_ref=dst,
            send_sem=send_sem,
            recv_sem=recv_sem,
            device_id={"dp": dp},
            device_id_type=MESH,
        )

    def wait_for(ref, sem):
        pltpu.make_async_copy(ref, ref, sem).wait()

    peers = []
    for jx in range(KV_HEADS):
        for jy in range(grid_y):
            peer_x, peer_y = (x + jx) % KV_HEADS, (y + jy) % grid_y
            peers.append((jx * grid_y + jy, peer_x * grid_y + peer_y, peer_x, peer_y))
    others = pl.ds(1, n_dp - 1)

    own_hidden = pltpu.make_async_copy(hb.at[x], hg.at[0], in_sem.at[0])
    own_hidden.start()
    for j, dp, peer_x, peer_y in peers[1:]:
        to_peer(dp, hb.at[peer_x], hg.at[j], h_send, h_recv).start()

    def transpose_h():
        own_hidden.wait()
        wait_for(hg.at[others], h_recv)

        def part(p, carry):
            rows = pl.ds(pl.multiple_of(p * T, T), T)
            for c in range(CHUNK // 256):
                hidden = hg[:, rows, pl.ds(c * 256, 256)].reshape(n_dp * T, 256)
                ht[p, pl.ds(c * 256, 256), :] = hidden.T
            return carry

        lax.fori_loop(0, pieces, part, 0)

    @pl.when(early)
    def _():
        transpose_w()
        transpose_h()

    def backward(step, carry):
        p = pieces - 1 - step
        start = pl.multiple_of(p * T, T)
        rows = pl.ds(start, T)
        window = pl.ds(start, WINDOW)
        own = pl.ds(pl.multiple_of(start + PAD, T), T)
        inner = jnp.zeros((T, 128), F32)
        for k in range(KV_HEADS):
            if k % 2 == 0:

                @pl.when(sec < n_sec - 1)
                def _():
                    for i in (k, k + 1):
                        pltpu.make_async_remote_copy(
                            src_ref=gb.at[i, rows],
                            dst_ref=gb.at[i, rows],
                            send_sem=g_send,
                            recv_sem=g_recv.at[p, i],
                            device_id={"section": sec},
                            device_id_type=MESH,
                        ).wait_recv()

            grads = to_rows(gb[k, rows, :])
            hidden = hb[k, rows, :]
            query = to_rows(hidden)
            keys = kvb[window, pl.ds(k * HEAD_DIM, HEAD_DIM)]
            vals = kvb[window, pl.ds(kv_width + k * HEAD_DIM, HEAD_DIM)]
            probs = pb[p, k]
            product = probs * dot_t(grads, vals)
            total = jnp.sum(product, -1, keepdims=True)
            d_low = ((product - probs * total) * SCALE).astype(BF16)
            probs_t = pt[p, k]
            product_t = probs_t * dot_t(vals, grads)
            total_t = jnp.sum(product_t, 0, keepdims=True)
            d_low_t = ((product_t - probs_t * total_t) * SCALE).astype(BF16)
            d_query = to_lanes(dot(d_low, keys))
            dqb[k] = d_query
            inner = inner + fold_lanes(d_query * hidden.astype(F32))
            dacc[k, window, :] += dot(d_low_t, query)
            dacc[KV_HEADS + k, window, :] += dot(probs_t.astype(BF16), grads)
        d_kv = jnp.concatenate([dacc[i, own, :] for i in range(2 * KV_HEADS)], axis=1).astype(
            BF16
        )
        for c in range(grid_y):
            do[p, c] = d_kv[:, c * cols : (c + 1) * cols]
        inner = inner + fold_lanes(d_kv.astype(F32) * kvb[own, :].astype(F32))
        mean = jnp.sum(inner, -1, keepdims=True) / width
        inverse = rb[rows, :][:, :1]

        def send_d_kv():
            dg[p, 0] = do[p, y]
            for j, dp, peer_x, peer_y in peers[1:]:
                to_peer(dp, do.at[p, peer_y], dg.at[p, j], d_send, d_recv.at[p]).start()

        @pl.when(first)
        def _():
            send_d_kv()

        def send_grads(chunks):
            @pl.when(sec > 0)
            def _():
                for k in chunks:
                    pltpu.make_async_remote_copy(
                        src_ref=go.at[k, rows],
                        dst_ref=gb.at[k, rows],
                        send_sem=g_send,
                        recv_sem=g_recv.at[p, k],
                        device_id={"section": sec - 1},
                        device_id_type=MESH,
                    ).start()

        for k in range(KV_HEADS):
            d_hidden = dqb[k] + dot(d_kv, wt[k])
            normed = xb[k, rows, :].astype(F32) * inverse
            moment = d_hidden * normed
            gsum[k] += moment[0:8] + moment[8:16] + moment[16:24] + moment[24:32]
            d_inputs = inverse * (d_hidden * gf[k, 0:1, :] - normed * mean)
            go[k, rows, :] = (gb[k, rows, :].astype(F32) + d_inputs).astype(BF16)
            if k < 2:
                send_grads([k])
            elif k == KV_HEADS - 1:
                send_grads([k - 1, k])

        @pl.when(sec > 0)
        def _():
            send_d_kv()

        return carry

    lax.fori_loop(0, pieces, backward, 0)

    def gain_block(dp):
        column = dp * block
        return gs.at[
            column // CHUNK, :, pl.ds(pl.multiple_of(column % CHUNK, block), block)
        ]

    for k in range(KV_HEADS):
        total = jnp.sum(gsum[k], 0, keepdims=True).astype(BF16).astype(F32)
        gs[k] = jnp.broadcast_to(total, (8, CHUNK))
    own_gain = pltpu.make_async_copy(gain_block(me), gg.at[0], in_sem.at[1])
    own_gain.start()
    for j, dp, peer_x, peer_y in peers[1:]:
        to_peer(dp, gain_block(dp), gg.at[j], s_send, s_recv).start()

    @pl.when(jnp.logical_not(early))
    def _():
        transpose_h()

    def multiply(step, carry):
        p = pieces - 1 - step
        wait_for(dg.at[p, others], d_recv.at[p])
        d_kv = dg[p].reshape(n_dp * T, cols)
        for c in range(CHUNK // 256):
            part = pl.ds(c * 256, 256)
            product = dot(ht[p, part, :], d_kv)
            wacc[part, :] = product + jnp.where(step > 0, wacc[part, :], 0.0)
        return carry

    lax.fori_loop(0, pieces - 1, multiply, 0)
    wait_for(dg.at[0, others], d_recv.at[0])
    d_kv = dg[0].reshape(n_dp * T, cols)
    for jy in list(range(1, grid_y)) + [0]:
        peer_y = (y + jy) % grid_y
        part = pl.ds(pl.multiple_of(peer_y * block, block), block)
        total = wacc[part, :] + dot(ht[0, part, :], d_kv)
        if jy == 0:
            out_w[:, pl.ds(pl.multiple_of(y * cols, cols), cols)] = total
        else:
            eo[jy] = total.astype(BF16)
            to_peer(
                x * grid_y + peer_y, eo.at[jy], eg.at[jy], e_send, e_recv.at[jy]
            ).start()

    own_gain.wait()
    wait_for(gg.at[others], s_recv)
    gain_total = gg[0]
    for j in range(1, n_dp):
        gain_total = gain_total + gg[j]
    out_g[...] = gain_total[0:1]

    for jy in range(1, grid_y):
        wait_for(eg.at[jy], e_recv.at[jy])
        source_y = (y + grid_y - jy) % grid_y
        out_w[:, pl.ds(pl.multiple_of(source_y * cols, cols), cols)] = eg[jy].astype(F32)

    if grid_y > 1:
        wait_for(eo.at[pl.ds(1, grid_y - 1)], e_send)
    wait_for(hg.at[others], h_send)
    wait_for(dg.at[:, others], d_send)
    wait_for(gg.at[others], s_send)

    @pl.when(sec < n_sec - 1)
    def _():
        wait_for(xo, f_send)

    @pl.when(sec > 0)
    def _():
        wait_for(go, g_send)


def local(n_sec, n_dp, tokens, upstream, gains, w_kv, doc_lengths, seg_lengths, block_mask):
    seq_len, width = tokens.shape[1:]
    pieces = seq_len // T
    kv2 = w_kv.shape[2]
    block = width // n_dp
    grid_y = n_dp // KV_HEADS
    cols = kv2 // grid_y
    any_spec = pl.BlockSpec(memory_space=pl.ANY)
    vmem = pl.BlockSpec(memory_space=pltpu.VMEM)
    smem = pl.BlockSpec(memory_space=pltpu.SMEM)
    features = (KV_HEADS, seq_len, CHUNK)
    dma = pltpu.SemaphoreType.DMA
    grad_weight, grad_gain = pl.pallas_call(
        functools.partial(kernel, n_sec, n_dp),
        out_shape=(
            jax.ShapeDtypeStruct((block, kv2), F32),
            jax.ShapeDtypeStruct((1, block), F32),
        ),
        in_specs=[any_spec, any_spec, vmem, any_spec, smem, smem, smem],
        out_specs=(vmem, vmem),
        scratch_shapes=[
            pltpu.VMEM(features, BF16),
            pltpu.VMEM(features, BF16),
            pltpu.VMEM(features, BF16),
            pltpu.VMEM(features, BF16),
            pltpu.VMEM(features, BF16),
            pltpu.VMEM((KV_HEADS, CHUNK, kv2), BF16),
            pltpu.VMEM((KV_HEADS, kv2, CHUNK), BF16),
            pltpu.VMEM((PAD + seq_len, kv2), BF16),
            pltpu.VMEM((2 * KV_HEADS, PAD + seq_len, HEAD_DIM), F32),
            pltpu.VMEM((pieces, KV_HEADS, GROUP * T, WINDOW), F32),
            pltpu.VMEM((pieces, KV_HEADS, WINDOW, GROUP * T), F32),
            pltpu.VMEM((KV_HEADS, T, CHUNK), F32),
            pltpu.VMEM((seq_len, 128), F32),
            pltpu.VMEM((pieces, T, WINDOW), F32),
            pltpu.VMEM((KV_HEADS, 8, CHUNK), F32),
            pltpu.VMEM((KV_HEADS, 8, CHUNK), F32),
            pltpu.VMEM((KV_HEADS, 8, CHUNK), F32),
            pltpu.VMEM((n_dp, seq_len, CHUNK), BF16),
            pltpu.VMEM((pieces, CHUNK, n_dp * T), BF16),
            pltpu.VMEM((pieces, grid_y, T, cols), BF16),
            pltpu.VMEM((pieces, n_dp, T, cols), BF16),
            pltpu.VMEM((CHUNK, cols), F32),
            pltpu.VMEM((grid_y, block, cols), BF16),
            pltpu.VMEM((grid_y, block, cols), BF16),
            pltpu.VMEM((n_dp, 8, block), F32),
            dma((KV_HEADS,)),
            dma((KV_HEADS,)),
            dma,
            dma((pieces, KV_HEADS)),
            dma,
            dma((pieces, KV_HEADS)),
            dma,
            dma,
            dma,
            dma((pieces,)),
            dma,
            dma((grid_y,)),
            dma,
            dma,
        ],
        compiler_params=pltpu.CompilerParams(
            collective_id=0, has_side_effects=True, vmem_limit_bytes=60 * 1024 * 1024
        ),
        cost_estimate=pl.CostEstimate(
            flops=7 * 10**9, bytes_accessed=12 * 2**20, transcendentals=10**6
        ),
        name="relay",
    )(tokens, upstream, gains, w_kv, doc_lengths, seg_lengths, block_mask)
    return grad_weight[None], grad_gain


def solution(mesh):
    placed = (
        P("dp", None, None),
        P("dp", None, None),
        P("section", None),
        P("section", None, None),
        P("dp", None),
        P("dp", None),
        P("dp", None, None),
    )
    return jax.shard_map(
        functools.partial(local, mesh.shape["section"], mesh.shape["dp"]),
        mesh=mesh,
        in_specs=placed,
        out_specs=(P("section", "dp", None), P("section", "dp")),
        check_vma=False,
    )
```

```python
import functools
import math

import jax
import jax.numpy as jnp
from jax import lax
from jax.experimental import pallas as pl
from jax.experimental.pallas import tpu as pltpu
from jax.sharding import PartitionSpec as P

HEADS = 32
KV_HEADS = 4
GROUP = 8
HEAD_DIM = 128
SEGS = 4
BLK = 16
EPSILON = 1e-06

T = 16
SPAN = 2
WINDOW = 128
PAD = WINDOW - T
CHUNK = GROUP * HEAD_DIM
MESH = pl.DeviceIdType.MESH
F32 = jnp.float32
BF16 = jnp.bfloat16
EXP_SCALE = HEAD_DIM**-0.5 * math.log2(math.e)
SCALE = HEAD_DIM**-0.5


def to_rows(block):
    return jnp.concatenate(
        [block[:, HEAD_DIM * g : HEAD_DIM * (g + 1)] for g in range(GROUP)], axis=0
    )


def to_lanes(block):
    return jnp.concatenate([block[T * g : T * (g + 1)] for g in range(GROUP)], axis=1)


def fold_lanes(block):
    total = block[:, :128]
    for g in range(1, block.shape[1] // 128):
        total = total + block[:, 128 * g : 128 * (g + 1)]
    return total


def dot_t(a, b):
    return lax.dot_general(a, b, (((1,), (1,)), ((), ())), preferred_element_type=F32)


def t_dot(a, b):
    return lax.dot_general(a, b, (((0,), (0,)), ((), ())), preferred_element_type=F32)


def dot(a, b):
    return jnp.dot(a, b, preferred_element_type=F32)


def kernel(
    n_sec,
    n_dp,
    tok,
    ups,
    gain,
    w,
    docs,
    segs,
    table,
    out_w,
    out_g,
    xb,
    hb,
    gb,
    xo,
    go,
    wb,
    wt,
    kvb,
    dacc,
    pb,
    pt,
    dqb,
    rb,
    bias,
    gf,
    gsum,
    gs,
    hg,
    ht,
    do,
    dg,
    wacc,
    eo,
    eg,
    gg,
    w_sem,
    in_sem,
    f_send,
    f_recv,
    g_send,
    g_recv,
    hx_send,
    hx_recv,
    hy_send,
    hy_recv,
    hr_send,
    hr_recv,
    d_send,
    d_recv,
    e_send,
    e_recv,
    s_send,
    s_recv,
):
    sec = lax.axis_index("section")
    me = lax.axis_index("dp")
    seq_len = xb.shape[1]
    pieces = seq_len // T
    width = KV_HEADS * CHUNK
    kv_width = KV_HEADS * HEAD_DIM
    block = width // n_dp
    grid_y = n_dp // KV_HEADS
    cols = 2 * kv_width // grid_y
    x, y = me // grid_y, me % grid_y
    span_rows = SPAN * T
    first = sec == 0
    last = sec == n_sec - 1
    early = sec < (n_sec + 3) // 4

    w_copies = [
        pltpu.make_async_copy(w.at[0, pl.ds(k * CHUNK, CHUNK)], wb.at[k], w_sem.at[k])
        for k in range(KV_HEADS)
    ]
    tok_copies = [
        pltpu.make_async_copy(tok.at[0, :, pl.ds(k * CHUNK, CHUNK)], xb.at[k], in_sem.at[k])
        for k in range(KV_HEADS)
    ]
    ups_copies = [
        pltpu.make_async_copy(ups.at[0, :, pl.ds(k * CHUNK, CHUNK)], xo.at[k], in_sem.at[k])
        for k in range(KV_HEADS)
    ]

    @pl.when(first)
    def _():
        for copy in tok_copies:
            copy.start()

    for copy in w_copies:
        copy.start()

    @pl.when(last)
    def _():
        for copy in ups_copies:
            copy.start()

    barrier = pltpu.get_barrier_semaphore()
    for neighbour in ((sec + 1) % n_sec, (sec + n_sec - 1) % n_sec):
        pl.semaphore_signal(
            barrier, inc=1, device_id={"section": neighbour}, device_id_type=MESH
        )
    for j in range(1, n_dp):
        pl.semaphore_signal(
            barrier, inc=1, device_id={"dp": (me + j) % n_dp}, device_id_type=MESH
        )

    kvb[pl.ds(0, PAD), :] = jnp.zeros((PAD, 2 * kv_width), BF16)
    dacc[...] = jnp.zeros_like(dacc)
    gsum[...] = jnp.zeros_like(gsum)
    for k in range(KV_HEADS):
        gf[k] = jnp.broadcast_to(
            gain[:, pl.ds(k * CHUNK, CHUNK)].astype(F32), (8, CHUNK)
        )

    doc_ends = [docs[0, 0]]
    for d in range(1, docs.shape[1] - 1):
        doc_ends.append(doc_ends[-1] + docs[0, d])

    def doc_of(positions):
        total = jnp.zeros_like(positions)
        for end in doc_ends:
            total = total + jnp.where(positions >= end, 1, 0)
        return total

    row = lax.broadcasted_iota(jnp.int32, (T, WINDOW), 0)
    column = lax.broadcasted_iota(jnp.int32, (T, WINDOW), 1)

    blocks = seq_len // BLK
    opened = table[0].astype(BF16)
    block_row = lax.broadcasted_iota(jnp.int32, (blocks, WINDOW), 0)
    block_column = lax.broadcasted_iota(jnp.int32, (blocks, WINDOW), 1) // BLK
    for p in range(pieces):
        queries = row + p * T
        keys = column + (p * T - PAD)
        spread = (block_row == block_column + (p * T - PAD) // BLK).astype(BF16)
        line = dot(opened, spread)[p : p + 1]
        allowed = (
            (keys >= 0)
            & (keys <= queries)
            & (doc_of(keys) == doc_of(queries))
            & ((column // BLK == PAD // BLK) | (line > 0.5))
        )
        bias[p] = jnp.where(allowed, 0.0, -1e30)

    @pl.when(last)
    def _():
        for copy in ups_copies:
            copy.wait()
        sizes = [segs[0, i] for i in range(SEGS)]

        def scale_piece(p, carry):
            rows = pl.ds(pl.multiple_of(p * T, T), T)
            positions = row + p * T
            count = jnp.zeros((T, WINDOW), jnp.int32) + sizes[0]
            end = sizes[0]
            for i in range(1, SEGS):
                count = jnp.where(positions >= end, sizes[i], count)
                end = end + sizes[i]
            factor = seq_len / (SEGS * count.astype(F32))
            factor = jnp.concatenate([factor] * (CHUNK // WINDOW), axis=1)
            for k in range(KV_HEADS):
                gb[k, rows, :] = (xo[k, rows, :].astype(F32) * factor).astype(BF16)
            return carry

        lax.fori_loop(0, pieces, scale_piece, 0)

    @pl.when(first)
    def _():
        for copy in tok_copies:
            copy.wait()

    def transpose_w():
        def part(i, carry):
            k, c = i // 4, i % 4
            source = pl.ds(pl.multiple_of(c * 256, 256), 256)
            for n in range(2 * kv_width // 256):
                wt[k, pl.ds(n * 256, 256), source] = wb[k, source, pl.ds(n * 256, 256)].T
            return carry

        lax.fori_loop(0, KV_HEADS * (CHUNK // 256), part, 0)

    @pl.when(jnp.logical_not(early))
    def _():
        for copy in w_copies:
            copy.wait()
        transpose_w()

    pl.semaphore_wait(barrier, n_dp + 1)

    def forward(p, carry):
        start = pl.multiple_of(p * T, T)
        rows = pl.ds(start, T)
        acc = jnp.zeros((T, 2 * kv_width), F32)
        squares = jnp.zeros((T, 128), F32)
        for k in range(KV_HEADS):
            arrival = pltpu.make_async_remote_copy(
                src_ref=xb.at[k, rows],
                dst_ref=xb.at[k, rows],
                send_sem=f_send,
                recv_sem=f_recv.at[p, k],
                device_id={"section": sec},
                device_id_type=MESH,
            )

            @pl.when(sec > 0)
            def _():
                arrival.wait_recv()

            @pl.when(early & (p == 0))
            def _():
                w_copies[k].wait()

            values = xb[k, rows, :].astype(F32)
            squares = squares + fold_lanes(values * values)
            acc = acc + dot((values * gf[k, 0:1, :]).astype(BF16), wb[k])
        inverse = lax.rsqrt(jnp.sum(squares, -1, keepdims=True) / width + EPSILON)
        rb[rows, :] = jnp.broadcast_to(inverse, (T, 128))
        kvb[pl.ds(pl.multiple_of(start + PAD, T), T), :] = (acc * inverse).astype(BF16)
        window = pl.ds(start, WINDOW)
        bias_rows = jnp.concatenate([bias[p]] * GROUP, axis=0)
        for k in range(KV_HEADS):
            values = xb[k, rows, :].astype(F32)
            hidden = (values * inverse * gf[k, 0:1, :]).astype(BF16)
            hb[k, rows, :] = hidden
            keys = kvb[window, pl.ds(k * HEAD_DIM, HEAD_DIM)]
            vals = kvb[window, pl.ds(kv_width + k * HEAD_DIM, HEAD_DIM)]
            scores = dot_t(to_rows(hidden), keys)
            raw = jnp.exp2(scores * EXP_SCALE + bias_rows)
            share = 1.0 / jnp.sum(raw, -1, keepdims=True)
            mixed = dot(raw.astype(BF16), vals) * share
            xo[k, rows, :] = (values + to_lanes(mixed)).astype(BF16)
            probs = raw * share
            pb[p, k] = probs
            pt[p, k] = probs.T

        @pl.when(sec < n_sec - 1)
        def _():
            for k in range(KV_HEADS):
                pltpu.make_async_remote_copy(
                    src_ref=xo.at[k, rows],
                    dst_ref=xb.at[k, rows],
                    send_sem=f_send,
                    recv_sem=f_recv.at[p, k],
                    device_id={"section": sec + 1},
                    device_id_type=MESH,
                ).start()

        return carry

    lax.fori_loop(0, pieces, forward, 0)

    def to_peer(dp, src, dst, send_sem, recv_sem):
        return pltpu.make_async_remote_copy(
            src_ref=src,
            dst_ref=dst,
            send_sem=send_sem,
            recv_sem=recv_sem,
            device_id={"dp": dp},
            device_id_type=MESH,
        )

    def wait_for(ref, sem):
        pltpu.make_async_copy(ref, ref, sem).wait()

    peers = []
    for jy in range(grid_y):
        for jx in range(KV_HEADS):
            peer_x, peer_y = (x + jx) % KV_HEADS, (y + jy) % grid_y
            peers.append((jy * KV_HEADS + jx, peer_x * grid_y + peer_y, peer_x, peer_y))
    others = pl.ds(1, n_dp - 1)

    upper, lower = x * grid_y + (y + 1) % grid_y, x * grid_y + (y + grid_y - 1) % grid_y
    half = seq_len // 2
    far = grid_y - 1

    own_hidden = pltpu.make_async_copy(hb.at[x], hg.at[0, 0], in_sem.at[0])
    own_hidden.start()
    for jx in range(1, KV_HEADS):
        peer_x = (x + jx) % KV_HEADS
        to_peer(peer_x * grid_y + y, hb.at[peer_x], hg.at[0, jx], hx_send, hx_recv).start()

    def spread_h():
        own_hidden.wait()
        wait_for(hg.at[0, pl.ds(1, KV_HEADS - 1)], hx_recv)
        if grid_y > 1:
            to_peer(upper, hg.at[0], hg.at[1], hy_send.at[0], hy_recv.at[0]).start()
            to_peer(lower, hg.at[0], hg.at[far], hy_send.at[1], hy_recv.at[1]).start()

    def relay_h():
        if grid_y > 1:
            wait_for(hg.at[1], hy_recv.at[0])
            wait_for(hg.at[far], hy_recv.at[1])
            for i, (dp, source) in enumerate(((upper, 1), (lower, far))):
                rows = pl.ds(i * half, half)
                to_peer(
                    dp, hg.at[source, :, rows], hg.at[2, :, rows], hr_send.at[i], hr_recv.at[i]
                ).start()

    def transpose_h():
        if grid_y > 1:
            for i in range(2):
                wait_for(hg.at[2, :, pl.ds(i * half, half)], hr_recv.at[i])

        def part(p, carry):
            rows = pl.ds(pl.multiple_of(p * span_rows, span_rows), span_rows)
            for c in range(CHUNK // 256):
                hidden = hg[:, :, rows, pl.ds(c * 256, 256)].reshape(n_dp * span_rows, 256)
                ht[p, pl.ds(c * 256, 256), :] = hidden.T
            return carry

        lax.fori_loop(0, pieces // SPAN, part, 0)

    middle = sec < n_sec - 4

    @pl.when(early)
    def _():
        transpose_w()

    @pl.when(early | middle)
    def _():
        spread_h()

    @pl.when(early)
    def _():
        relay_h()
        transpose_h()

    def backward(step, carry):
        p = pieces - 1 - step
        start = pl.multiple_of(p * T, T)
        rows = pl.ds(start, T)
        window = pl.ds(start, WINDOW)
        own = pl.ds(pl.multiple_of(start + PAD, T), T)
        inner = jnp.zeros((T, 128), F32)
        for k in range(KV_HEADS):
            if k % 2 == 0:

                @pl.when(sec < n_sec - 1)
                def _():
                    for i in (k, k + 1):
                        pltpu.make_async_remote_copy(
                            src_ref=gb.at[i, rows],
                            dst_ref=gb.at[i, rows],
                            send_sem=g_send,
                            recv_sem=g_recv.at[p, i],
                            device_id={"section": sec},
                            device_id_type=MESH,
                        ).wait_recv()

            grads = to_rows(gb[k, rows, :])
            hidden = hb[k, rows, :]
            query = to_rows(hidden)
            keys = kvb[window, pl.ds(k * HEAD_DIM, HEAD_DIM)]
            vals = kvb[window, pl.ds(kv_width + k * HEAD_DIM, HEAD_DIM)]
            probs = pb[p, k]
            product = probs * dot_t(grads, vals)
            total = jnp.sum(product, -1, keepdims=True)
            d_low = ((product - probs * total) * SCALE).astype(BF16)
            probs_t = pt[p, k]
            product_t = probs_t * dot_t(vals, grads)
            total_t = jnp.sum(product_t, 0, keepdims=True)
            d_low_t = ((product_t - probs_t * total_t) * SCALE).astype(BF16)
            d_query = to_lanes(dot(d_low, keys))
            dqb[k] = d_query
            inner = inner + fold_lanes(d_query * hidden.astype(F32))
            dacc[k, window, :] += dot(d_low_t, query)
            dacc[KV_HEADS + k, window, :] += dot(probs_t.astype(BF16), grads)
        d_kv = jnp.concatenate([dacc[i, own, :] for i in range(2 * KV_HEADS)], axis=1).astype(
            BF16
        )
        for c in range(grid_y):
            do[p // SPAN, c, pl.ds(pl.multiple_of((p % SPAN) * T, T), T), :] = d_kv[
                :, c * cols : (c + 1) * cols
            ]
        inner = inner + fold_lanes(d_kv.astype(F32) * kvb[own, :].astype(F32))
        mean = jnp.sum(inner, -1, keepdims=True) / width
        inverse = rb[rows, :][:, :1]

        def send_d_kv():
            q = p // SPAN
            dg[q, 0] = do[q, y]
            for j, dp, peer_x, peer_y in peers[1:]:
                to_peer(dp, do.at[q, peer_y], dg.at[q, j], d_send, d_recv.at[q]).start()

        @pl.when(first & (p % SPAN == 0))
        def _():
            send_d_kv()

        def send_grads(chunks):
            @pl.when(sec > 0)
            def _():
                for k in chunks:
                    pltpu.make_async_remote_copy(
                        src_ref=go.at[k, rows],
                        dst_ref=gb.at[k, rows],
                        send_sem=g_send,
                        recv_sem=g_recv.at[p, k],
                        device_id={"section": sec - 1},
                        device_id_type=MESH,
                    ).start()

        for k in range(KV_HEADS):
            d_hidden = dqb[k] + dot(d_kv, wt[k])
            normed = xb[k, rows, :].astype(F32) * inverse
            moment = d_hidden * normed
            gsum[k] += moment[0:8] + moment[8:16]
            d_inputs = inverse * (d_hidden * gf[k, 0:1, :] - normed * mean)
            go[k, rows, :] = (gb[k, rows, :].astype(F32) + d_inputs).astype(BF16)
            if k < 2:
                send_grads([k])
            elif k == KV_HEADS - 1:
                send_grads([k - 1, k])

        @pl.when((sec > 0) & (p % SPAN == 0))
        def _():
            send_d_kv()

        @pl.when(jnp.logical_not(early | middle) & (step == pieces // 2 + 1))
        def _():
            spread_h()

        return carry

    lax.fori_loop(0, pieces, backward, 0)

    def gain_block(dp):
        column = dp * block
        return gs.at[
            column // CHUNK, :, pl.ds(pl.multiple_of(column % CHUNK, block), block)
        ]

    for k in range(KV_HEADS):
        total = jnp.sum(gsum[k], 0, keepdims=True).astype(BF16).astype(F32)
        gs[k] = jnp.broadcast_to(total, (8, CHUNK))
    own_gain = pltpu.make_async_copy(gain_block(me), gg.at[0], in_sem.at[1])
    own_gain.start()
    for j, dp, peer_x, peer_y in peers[1:]:
        to_peer(dp, gain_block(dp), gg.at[j], s_send, s_recv).start()

    @pl.when(jnp.logical_not(early))
    def _():
        relay_h()
        transpose_h()

    def multiply(step, carry):
        p = pieces // SPAN - 1 - step
        wait_for(dg.at[p, others], d_recv.at[p])
        d_kv = dg[p].reshape(n_dp * span_rows, cols)
        for c in range(CHUNK // 256):
            part = pl.ds(c * 256, 256)
            product = dot(ht[p, part, :], d_kv)
            wacc[part, :] = product + jnp.where(step > 0, wacc[part, :], 0.0)
        return carry

    lax.fori_loop(0, pieces // SPAN - 1, multiply, 0)
    wait_for(dg.at[0, others], d_recv.at[0])
    d_kv = dg[0].reshape(n_dp * span_rows, cols)
    for jy in list(range(1, grid_y)) + [0]:
        peer_y = (y + jy) % grid_y
        part = pl.ds(pl.multiple_of(peer_y * block, block), block)
        total = wacc[part, :] + dot(ht[0, part, :], d_kv)
        if jy == 0:
            out_w[:, pl.ds(pl.multiple_of(y * cols, cols), cols)] = total
        else:
            eo[jy] = total.astype(BF16)
            to_peer(
                x * grid_y + peer_y, eo.at[jy], eg.at[jy], e_send, e_recv.at[jy]
            ).start()

    own_gain.wait()
    wait_for(gg.at[others], s_recv)
    gain_total = gg[0]
    for j in range(1, n_dp):
        gain_total = gain_total + gg[j]
    out_g[...] = gain_total[0:1]

    for jy in range(1, grid_y):
        wait_for(eg.at[jy], e_recv.at[jy])
        source_y = (y + grid_y - jy) % grid_y
        out_w[:, pl.ds(pl.multiple_of(source_y * cols, cols), cols)] = eg[jy].astype(F32)

    if grid_y > 1:
        wait_for(eo.at[pl.ds(1, grid_y - 1)], e_send)
        for i in range(2):
            wait_for(hg.at[0], hy_send.at[i])
            wait_for(hg.at[2, :, pl.ds(i * half, half)], hr_send.at[i])
    wait_for(hg.at[0, pl.ds(1, KV_HEADS - 1)], hx_send)
    wait_for(dg.at[:, others], d_send)
    wait_for(gg.at[others], s_send)

    @pl.when(sec < n_sec - 1)
    def _():
        wait_for(xo, f_send)

    @pl.when(sec > 0)
    def _():
        wait_for(go, g_send)


def local(n_sec, n_dp, tokens, upstream, gains, w_kv, doc_lengths, seg_lengths, block_mask):
    seq_len, width = tokens.shape[1:]
    pieces = seq_len // T
    kv2 = w_kv.shape[2]
    block = width // n_dp
    grid_y = n_dp // KV_HEADS
    cols = kv2 // grid_y
    any_spec = pl.BlockSpec(memory_space=pl.ANY)
    vmem = pl.BlockSpec(memory_space=pltpu.VMEM)
    smem = pl.BlockSpec(memory_space=pltpu.SMEM)
    features = (KV_HEADS, seq_len, CHUNK)
    dma = pltpu.SemaphoreType.DMA
    grad_weight, grad_gain = pl.pallas_call(
        functools.partial(kernel, n_sec, n_dp),
        out_shape=(
            jax.ShapeDtypeStruct((block, kv2), F32),
            jax.ShapeDtypeStruct((1, block), F32),
        ),
        in_specs=[any_spec, any_spec, vmem, any_spec, smem, smem, vmem],
        out_specs=(vmem, vmem),
        scratch_shapes=[
            pltpu.VMEM(features, BF16),
            pltpu.VMEM(features, BF16),
            pltpu.VMEM(features, BF16),
            pltpu.VMEM(features, BF16),
            pltpu.VMEM(features, BF16),
            pltpu.VMEM((KV_HEADS, CHUNK, kv2), BF16),
            pltpu.VMEM((KV_HEADS, kv2, CHUNK), BF16),
            pltpu.VMEM((PAD + seq_len, kv2), BF16),
            pltpu.VMEM((2 * KV_HEADS, PAD + seq_len, HEAD_DIM), F32),
            pltpu.VMEM((pieces, KV_HEADS, GROUP * T, WINDOW), F32),
            pltpu.VMEM((pieces, KV_HEADS, WINDOW, GROUP * T), F32),
            pltpu.VMEM((KV_HEADS, T, CHUNK), F32),
            pltpu.VMEM((seq_len, 128), F32),
            pltpu.VMEM((pieces, T, WINDOW), F32),
            pltpu.VMEM((KV_HEADS, 8, CHUNK), F32),
            pltpu.VMEM((KV_HEADS, 8, CHUNK), F32),
            pltpu.VMEM((KV_HEADS, 8, CHUNK), F32),
            pltpu.VMEM((grid_y, KV_HEADS, seq_len, CHUNK), BF16),
            pltpu.VMEM((pieces // SPAN, CHUNK, n_dp * SPAN * T), BF16),
            pltpu.VMEM((pieces // SPAN, grid_y, SPAN * T, cols), BF16),
            pltpu.VMEM((pieces // SPAN, n_dp, SPAN * T, cols), BF16),
            pltpu.VMEM((CHUNK, cols), F32),
            pltpu.VMEM((grid_y, block, cols), BF16),
            pltpu.VMEM((grid_y, block, cols), BF16),
            pltpu.VMEM((n_dp, 8, block), F32),
            dma((KV_HEADS,)),
            dma((KV_HEADS,)),
            dma,
            dma((pieces, KV_HEADS)),
            dma,
            dma((pieces, KV_HEADS)),
            dma,
            dma,
            dma((2,)),
            dma((2,)),
            dma((2,)),
            dma((2,)),
            dma,
            dma((pieces // SPAN,)),
            dma,
            dma((grid_y,)),
            dma,
            dma,
        ],
        compiler_params=pltpu.CompilerParams(
            collective_id=0, has_side_effects=True, vmem_limit_bytes=60 * 1024 * 1024
        ),
        cost_estimate=pl.CostEstimate(
            flops=7 * 10**9, bytes_accessed=12 * 2**20, transcendentals=10**6
        ),
        name="relay",
    )(tokens, upstream, gains, w_kv, doc_lengths, seg_lengths, block_mask)
    return grad_weight[None], grad_gain


def solution(mesh):
    placed = (
        P("dp", None, None),
        P("dp", None, None),
        P("section", None),
        P("section", None, None),
        P("dp", None),
        P("dp", None),
        P("dp", None, None),
    )
    return jax.shard_map(
        functools.partial(local, mesh.shape["section"], mesh.shape["dp"]),
        mesh=mesh,
        in_specs=placed,
        out_specs=(P("section", "dp", None), P("section", "dp")),
        check_vma=False,
    )
```

```python
import functools
import math

import jax
import jax.numpy as jnp
from jax import lax
from jax.experimental import pallas as pl
from jax.experimental.pallas import tpu as pltpu
from jax.sharding import PartitionSpec as P

HEADS = 32
KV_HEADS = 4
GROUP = 8
HEAD_DIM = 128
SEGS = 4
BLK = 16
EPSILON = 1e-06

T = 16
SPAN = 2
WINDOW = 128
PAD = WINDOW - T
CHUNK = GROUP * HEAD_DIM
MESH = pl.DeviceIdType.MESH
F32 = jnp.float32
BF16 = jnp.bfloat16
EXP_SCALE = HEAD_DIM**-0.5 * math.log2(math.e)
SCALE = HEAD_DIM**-0.5


def to_rows(block):
    return jnp.concatenate(
        [block[:, HEAD_DIM * g : HEAD_DIM * (g + 1)] for g in range(GROUP)], axis=0
    )


def to_lanes(block):
    return jnp.concatenate([block[T * g : T * (g + 1)] for g in range(GROUP)], axis=1)


def fold_lanes(block):
    total = block[:, :128]
    for g in range(1, block.shape[1] // 128):
        total = total + block[:, 128 * g : 128 * (g + 1)]
    return total


def dot_t(a, b):
    return lax.dot_general(a, b, (((1,), (1,)), ((), ())), preferred_element_type=F32)


def t_dot(a, b):
    return lax.dot_general(a, b, (((0,), (0,)), ((), ())), preferred_element_type=F32)


def dot(a, b):
    return jnp.dot(a, b, preferred_element_type=F32)


def kernel(
    n_sec,
    n_dp,
    tok,
    ups,
    gain,
    w,
    docs,
    segs,
    table,
    out_w,
    out_g,
    xb,
    hb,
    gb,
    xo,
    go,
    wb,
    wt,
    kvb,
    dacc,
    pb,
    pt,
    dqb,
    rb,
    bias,
    gf,
    gsum,
    gs,
    hg,
    ht,
    do,
    dg,
    wacc,
    eo,
    eg,
    gg,
    w_sem,
    in_sem,
    f_send,
    f_recv,
    g_send,
    g_recv,
    hx_send,
    hx_recv,
    hy_send,
    hy_recv,
    hr_send,
    hr_recv,
    d_send,
    d_recv,
    e_send,
    e_recv,
    s_send,
    s_recv,
):
    sec = lax.axis_index("section")
    me = lax.axis_index("dp")
    seq_len = xb.shape[1]
    pieces = seq_len // T
    width = KV_HEADS * CHUNK
    kv_width = KV_HEADS * HEAD_DIM
    block = width // n_dp
    grid_y = n_dp // KV_HEADS
    cols = 2 * kv_width // grid_y
    x, y = me // grid_y, me % grid_y
    span_rows = SPAN * T
    first = sec == 0
    last = sec == n_sec - 1
    early = sec < (n_sec + 3) // 4

    w_copies = [
        pltpu.make_async_copy(w.at[0, pl.ds(k * CHUNK, CHUNK)], wb.at[k], w_sem.at[k])
        for k in range(KV_HEADS)
    ]
    tok_copies = [
        pltpu.make_async_copy(tok.at[0, :, pl.ds(k * CHUNK, CHUNK)], xb.at[k], in_sem.at[k])
        for k in range(KV_HEADS)
    ]
    ups_copies = [
        pltpu.make_async_copy(ups.at[0, :, pl.ds(k * CHUNK, CHUNK)], xo.at[k], in_sem.at[k])
        for k in range(KV_HEADS)
    ]

    @pl.when(first)
    def _():
        for copy in tok_copies:
            copy.start()

    for copy in w_copies:
        copy.start()

    @pl.when(last)
    def _():
        for copy in ups_copies:
            copy.start()

    barrier = pltpu.get_barrier_semaphore()

    @pl.when(sec > 0)
    def _():
        pl.semaphore_signal(barrier, inc=1, device_id={"section": sec - 1}, device_id_type=MESH)

    @pl.when(sec < n_sec - 1)
    def _():
        pl.semaphore_signal(barrier, inc=1, device_id={"section": sec + 1}, device_id_type=MESH)

    for j in range(1, n_dp):
        pl.semaphore_signal(
            barrier, inc=1, device_id={"dp": (me + j) % n_dp}, device_id_type=MESH
        )

    kvb[pl.ds(0, PAD), :] = jnp.zeros((PAD, 2 * kv_width), BF16)
    dacc[...] = jnp.zeros_like(dacc)
    gsum[...] = jnp.zeros_like(gsum)
    for k in range(KV_HEADS):
        gf[k] = jnp.broadcast_to(
            gain[:, pl.ds(k * CHUNK, CHUNK)].astype(F32), (8, CHUNK)
        )

    doc_ends = [docs[0, 0]]
    for d in range(1, docs.shape[1] - 1):
        doc_ends.append(doc_ends[-1] + docs[0, d])

    def doc_of(positions):
        total = jnp.zeros_like(positions)
        for end in doc_ends:
            total = total + jnp.where(positions >= end, 1, 0)
        return total

    row = lax.broadcasted_iota(jnp.int32, (T, WINDOW), 0)
    column = lax.broadcasted_iota(jnp.int32, (T, WINDOW), 1)

    blocks = seq_len // BLK
    opened = table[:, 0, :].astype(BF16)
    block_row = lax.broadcasted_iota(jnp.int32, (blocks, WINDOW), 0)
    block_column = lax.broadcasted_iota(jnp.int32, (blocks, WINDOW), 1) // BLK
    for p in range(pieces):
        queries = row + p * T
        keys = column + (p * T - PAD)
        spread = (block_row == block_column + (p * T - PAD) // BLK).astype(BF16)
        line = dot(opened, spread)[p : p + 1]
        allowed = (
            (keys >= 0)
            & (keys <= queries)
            & (doc_of(keys) == doc_of(queries))
            & ((column // BLK == PAD // BLK) | (line > 0.5))
        )
        bias[p] = jnp.where(allowed, 0.0, -1e30)

    @pl.when(last)
    def _():
        for copy in ups_copies:
            copy.wait()
        sizes = [segs[0, i] for i in range(SEGS)]

        def scale_piece(p, carry):
            rows = pl.ds(pl.multiple_of(p * T, T), T)
            positions = row + p * T
            count = jnp.zeros((T, WINDOW), jnp.int32) + sizes[0]
            end = sizes[0]
            for i in range(1, SEGS):
                count = jnp.where(positions >= end, sizes[i], count)
                end = end + sizes[i]
            factor = seq_len / (SEGS * count.astype(F32))
            factor = jnp.concatenate([factor] * (CHUNK // WINDOW), axis=1)
            for k in range(KV_HEADS):
                gb[k, rows, :] = (xo[k, rows, :].astype(F32) * factor).astype(BF16)
            return carry

        lax.fori_loop(0, pieces, scale_piece, 0)

    @pl.when(first)
    def _():
        for copy in tok_copies:
            copy.wait()

    def transpose_w():
        def part(i, carry):
            k, c = i // 4, i % 4
            source = pl.ds(pl.multiple_of(c * 256, 256), 256)
            for n in range(2 * kv_width // 256):
                wt[k, pl.ds(n * 256, 256), source] = wb[k, source, pl.ds(n * 256, 256)].T
            return carry

        lax.fori_loop(0, KV_HEADS * (CHUNK // 256), part, 0)

    @pl.when(jnp.logical_not(early))
    def _():
        for copy in w_copies:
            copy.wait()
        transpose_w()

    before, after = (sec + n_sec - 1) // n_sec, (2 * n_sec - 2 - sec) // n_sec
    pl.semaphore_wait(barrier, n_dp - 1 + before + after)

    def forward(p, carry):
        start = pl.multiple_of(p * T, T)
        rows = pl.ds(start, T)
        acc = jnp.zeros((T, 2 * kv_width), F32)
        squares = jnp.zeros((T, 128), F32)
        for k in range(KV_HEADS):
            arrival = pltpu.make_async_remote_copy(
                src_ref=xb.at[k, rows],
                dst_ref=xb.at[k, rows],
                send_sem=f_send,
                recv_sem=f_recv.at[p, k],
                device_id={"section": sec},
                device_id_type=MESH,
            )

            @pl.when(sec > 0)
            def _():
                arrival.wait_recv()

            @pl.when(early & (p == 0))
            def _():
                w_copies[k].wait()

            values = xb[k, rows, :].astype(F32)
            squares = squares + fold_lanes(values * values)
            acc = acc + dot((values * gf[k, 0:1, :]).astype(BF16), wb[k])
        inverse = lax.rsqrt(jnp.sum(squares, -1, keepdims=True) / width + EPSILON)
        rb[rows, :] = jnp.broadcast_to(inverse, (T, 128))
        kvb[pl.ds(pl.multiple_of(start + PAD, T), T), :] = (acc * inverse).astype(BF16)
        window = pl.ds(start, WINDOW)
        bias_rows = jnp.concatenate([bias[p]] * GROUP, axis=0)
        for k in range(KV_HEADS):
            values = xb[k, rows, :].astype(F32)
            hidden = (values * inverse * gf[k, 0:1, :]).astype(BF16)
            hb[k, rows, :] = hidden
            keys = kvb[window, pl.ds(k * HEAD_DIM, HEAD_DIM)]
            vals = kvb[window, pl.ds(kv_width + k * HEAD_DIM, HEAD_DIM)]
            scores = dot_t(to_rows(hidden), keys)
            raw = jnp.exp2(scores * EXP_SCALE + bias_rows)
            share = 1.0 / jnp.sum(raw, -1, keepdims=True)
            mixed = dot(raw.astype(BF16), vals) * share
            xo[k, rows, :] = (values + to_lanes(mixed)).astype(BF16)
            probs = raw * share
            pb[p, k] = probs
            pt[p, k] = probs.T

        @pl.when(sec < n_sec - 1)
        def _():
            for k in range(KV_HEADS):
                pltpu.make_async_remote_copy(
                    src_ref=xo.at[k, rows],
                    dst_ref=xb.at[k, rows],
                    send_sem=f_send,
                    recv_sem=f_recv.at[p, k],
                    device_id={"section": sec + 1},
                    device_id_type=MESH,
                ).start()

        return carry

    lax.fori_loop(0, pieces, forward, 0)

    def to_peer(dp, src, dst, send_sem, recv_sem):
        return pltpu.make_async_remote_copy(
            src_ref=src,
            dst_ref=dst,
            send_sem=send_sem,
            recv_sem=recv_sem,
            device_id={"dp": dp},
            device_id_type=MESH,
        )

    def wait_for(ref, sem):
        pltpu.make_async_copy(ref, ref, sem).wait()

    peers = []
    for jy in range(grid_y):
        for jx in range(KV_HEADS):
            peer_x, peer_y = (x + jx) % KV_HEADS, (y + jy) % grid_y
            peers.append((jy * KV_HEADS + jx, peer_x * grid_y + peer_y, peer_x, peer_y))
    others = pl.ds(1, n_dp - 1)

    upper, lower = x * grid_y + (y + 1) % grid_y, x * grid_y + (y + grid_y - 1) % grid_y
    half = seq_len // 2
    far = grid_y - 1

    own_hidden = pltpu.make_async_copy(hb.at[x], hg.at[0, 0], in_sem.at[0])
    own_hidden.start()
    for jx in range(1, KV_HEADS):
        peer_x = (x + jx) % KV_HEADS
        to_peer(peer_x * grid_y + y, hb.at[peer_x], hg.at[0, jx], hx_send, hx_recv).start()

    def spread_h():
        own_hidden.wait()
        wait_for(hg.at[0, pl.ds(1, KV_HEADS - 1)], hx_recv)
        if grid_y > 1:
            to_peer(upper, hg.at[0], hg.at[1], hy_send.at[0], hy_recv.at[0]).start()
            to_peer(lower, hg.at[0], hg.at[far], hy_send.at[1], hy_recv.at[1]).start()

    def relay_h():
        if grid_y > 1:
            wait_for(hg.at[1], hy_recv.at[0])
            wait_for(hg.at[far], hy_recv.at[1])
            for i, (dp, source) in enumerate(((upper, 1), (lower, far))):
                rows = pl.ds(i * half, half)
                to_peer(
                    dp, hg.at[source, :, rows], hg.at[2, :, rows], hr_send.at[i], hr_recv.at[i]
                ).start()

    def transpose_h():
        if grid_y > 1:
            for i in range(2):
                wait_for(hg.at[2, :, pl.ds(i * half, half)], hr_recv.at[i])

        def part(p, carry):
            rows = pl.ds(pl.multiple_of(p * span_rows, span_rows), span_rows)
            for c in range(CHUNK // 256):
                hidden = hg[:, :, rows, pl.ds(c * 256, 256)].reshape(n_dp * span_rows, 256)
                ht[p, pl.ds(c * 256, 256), :] = hidden.T
            return carry

        lax.fori_loop(0, pieces // SPAN, part, 0)

    late = jnp.logical_not(early) & (sec >= n_sec - 3)
    middle = jnp.logical_not(early | late)
    base = 3 * n_sec // 8
    relay_turn = 2 * (sec - base)
    late_turn = 2 * pieces // 3 - 3 * (n_sec - 1 - sec)

    @pl.when(early)
    def _():
        transpose_w()

    @pl.when(early | middle)
    def _():
        spread_h()

    @pl.when(early)
    def _():
        relay_h()
        transpose_h()

    def backward(step, carry):
        p = pieces - 1 - step
        start = pl.multiple_of(p * T, T)
        rows = pl.ds(start, T)
        window = pl.ds(start, WINDOW)
        own = pl.ds(pl.multiple_of(start + PAD, T), T)
        previous = pl.ds(start, PAD)
        own_keys, own_vals = [], []
        inner = jnp.zeros((T, 128), F32)
        for k in range(KV_HEADS):
            if k % 2 == 0:

                @pl.when(sec < n_sec - 1)
                def _():
                    for i in (k, k + 1):
                        pltpu.make_async_remote_copy(
                            src_ref=gb.at[i, rows],
                            dst_ref=gb.at[i, rows],
                            send_sem=g_send,
                            recv_sem=g_recv.at[p, i],
                            device_id={"section": sec},
                            device_id_type=MESH,
                        ).wait_recv()

            grads = to_rows(gb[k, rows, :])
            hidden = hb[k, rows, :]
            query = to_rows(hidden)
            keys = kvb[window, pl.ds(k * HEAD_DIM, HEAD_DIM)]
            vals = kvb[window, pl.ds(kv_width + k * HEAD_DIM, HEAD_DIM)]
            probs = pb[p, k]
            product = probs * dot_t(grads, vals)
            total = jnp.sum(product, -1, keepdims=True)
            d_low = ((product - probs * total) * SCALE).astype(BF16)
            probs_t = pt[p, k]
            product_t = probs_t * dot_t(vals, grads)
            total_t = jnp.sum(product_t, 0, keepdims=True)
            d_low_t = ((product_t - probs_t * total_t) * SCALE).astype(BF16)
            d_query = to_lanes(dot(d_low, keys))
            dqb[k] = d_query
            inner = inner + fold_lanes(d_query * hidden.astype(F32))
            d_vals = dot(probs_t.astype(BF16), grads)
            d_keys = dot(d_low_t, query)
            own_vals.append(dacc[KV_HEADS + k, own, :] + d_vals[PAD:])
            own_keys.append(dacc[k, own, :] + d_keys[PAD:])
            dacc[KV_HEADS + k, previous, :] += d_vals[:PAD]
            dacc[k, previous, :] += d_keys[:PAD]
        d_keys = jnp.concatenate(own_keys, axis=1).astype(BF16)
        d_vals = jnp.concatenate(own_vals, axis=1).astype(BF16)
        d_kv = jnp.concatenate([d_keys, d_vals], axis=1)
        for c in range(grid_y):
            do[p // SPAN, c, pl.ds(pl.multiple_of((p % SPAN) * T, T), T), :] = d_kv[
                :, c * cols : (c + 1) * cols
            ]
        inner = inner + fold_lanes(d_kv.astype(F32) * kvb[own, :].astype(F32))
        mean = jnp.sum(inner, -1, keepdims=True) / width
        inverse = rb[rows, :][:, :1]

        def send_d_kv():
            q = p // SPAN
            dg[q, 0] = do[q, y]
            for j, dp, peer_x, peer_y in peers[1:]:
                to_peer(dp, do.at[q, peer_y], dg.at[q, j], d_send, d_recv.at[q]).start()

        def send_grads(chunks):
            @pl.when(sec > 0)
            def _():
                for k in chunks:
                    pltpu.make_async_remote_copy(
                        src_ref=go.at[k, rows],
                        dst_ref=gb.at[k, rows],
                        send_sem=g_send,
                        recv_sem=g_recv.at[p, k],
                        device_id={"section": sec - 1},
                        device_id_type=MESH,
                    ).start()

        for k in range(KV_HEADS):
            d_hidden = dot(d_vals, wt[k, pl.ds(kv_width, kv_width), :]) + dqb[k]
            d_hidden = d_hidden + dot(d_keys, wt[k, pl.ds(0, kv_width), :])
            normed = xb[k, rows, :].astype(F32) * inverse
            moment = d_hidden * normed
            gsum[k] += moment[0:8] + moment[8:16]
            d_inputs = inverse * (d_hidden * gf[k, 0:1, :] - normed * mean)
            go[k, rows, :] = (gb[k, rows, :].astype(F32) + d_inputs).astype(BF16)
            if k == 0:

                @pl.when(first & (p % SPAN == 0))
                def _():
                    send_d_kv()

            if k < 2:
                send_grads([k])
            elif k == KV_HEADS - 1:
                send_grads([k - 1, k])

        @pl.when((sec > 0) & (p % SPAN == 0))
        def _():
            send_d_kv()

        @pl.when(late & (step == late_turn))
        def _():
            spread_h()

        @pl.when(
            middle
            & (
                (step == relay_turn)
                | ((step == 0) & (relay_turn < 0))
                | ((step == pieces - 1) & (relay_turn >= pieces))
            )
        )
        def _():
            relay_h()

        return carry

    lax.fori_loop(0, pieces, backward, 0)

    def gain_block(dp):
        column = dp * block
        return gs.at[
            column // CHUNK, :, pl.ds(pl.multiple_of(column % CHUNK, block), block)
        ]

    for k in range(KV_HEADS):
        total = jnp.sum(gsum[k], 0, keepdims=True).astype(BF16).astype(F32)
        gs[k] = jnp.broadcast_to(total, (8, CHUNK))
    own_gain = pltpu.make_async_copy(gain_block(me), gg.at[0], in_sem.at[1])
    own_gain.start()
    for j, dp, peer_x, peer_y in peers[1:]:
        to_peer(dp, gain_block(dp), gg.at[j], s_send, s_recv).start()

    @pl.when(late)
    def _():
        relay_h()

    @pl.when(jnp.logical_not(early))
    def _():
        transpose_h()

    def multiply(step, carry):
        p = pieces // SPAN - 1 - step
        wait_for(dg.at[p, others], d_recv.at[p])
        d_kv = dg[p].reshape(n_dp * span_rows, cols)
        for c in range(CHUNK // 256):
            part = pl.ds(c * 256, 256)
            product = dot(ht[p, part, :], d_kv)
            wacc[part, :] = product + jnp.where(step > 0, wacc[part, :], 0.0)
        return carry

    lax.fori_loop(0, pieces // SPAN - 1, multiply, 0)
    wait_for(dg.at[0, others], d_recv.at[0])
    d_kv = dg[0].reshape(n_dp * span_rows, cols)
    for jy in list(range(1, grid_y)) + [0]:
        peer_y = (y + jy) % grid_y
        part = pl.ds(pl.multiple_of(peer_y * block, block), block)
        total = wacc[part, :] + dot(ht[0, part, :], d_kv)
        if jy == 0:
            out_w[:, pl.ds(pl.multiple_of(y * cols, cols), cols)] = total
        else:
            eo[jy] = total.astype(BF16)
            to_peer(
                x * grid_y + peer_y, eo.at[jy], eg.at[jy], e_send, e_recv.at[jy]
            ).start()

    own_gain.wait()
    wait_for(gg.at[others], s_recv)
    gain_total = gg[0]
    for j in range(1, n_dp):
        gain_total = gain_total + gg[j]
    out_g[...] = gain_total[0:1]

    for jy in range(1, grid_y):
        wait_for(eg.at[jy], e_recv.at[jy])
        source_y = (y + grid_y - jy) % grid_y
        out_w[:, pl.ds(pl.multiple_of(source_y * cols, cols), cols)] = eg[jy].astype(F32)

    if grid_y > 1:
        wait_for(eo.at[pl.ds(1, grid_y - 1)], e_send)
        for i in range(2):
            wait_for(hg.at[0], hy_send.at[i])
            wait_for(hg.at[2, :, pl.ds(i * half, half)], hr_send.at[i])
    wait_for(hg.at[0, pl.ds(1, KV_HEADS - 1)], hx_send)
    wait_for(dg.at[:, others], d_send)
    wait_for(gg.at[others], s_send)

    @pl.when(sec < n_sec - 1)
    def _():
        wait_for(xo, f_send)

    @pl.when(sec > 0)
    def _():
        wait_for(go, g_send)


def local(n_sec, n_dp, tokens, upstream, gains, w_kv, doc_lengths, seg_lengths, block_mask):
    seq_len, width = tokens.shape[1:]
    pieces = seq_len // T
    kv2 = w_kv.shape[2]
    block = width // n_dp
    grid_y = n_dp // KV_HEADS
    cols = kv2 // grid_y
    any_spec = pl.BlockSpec(memory_space=pl.ANY)
    vmem = pl.BlockSpec(memory_space=pltpu.VMEM)
    smem = pl.BlockSpec(memory_space=pltpu.SMEM)
    features = (KV_HEADS, seq_len, CHUNK)
    dma = pltpu.SemaphoreType.DMA
    grad_weight, grad_gain = pl.pallas_call(
        functools.partial(kernel, n_sec, n_dp),
        out_shape=(
            jax.ShapeDtypeStruct((block, kv2), F32),
            jax.ShapeDtypeStruct((1, block), F32),
        ),
        in_specs=[any_spec, any_spec, vmem, any_spec, smem, smem, vmem],
        out_specs=(vmem, vmem),
        scratch_shapes=[
            pltpu.VMEM(features, BF16),
            pltpu.VMEM(features, BF16),
            pltpu.VMEM(features, BF16),
            pltpu.VMEM(features, BF16),
            pltpu.VMEM(features, BF16),
            pltpu.VMEM((KV_HEADS, CHUNK, kv2), BF16),
            pltpu.VMEM((KV_HEADS, kv2, CHUNK), BF16),
            pltpu.VMEM((PAD + seq_len, kv2), BF16),
            pltpu.VMEM((2 * KV_HEADS, PAD + seq_len, HEAD_DIM), F32),
            pltpu.VMEM((pieces, KV_HEADS, GROUP * T, WINDOW), F32),
            pltpu.VMEM((pieces, KV_HEADS, WINDOW, GROUP * T), F32),
            pltpu.VMEM((KV_HEADS, T, CHUNK), F32),
            pltpu.VMEM((seq_len, 128), F32),
            pltpu.VMEM((pieces, T, WINDOW), F32),
            pltpu.VMEM((KV_HEADS, 8, CHUNK), F32),
            pltpu.VMEM((KV_HEADS, 8, CHUNK), F32),
            pltpu.VMEM((KV_HEADS, 8, CHUNK), F32),
            pltpu.VMEM((grid_y, KV_HEADS, seq_len, CHUNK), BF16),
            pltpu.VMEM((pieces // SPAN, CHUNK, n_dp * SPAN * T), BF16),
            pltpu.VMEM((pieces // SPAN, grid_y, SPAN * T, cols), BF16),
            pltpu.VMEM((pieces // SPAN, n_dp, SPAN * T, cols), BF16),
            pltpu.VMEM((CHUNK, cols), F32),
            pltpu.VMEM((grid_y, block, cols), BF16),
            pltpu.VMEM((grid_y, block, cols), BF16),
            pltpu.VMEM((n_dp, 8, block), F32),
            dma((KV_HEADS,)),
            dma((KV_HEADS,)),
            dma,
            dma((pieces, KV_HEADS)),
            dma,
            dma((pieces, KV_HEADS)),
            dma,
            dma,
            dma((2,)),
            dma((2,)),
            dma((2,)),
            dma((2,)),
            dma,
            dma((pieces // SPAN,)),
            dma,
            dma((grid_y,)),
            dma,
            dma,
        ],
        compiler_params=pltpu.CompilerParams(
            collective_id=0, has_side_effects=True, vmem_limit_bytes=52 * 1024 * 1024
        ),
        cost_estimate=pl.CostEstimate(
            flops=7 * 10**9, bytes_accessed=12 * 2**20, transcendentals=10**6
        ),
        name="relay",
    )(tokens, upstream, gains, w_kv, doc_lengths, seg_lengths, block_mask.transpose(1, 0, 2))
    return grad_weight[None], grad_gain


def solution(mesh):
    placed = (
        P("dp", None, None),
        P("dp", None, None),
        P("section", None),
        P("section", None, None),
        P("dp", None),
        P("dp", None),
        P("dp", None, None),
    )
    return jax.shard_map(
        functools.partial(local, mesh.shape["section"], mesh.shape["dp"]),
        mesh=mesh,
        in_specs=placed,
        out_specs=(P("section", "dp", None), P("section", "dp")),
        check_vma=False,
    )
```

```python
import functools
import math

import jax
import jax.numpy as jnp
from jax import lax
from jax.experimental import pallas as pl
from jax.experimental.pallas import tpu as pltpu
from jax.sharding import PartitionSpec as P

HEADS = 32
KV_HEADS = 4
GROUP = 8
HEAD_DIM = 128
SEGS = 4
BLK = 16
EPSILON = 1e-06

T = 16
SPAN = 2
WINDOW = 128
PAD = WINDOW - T
CHUNK = GROUP * HEAD_DIM
MESH = pl.DeviceIdType.MESH
F32 = jnp.float32
BF16 = jnp.bfloat16
EXP_SCALE = HEAD_DIM**-0.5 * math.log2(math.e)
SCALE = HEAD_DIM**-0.5


def to_rows(block):
    return jnp.concatenate(
        [block[:, HEAD_DIM * g : HEAD_DIM * (g + 1)] for g in range(GROUP)], axis=0
    )


def to_lanes(block):
    return jnp.concatenate([block[T * g : T * (g + 1)] for g in range(GROUP)], axis=1)


def fold_lanes(block):
    total = block[:, :128]
    for g in range(1, block.shape[1] // 128):
        total = total + block[:, 128 * g : 128 * (g + 1)]
    return total


def dot_t(a, b):
    return lax.dot_general(a, b, (((1,), (1,)), ((), ())), preferred_element_type=F32)


def t_dot(a, b):
    return lax.dot_general(a, b, (((0,), (0,)), ((), ())), preferred_element_type=F32)


def dot(a, b):
    return jnp.dot(a, b, preferred_element_type=F32)


def kernel(
    n_sec,
    n_dp,
    tok,
    ups,
    gain,
    w,
    docs,
    segs,
    table,
    out_w,
    out_g,
    xb,
    hb,
    gb,
    xo,
    go,
    wb,
    wt,
    kb,
    vb,
    dk_acc,
    dv_acc,
    pb,
    pt,
    dqb,
    rb,
    bias,
    gf,
    gsum,
    gs,
    hg,
    ht,
    do,
    dg,
    wacc,
    eo,
    eg,
    gg,
    w_sem,
    in_sem,
    f_send,
    f_recv,
    g_send,
    g_recv,
    hx_send,
    hx_recv,
    hy_send,
    hy_recv,
    hr_send,
    hr_recv,
    d_send,
    d_recv,
    e_send,
    e_recv,
    s_send,
    s_recv,
):
    sec = lax.axis_index("section")
    me = lax.axis_index("dp")
    seq_len = xb.shape[1]
    pieces = seq_len // T
    width = KV_HEADS * CHUNK
    kv_width = KV_HEADS * HEAD_DIM
    block = width // n_dp
    grid_y = n_dp // KV_HEADS
    cols = 2 * kv_width // grid_y
    x, y = me // grid_y, me % grid_y
    span_rows = SPAN * T
    first = sec == 0
    last = sec == n_sec - 1
    early = sec < (n_sec + 3) // 4

    w_copies = [
        pltpu.make_async_copy(w.at[0, pl.ds(k * CHUNK, CHUNK)], wb.at[k], w_sem.at[k])
        for k in range(KV_HEADS)
    ]
    tok_copies = [
        pltpu.make_async_copy(tok.at[0, :, pl.ds(k * CHUNK, CHUNK)], xb.at[k], in_sem.at[k])
        for k in range(KV_HEADS)
    ]
    ups_copies = [
        pltpu.make_async_copy(ups.at[0, :, pl.ds(k * CHUNK, CHUNK)], xo.at[k], in_sem.at[k])
        for k in range(KV_HEADS)
    ]

    @pl.when(first)
    def _():
        for copy in tok_copies:
            copy.start()

    for copy in w_copies:
        copy.start()

    @pl.when(last)
    def _():
        for copy in ups_copies:
            copy.start()

    barrier = pltpu.get_barrier_semaphore()

    @pl.when(sec > 0)
    def _():
        pl.semaphore_signal(barrier, inc=1, device_id={"section": sec - 1}, device_id_type=MESH)

    @pl.when(sec < n_sec - 1)
    def _():
        pl.semaphore_signal(barrier, inc=1, device_id={"section": sec + 1}, device_id_type=MESH)

    for j in range(1, n_dp):
        pl.semaphore_signal(
            barrier, inc=1, device_id={"dp": (me + j) % n_dp}, device_id_type=MESH
        )

    kb[pl.ds(0, PAD), :] = jnp.zeros((PAD, kv_width), BF16)
    vb[pl.ds(0, PAD), :] = jnp.zeros((PAD, kv_width), BF16)
    dk_acc[...] = jnp.zeros_like(dk_acc)
    dv_acc[...] = jnp.zeros_like(dv_acc)
    gsum[...] = jnp.zeros_like(gsum)
    for k in range(KV_HEADS):
        gf[k] = jnp.broadcast_to(
            gain[:, pl.ds(k * CHUNK, CHUNK)].astype(F32), (8, CHUNK)
        )

    doc_ends = [docs[0, 0]]
    for d in range(1, docs.shape[1] - 1):
        doc_ends.append(doc_ends[-1] + docs[0, d])

    def doc_of(positions):
        total = jnp.zeros_like(positions)
        for end in doc_ends:
            total = total + jnp.where(positions >= end, 1, 0)
        return total

    row = lax.broadcasted_iota(jnp.int32, (T, WINDOW), 0)
    column = lax.broadcasted_iota(jnp.int32, (T, WINDOW), 1)

    blocks = seq_len // BLK
    opened = table[:, 0, :].astype(BF16)
    block_row = lax.broadcasted_iota(jnp.int32, (blocks, WINDOW), 0)
    block_column = lax.broadcasted_iota(jnp.int32, (blocks, WINDOW), 1) // BLK
    for p in range(pieces):
        queries = row + p * T
        keys = column + (p * T - PAD)
        spread = (block_row == block_column + (p * T - PAD) // BLK).astype(BF16)
        line = dot(opened, spread)[p : p + 1]
        allowed = (
            (keys >= 0)
            & (keys <= queries)
            & (doc_of(keys) == doc_of(queries))
            & ((column // BLK == PAD // BLK) | (line > 0.5))
        )
        bias[p] = jnp.where(allowed, 0.0, -1e30)

    @pl.when(last)
    def _():
        for copy in ups_copies:
            copy.wait()
        sizes = [segs[0, i] for i in range(SEGS)]

        def scale_piece(p, carry):
            rows = pl.ds(pl.multiple_of(p * T, T), T)
            positions = row + p * T
            count = jnp.zeros((T, WINDOW), jnp.int32) + sizes[0]
            end = sizes[0]
            for i in range(1, SEGS):
                count = jnp.where(positions >= end, sizes[i], count)
                end = end + sizes[i]
            factor = seq_len / (SEGS * count.astype(F32))
            factor = jnp.concatenate([factor] * (CHUNK // WINDOW), axis=1)
            for k in range(KV_HEADS):
                gb[k, rows, :] = (xo[k, rows, :].astype(F32) * factor).astype(BF16)
            return carry

        lax.fori_loop(0, pieces, scale_piece, 0)

    @pl.when(first)
    def _():
        for copy in tok_copies:
            copy.wait()

    def transpose_w():
        def part(i, carry):
            k, c = i // 4, i % 4
            source = pl.ds(pl.multiple_of(c * 256, 256), 256)
            for n in range(2 * kv_width // 256):
                wt[k, pl.ds(n * 256, 256), source] = wb[k, source, pl.ds(n * 256, 256)].T
            return carry

        lax.fori_loop(0, KV_HEADS * (CHUNK // 256), part, 0)

    @pl.when(jnp.logical_not(early))
    def _():
        for copy in w_copies:
            copy.wait()
        transpose_w()

    before, after = (sec + n_sec - 1) // n_sec, (2 * n_sec - 2 - sec) // n_sec
    pl.semaphore_wait(barrier, n_dp - 1 + before + after)

    def forward(p, carry):
        start = pl.multiple_of(p * T, T)
        rows = pl.ds(start, T)
        keys_part, vals_part = pl.ds(0, kv_width), pl.ds(kv_width, kv_width)
        new_keys = jnp.zeros((T, kv_width), F32)
        new_vals = jnp.zeros((T, kv_width), F32)
        scaled = []
        squares = jnp.zeros((T, 128), F32)
        for k in range(KV_HEADS):
            arrival = pltpu.make_async_remote_copy(
                src_ref=xb.at[k, rows],
                dst_ref=xb.at[k, rows],
                send_sem=f_send,
                recv_sem=f_recv.at[p, k],
                device_id={"section": sec},
                device_id_type=MESH,
            )

            @pl.when(sec > 0)
            def _():
                arrival.wait_recv()

            @pl.when(early & (p == 0))
            def _():
                w_copies[k].wait()

            values = xb[k, rows, :].astype(F32)
            squares = squares + fold_lanes(values * values)
            scaled.append((values * gf[k, 0:1, :]).astype(BF16))
            new_keys = new_keys + dot(scaled[k], wb[k, :, keys_part])
            if k > 0:
                new_vals = new_vals + dot(scaled[k - 1], wb[k - 1, :, vals_part])
        inverse = lax.rsqrt(jnp.sum(squares, -1, keepdims=True) / width + EPSILON)
        rb[rows, :] = jnp.broadcast_to(inverse, (T, 128))
        own = pl.ds(pl.multiple_of(start + PAD, T), T)
        window = pl.ds(start, WINDOW)
        kb[own, :] = (new_keys * inverse).astype(BF16)
        bias_rows = jnp.concatenate([bias[p]] * GROUP, axis=0)
        raws = []
        for k in range(KV_HEADS):
            values = xb[k, rows, :].astype(F32)
            hidden = (values * inverse * gf[k, 0:1, :]).astype(BF16)
            hb[k, rows, :] = hidden
            keys = kb[window, pl.ds(k * HEAD_DIM, HEAD_DIM)]
            scores = dot_t(to_rows(hidden), keys)
            raws.append(jnp.exp2(scores * EXP_SCALE + bias_rows))
        last_k = KV_HEADS - 1
        new_vals = new_vals + dot(scaled[last_k], wb[last_k, :, vals_part])
        vb[own, :] = (new_vals * inverse).astype(BF16)
        for k in range(KV_HEADS):
            raw = raws[k]
            vals = vb[window, pl.ds(k * HEAD_DIM, HEAD_DIM)]
            share = 1.0 / jnp.sum(raw, -1, keepdims=True)
            mixed = dot(raw.astype(BF16), vals) * share
            xo[k, rows, :] = (xb[k, rows, :].astype(F32) + to_lanes(mixed)).astype(BF16)
            probs = raw * share
            pb[p, k] = probs
            pt[p, k] = probs.T

        @pl.when(sec < n_sec - 1)
        def _():
            for k in range(KV_HEADS):
                pltpu.make_async_remote_copy(
                    src_ref=xo.at[k, rows],
                    dst_ref=xb.at[k, rows],
                    send_sem=f_send,
                    recv_sem=f_recv.at[p, k],
                    device_id={"section": sec + 1},
                    device_id_type=MESH,
                ).start()

        return carry

    lax.fori_loop(0, pieces, forward, 0)

    def to_peer(dp, src, dst, send_sem, recv_sem):
        return pltpu.make_async_remote_copy(
            src_ref=src,
            dst_ref=dst,
            send_sem=send_sem,
            recv_sem=recv_sem,
            device_id={"dp": dp},
            device_id_type=MESH,
        )

    def wait_for(ref, sem):
        pltpu.make_async_copy(ref, ref, sem).wait()

    peers = []
    for jy in range(grid_y):
        for jx in range(KV_HEADS):
            peer_x, peer_y = (x + jx) % KV_HEADS, (y + jy) % grid_y
            peers.append((jy * KV_HEADS + jx, peer_x * grid_y + peer_y, peer_x, peer_y))
    others = pl.ds(1, n_dp - 1)

    upper, lower = x * grid_y + (y + 1) % grid_y, x * grid_y + (y + grid_y - 1) % grid_y
    half = seq_len // 2
    far = grid_y - 1

    own_hidden = pltpu.make_async_copy(hb.at[x], hg.at[0, 0], in_sem.at[0])
    own_hidden.start()
    for jx in range(1, KV_HEADS):
        peer_x = (x + jx) % KV_HEADS
        to_peer(peer_x * grid_y + y, hb.at[peer_x], hg.at[0, jx], hx_send, hx_recv).start()

    def spread_h():
        own_hidden.wait()
        wait_for(hg.at[0, pl.ds(1, KV_HEADS - 1)], hx_recv)
        if grid_y > 1:
            to_peer(upper, hg.at[0], hg.at[1], hy_send.at[0], hy_recv.at[0]).start()
            to_peer(lower, hg.at[0], hg.at[far], hy_send.at[1], hy_recv.at[1]).start()

    def relay_h():
        if grid_y > 1:
            wait_for(hg.at[1], hy_recv.at[0])
            wait_for(hg.at[far], hy_recv.at[1])
            for i, (dp, source) in enumerate(((upper, 1), (lower, far))):
                rows = pl.ds(i * half, half)
                to_peer(
                    dp, hg.at[source, :, rows], hg.at[2, :, rows], hr_send.at[i], hr_recv.at[i]
                ).start()

    def transpose_h():
        if grid_y > 1:
            for i in range(2):
                wait_for(hg.at[2, :, pl.ds(i * half, half)], hr_recv.at[i])

        def part(p, carry):
            rows = pl.ds(pl.multiple_of(p * span_rows, span_rows), span_rows)
            for c in range(CHUNK // 256):
                hidden = hg[:, :, rows, pl.ds(c * 256, 256)].reshape(n_dp * span_rows, 256)
                ht[p, pl.ds(c * 256, 256), :] = hidden.T
            return carry

        lax.fori_loop(0, pieces // SPAN, part, 0)

    late = jnp.logical_not(early) & (sec >= n_sec - 3)
    middle = jnp.logical_not(early | late)
    base = 3 * n_sec // 8
    relay_turn = 2 * (sec - base)
    late_turn = 2 * pieces // 3 - 3 * (n_sec - 1 - sec)

    @pl.when(early)
    def _():
        transpose_w()

    @pl.when(early | middle)
    def _():
        spread_h()

    @pl.when(early)
    def _():
        relay_h()
        transpose_h()

    def backward(step, carry):
        p = pieces - 1 - step
        start = pl.multiple_of(p * T, T)
        rows = pl.ds(start, T)
        window = pl.ds(start, WINDOW)
        own = pl.ds(pl.multiple_of(start + PAD, T), T)
        previous = pl.ds(start, PAD)
        own_keys, own_vals = [], []
        partial = [0.0] * KV_HEADS
        inner = jnp.zeros((T, 128), F32)
        for pair in range(KV_HEADS // 2):
            heads = (2 * pair, 2 * pair + 1)

            @pl.when(sec < n_sec - 1)
            def _():
                for i in heads:
                    pltpu.make_async_remote_copy(
                        src_ref=gb.at[i, rows],
                        dst_ref=gb.at[i, rows],
                        send_sem=g_send,
                        recv_sem=g_recv.at[p, i],
                        device_id={"section": sec},
                        device_id_type=MESH,
                    ).wait_recv()

            grads, d_vals = {}, {}
            for k in heads:
                grads[k] = to_rows(gb[k, rows, :])
                d_vals[k] = dot(pt[p, k].astype(BF16), grads[k])
                own_vals.append(dv_acc[k, own, :] + d_vals[k][PAD:])
            pair_vals = jnp.concatenate(own_vals[-2:], axis=1).astype(BF16)
            d_probs, d_probs_t = {}, {}
            for k in heads:
                vals = vb[window, pl.ds(k * HEAD_DIM, HEAD_DIM)]
                d_probs[k] = dot_t(grads[k], vals)
                d_probs_t[k] = dot_t(vals, grads[k])
            part = pl.ds(kv_width + pair * 2 * HEAD_DIM, 2 * HEAD_DIM)
            for c in range(KV_HEADS):
                partial[c] = partial[c] + dot(pair_vals, wt[c, part, :])
            for k in heads:
                hidden = hb[k, rows, :]
                query = to_rows(hidden)
                keys = kb[window, pl.ds(k * HEAD_DIM, HEAD_DIM)]
                probs = pb[p, k]
                product = probs * d_probs[k]
                total = jnp.sum(product, -1, keepdims=True)
                d_low = ((product - probs * total) * SCALE).astype(BF16)
                probs_t = pt[p, k]
                product_t = probs_t * d_probs_t[k]
                total_t = jnp.sum(product_t, 0, keepdims=True)
                d_low_t = ((product_t - probs_t * total_t) * SCALE).astype(BF16)
                d_keys = dot(d_low_t, query)
                own_keys.append(dk_acc[k, own, :] + d_keys[PAD:])
                d_query = to_lanes(dot(d_low, keys))
                dqb[k] = d_query
                inner = inner + fold_lanes(d_query * hidden.astype(F32))
                dk_acc[k, previous, :] += d_keys[:PAD]
                dv_acc[k, previous, :] += d_vals[k][:PAD]
        d_keys = jnp.concatenate(own_keys, axis=1).astype(BF16)
        d_vals = jnp.concatenate(own_vals, axis=1).astype(BF16)
        d_kv = jnp.concatenate([d_keys, d_vals], axis=1)
        for c in range(grid_y):
            do[p // SPAN, c, pl.ds(pl.multiple_of((p % SPAN) * T, T), T), :] = d_kv[
                :, c * cols : (c + 1) * cols
            ]
        inner = inner + fold_lanes(d_keys.astype(F32) * kb[own, :].astype(F32))
        inner = inner + fold_lanes(d_vals.astype(F32) * vb[own, :].astype(F32))
        mean = jnp.sum(inner, -1, keepdims=True) / width
        inverse = rb[rows, :][:, :1]

        def send_d_kv(part):
            q = p // SPAN
            dg[q, 0, part] = do[q, y, part]
            for j, dp, peer_x, peer_y in peers[1:]:
                to_peer(
                    dp, do.at[q, peer_y, part], dg.at[q, j, part], d_send, d_recv.at[q]
                ).start()

        def send_grads(chunks):
            @pl.when(sec > 0)
            def _():
                for k in chunks:
                    pltpu.make_async_remote_copy(
                        src_ref=go.at[k, rows],
                        dst_ref=gb.at[k, rows],
                        send_sem=g_send,
                        recv_sem=g_recv.at[p, k],
                        device_id={"section": sec - 1},
                        device_id_type=MESH,
                    ).start()

        for k in range(KV_HEADS):
            d_hidden = partial[k] + dqb[k] + dot(d_keys, wt[k, pl.ds(0, kv_width), :])
            normed = xb[k, rows, :].astype(F32) * inverse
            moment = d_hidden * normed
            gsum[k] += moment[0:8] + moment[8:16]
            d_inputs = inverse * (d_hidden * gf[k, 0:1, :] - normed * mean)
            go[k, rows, :] = (gb[k, rows, :].astype(F32) + d_inputs).astype(BF16)
            if k == 0:

                @pl.when(first)
                def _():
                    send_d_kv(pl.ds(pl.multiple_of((p % SPAN) * T, T), T))

            if k < 2:
                send_grads([k])
            elif k == KV_HEADS - 1:
                send_grads([k - 1, k])

        @pl.when((sec > 0) & (p % SPAN == 0))
        def _():
            send_d_kv(pl.ds(0, span_rows))

        @pl.when(late & (step == late_turn))
        def _():
            spread_h()

        @pl.when(
            middle
            & (
                (step == relay_turn)
                | ((step == 0) & (relay_turn < 0))
                | ((step == pieces - 1) & (relay_turn >= pieces))
            )
        )
        def _():
            relay_h()

        return carry

    lax.fori_loop(0, pieces, backward, 0)

    def gain_block(dp):
        column = dp * block
        return gs.at[
            column // CHUNK, :, pl.ds(pl.multiple_of(column % CHUNK, block), block)
        ]

    for k in range(KV_HEADS):
        total = jnp.sum(gsum[k], 0, keepdims=True).astype(BF16).astype(F32)
        gs[k] = jnp.broadcast_to(total, (8, CHUNK))
    own_gain = pltpu.make_async_copy(gain_block(me), gg.at[0], in_sem.at[1])
    own_gain.start()
    for j, dp, peer_x, peer_y in peers[1:]:
        to_peer(dp, gain_block(dp), gg.at[j], s_send, s_recv).start()

    @pl.when(late)
    def _():
        relay_h()

    @pl.when(jnp.logical_not(early))
    def _():
        transpose_h()

    def multiply(step, carry):
        p = pieces // SPAN - 1 - step
        wait_for(dg.at[p, others], d_recv.at[p])
        d_kv = dg[p].reshape(n_dp * span_rows, cols)
        for c in range(CHUNK // 256):
            part = pl.ds(c * 256, 256)
            product = dot(ht[p, part, :], d_kv)
            wacc[part, :] = product + jnp.where(step > 0, wacc[part, :], 0.0)
        return carry

    lax.fori_loop(0, pieces // SPAN - 1, multiply, 0)
    wait_for(dg.at[0, others], d_recv.at[0])
    d_kv = dg[0].reshape(n_dp * span_rows, cols)
    for jy in list(range(1, grid_y)) + [0]:
        peer_y = (y + jy) % grid_y
        part = pl.ds(pl.multiple_of(peer_y * block, block), block)
        total = wacc[part, :] + dot(ht[0, part, :], d_kv)
        if jy == 0:
            out_w[:, pl.ds(pl.multiple_of(y * cols, cols), cols)] = total
        else:
            eo[jy] = total.astype(BF16)
            to_peer(
                x * grid_y + peer_y, eo.at[jy], eg.at[jy], e_send, e_recv.at[jy]
            ).start()

    own_gain.wait()
    wait_for(gg.at[others], s_recv)
    gain_total = gg[0]
    for j in range(1, n_dp):
        gain_total = gain_total + gg[j]
    out_g[...] = gain_total[0:1]

    for jy in range(1, grid_y):
        wait_for(eg.at[jy], e_recv.at[jy])
        source_y = (y + grid_y - jy) % grid_y
        out_w[:, pl.ds(pl.multiple_of(source_y * cols, cols), cols)] = eg[jy].astype(F32)

    if grid_y > 1:
        wait_for(eo.at[pl.ds(1, grid_y - 1)], e_send)
        for i in range(2):
            wait_for(hg.at[0], hy_send.at[i])
            wait_for(hg.at[2, :, pl.ds(i * half, half)], hr_send.at[i])
    wait_for(hg.at[0, pl.ds(1, KV_HEADS - 1)], hx_send)
    wait_for(dg.at[:, others], d_send)
    wait_for(gg.at[others], s_send)

    @pl.when(sec < n_sec - 1)
    def _():
        wait_for(xo, f_send)

    @pl.when(sec > 0)
    def _():
        wait_for(go, g_send)


def local(n_sec, n_dp, tokens, upstream, gains, w_kv, doc_lengths, seg_lengths, block_mask):
    seq_len, width = tokens.shape[1:]
    pieces = seq_len // T
    kv2 = w_kv.shape[2]
    block = width // n_dp
    grid_y = n_dp // KV_HEADS
    cols = kv2 // grid_y
    any_spec = pl.BlockSpec(memory_space=pl.ANY)
    vmem = pl.BlockSpec(memory_space=pltpu.VMEM)
    smem = pl.BlockSpec(memory_space=pltpu.SMEM)
    features = (KV_HEADS, seq_len, CHUNK)
    dma = pltpu.SemaphoreType.DMA
    grad_weight, grad_gain = pl.pallas_call(
        functools.partial(kernel, n_sec, n_dp),
        out_shape=(
            jax.ShapeDtypeStruct((block, kv2), F32),
            jax.ShapeDtypeStruct((1, block), F32),
        ),
        in_specs=[any_spec, any_spec, vmem, any_spec, smem, smem, vmem],
        out_specs=(vmem, vmem),
        scratch_shapes=[
            pltpu.VMEM(features, BF16),
            pltpu.VMEM(features, BF16),
            pltpu.VMEM(features, BF16),
            pltpu.VMEM(features, BF16),
            pltpu.VMEM(features, BF16),
            pltpu.VMEM((KV_HEADS, CHUNK, kv2), BF16),
            pltpu.VMEM((KV_HEADS, kv2, CHUNK), BF16),
            pltpu.VMEM((PAD + seq_len, kv2 // 2), BF16),
            pltpu.VMEM((PAD + seq_len, kv2 // 2), BF16),
            pltpu.VMEM((KV_HEADS, PAD + seq_len, HEAD_DIM), F32),
            pltpu.VMEM((KV_HEADS, PAD + seq_len, HEAD_DIM), F32),
            pltpu.VMEM((pieces, KV_HEADS, GROUP * T, WINDOW), F32),
            pltpu.VMEM((pieces, KV_HEADS, WINDOW, GROUP * T), F32),
            pltpu.VMEM((KV_HEADS, T, CHUNK), F32),
            pltpu.VMEM((seq_len, 128), F32),
            pltpu.VMEM((pieces, T, WINDOW), F32),
            pltpu.VMEM((KV_HEADS, 8, CHUNK), F32),
            pltpu.VMEM((KV_HEADS, 8, CHUNK), F32),
            pltpu.VMEM((KV_HEADS, 8, CHUNK), F32),
            pltpu.VMEM((grid_y, KV_HEADS, seq_len, CHUNK), BF16),
            pltpu.VMEM((pieces // SPAN, CHUNK, n_dp * SPAN * T), BF16),
            pltpu.VMEM((pieces // SPAN, grid_y, SPAN * T, cols), BF16),
            pltpu.VMEM((pieces // SPAN, n_dp, SPAN * T, cols), BF16),
            pltpu.VMEM((CHUNK, cols), F32),
            pltpu.VMEM((grid_y, block, cols), BF16),
            pltpu.VMEM((grid_y, block, cols), BF16),
            pltpu.VMEM((n_dp, 8, block), F32),
            dma((KV_HEADS,)),
            dma((KV_HEADS,)),
            dma,
            dma((pieces, KV_HEADS)),
            dma,
            dma((pieces, KV_HEADS)),
            dma,
            dma,
            dma((2,)),
            dma((2,)),
            dma((2,)),
            dma((2,)),
            dma,
            dma((pieces // SPAN,)),
            dma,
            dma((grid_y,)),
            dma,
            dma,
        ],
        compiler_params=pltpu.CompilerParams(
            collective_id=0, has_side_effects=True, vmem_limit_bytes=60 * 1024 * 1024
        ),
        cost_estimate=pl.CostEstimate(
            flops=7 * 10**9, bytes_accessed=12 * 2**20, transcendentals=10**6
        ),
        name="relay",
    )(tokens, upstream, gains, w_kv, doc_lengths, seg_lengths, block_mask.transpose(1, 0, 2))
    return grad_weight[None], grad_gain


def solution(mesh):
    placed = (
        P("dp", None, None),
        P("dp", None, None),
        P("section", None),
        P("section", None, None),
        P("dp", None),
        P("dp", None),
        P("dp", None, None),
    )
    return jax.shard_map(
        functools.partial(local, mesh.shape["section"], mesh.shape["dp"]),
        mesh=mesh,
        in_specs=placed,
        out_specs=(P("section", "dp", None), P("section", "dp")),
        check_vma=False,
    )
```

```python
import functools
import math

import jax
import jax.numpy as jnp
from jax import lax
from jax.experimental import pallas as pl
from jax.experimental.pallas import tpu as pltpu
from jax.sharding import PartitionSpec as P

HEADS = 32
KV_HEADS = 4
GROUP = 8
HEAD_DIM = 128
SEGS = 4
BLK = 16
EPSILON = 1e-06

T = 16
SPAN = 4
WINDOW = 128
PAD = WINDOW - T
CHUNK = GROUP * HEAD_DIM
MESH = pl.DeviceIdType.MESH
F32 = jnp.float32
BF16 = jnp.bfloat16
EXP_SCALE = HEAD_DIM**-0.5 * math.log2(math.e)
SCALE = HEAD_DIM**-0.5


def to_rows(block):
    return jnp.concatenate(
        [block[:, HEAD_DIM * g : HEAD_DIM * (g + 1)] for g in range(GROUP)], axis=0
    )


def to_lanes(block):
    return jnp.concatenate([block[T * g : T * (g + 1)] for g in range(GROUP)], axis=1)


def fold_lanes(block):
    total = block[:, :128]
    for g in range(1, block.shape[1] // 128):
        total = total + block[:, 128 * g : 128 * (g + 1)]
    return total


def dot_t(a, b):
    return lax.dot_general(a, b, (((1,), (1,)), ((), ())), preferred_element_type=F32)


def t_dot(a, b):
    return lax.dot_general(a, b, (((0,), (0,)), ((), ())), preferred_element_type=F32)


def dot(a, b):
    return jnp.dot(a, b, preferred_element_type=F32)


def kernel(
    n_sec,
    n_dp,
    tok,
    ups,
    gain,
    w,
    docs,
    segs,
    table,
    out_w,
    out_g,
    xb,
    hb,
    gb,
    xo,
    go,
    wb,
    wt,
    kb,
    vb,
    dk_acc,
    dv_acc,
    pb,
    pt,
    dqb,
    rb,
    bias,
    gf,
    gsum,
    gs,
    hg,
    ht,
    do,
    dg,
    wacc,
    eo,
    eg,
    gg,
    w_sem,
    in_sem,
    f_send,
    f_recv,
    g_send,
    g_recv,
    hx_send,
    hx_recv,
    hy_send,
    hy_recv,
    hr_send,
    hr_recv,
    d_send,
    d_recv,
    e_send,
    e_recv,
    s_send,
    s_recv,
):
    sec = lax.axis_index("section")
    me = lax.axis_index("dp")
    seq_len = xb.shape[1]
    pieces = seq_len // T
    width = KV_HEADS * CHUNK
    kv_width = KV_HEADS * HEAD_DIM
    block = width // n_dp
    grid_y = n_dp // KV_HEADS
    cols = 2 * kv_width // grid_y
    x, y = me // grid_y, me % grid_y
    span_rows = SPAN * T
    first = sec == 0
    last = sec == n_sec - 1
    early = sec < (n_sec + 3) // 4

    w_copies = [
        pltpu.make_async_copy(w.at[0, pl.ds(k * CHUNK, CHUNK)], wb.at[k], w_sem.at[k])
        for k in range(KV_HEADS)
    ]
    tok_copies = [
        pltpu.make_async_copy(tok.at[0, :, pl.ds(k * CHUNK, CHUNK)], xb.at[k], in_sem.at[k])
        for k in range(KV_HEADS)
    ]
    ups_copies = [
        pltpu.make_async_copy(ups.at[0, :, pl.ds(k * CHUNK, CHUNK)], xo.at[k], in_sem.at[k])
        for k in range(KV_HEADS)
    ]

    @pl.when(first)
    def _():
        for copy in tok_copies:
            copy.start()

    for copy in w_copies:
        copy.start()

    @pl.when(last)
    def _():
        for copy in ups_copies:
            copy.start()

    barrier = pltpu.get_barrier_semaphore()

    @pl.when(sec > 0)
    def _():
        pl.semaphore_signal(barrier, inc=1, device_id={"section": sec - 1}, device_id_type=MESH)

    @pl.when(sec < n_sec - 1)
    def _():
        pl.semaphore_signal(barrier, inc=1, device_id={"section": sec + 1}, device_id_type=MESH)

    for j in range(1, n_dp):
        pl.semaphore_signal(
            barrier, inc=1, device_id={"dp": (me + j) % n_dp}, device_id_type=MESH
        )

    kb[pl.ds(0, PAD), :] = jnp.zeros((PAD, kv_width), BF16)
    vb[pl.ds(0, PAD), :] = jnp.zeros((PAD, kv_width), BF16)
    dk_acc[...] = jnp.zeros_like(dk_acc)
    dv_acc[...] = jnp.zeros_like(dv_acc)
    gsum[...] = jnp.zeros_like(gsum)
    for k in range(KV_HEADS):
        gf[k] = jnp.broadcast_to(
            gain[:, pl.ds(k * CHUNK, CHUNK)].astype(F32), (8, CHUNK)
        )

    doc_ends = [docs[0, 0]]
    for d in range(1, docs.shape[1] - 1):
        doc_ends.append(doc_ends[-1] + docs[0, d])

    def doc_of(positions):
        total = jnp.zeros_like(positions)
        for end in doc_ends:
            total = total + jnp.where(positions >= end, 1, 0)
        return total

    row = lax.broadcasted_iota(jnp.int32, (T, WINDOW), 0)
    column = lax.broadcasted_iota(jnp.int32, (T, WINDOW), 1)

    blocks = seq_len // BLK
    opened = table[:, 0, :].astype(BF16)
    block_row = lax.broadcasted_iota(jnp.int32, (blocks, WINDOW), 0)
    block_column = lax.broadcasted_iota(jnp.int32, (blocks, WINDOW), 1) // BLK
    for p in range(pieces):
        queries = row + p * T
        keys = column + (p * T - PAD)
        spread = (block_row == block_column + (p * T - PAD) // BLK).astype(BF16)
        line = dot(opened, spread)[p : p + 1]
        allowed = (
            (keys >= 0)
            & (keys <= queries)
            & (doc_of(keys) == doc_of(queries))
            & ((column // BLK == PAD // BLK) | (line > 0.5))
        )
        bias[p] = jnp.where(allowed, 0.0, -1e30)

    @pl.when(last)
    def _():
        for copy in ups_copies:
            copy.wait()
        sizes = [segs[0, i] for i in range(SEGS)]

        def scale_piece(p, carry):
            rows = pl.ds(pl.multiple_of(p * T, T), T)
            positions = row + p * T
            count = jnp.zeros((T, WINDOW), jnp.int32) + sizes[0]
            end = sizes[0]
            for i in range(1, SEGS):
                count = jnp.where(positions >= end, sizes[i], count)
                end = end + sizes[i]
            factor = seq_len / (SEGS * count.astype(F32))
            factor = jnp.concatenate([factor] * (CHUNK // WINDOW), axis=1)
            for k in range(KV_HEADS):
                gb[k, rows, :] = (xo[k, rows, :].astype(F32) * factor).astype(BF16)
            return carry

        lax.fori_loop(0, pieces, scale_piece, 0)

    @pl.when(first)
    def _():
        for copy in tok_copies:
            copy.wait()

    def transpose_w():
        def part(i, carry):
            k, c = i // 4, i % 4
            source = pl.ds(pl.multiple_of(c * 256, 256), 256)
            for n in range(2 * kv_width // 256):
                wt[k, pl.ds(n * 256, 256), source] = wb[k, source, pl.ds(n * 256, 256)].T
            return carry

        lax.fori_loop(0, KV_HEADS * (CHUNK // 256), part, 0)

    @pl.when(jnp.logical_not(early))
    def _():
        for copy in w_copies:
            copy.wait()
        transpose_w()

    before, after = (sec + n_sec - 1) // n_sec, (2 * n_sec - 2 - sec) // n_sec

    def forward(p, carry):
        start = pl.multiple_of(p * T, T)
        rows = pl.ds(start, T)
        keys_part, vals_part = pl.ds(0, kv_width), pl.ds(kv_width, kv_width)
        new_keys = jnp.zeros((T, kv_width), F32)
        new_vals = jnp.zeros((T, kv_width), F32)
        scaled = []
        squares = jnp.zeros((T, 128), F32)
        for k in range(KV_HEADS):
            arrival = pltpu.make_async_remote_copy(
                src_ref=xb.at[k, rows],
                dst_ref=xb.at[k, rows],
                send_sem=f_send,
                recv_sem=f_recv.at[p, k],
                device_id={"section": sec},
                device_id_type=MESH,
            )

            @pl.when(sec > 0)
            def _():
                arrival.wait_recv()

            @pl.when(early & (p == 0))
            def _():
                w_copies[k].wait()

            values = xb[k, rows, :].astype(F32)
            squares = squares + fold_lanes(values * values)
            scaled.append((values * gf[k, 0:1, :]).astype(BF16))
            new_keys = new_keys + dot(scaled[k], wb[k, :, keys_part])
            if k > 0:
                new_vals = new_vals + dot(scaled[k - 1], wb[k - 1, :, vals_part])
        inverse = lax.rsqrt(jnp.sum(squares, -1, keepdims=True) / width + EPSILON)
        rb[rows, :] = jnp.broadcast_to(inverse, (T, 128))
        own = pl.ds(pl.multiple_of(start + PAD, T), T)
        window = pl.ds(start, WINDOW)
        kb[own, :] = (new_keys * inverse).astype(BF16)
        bias_rows = jnp.concatenate([bias[p]] * GROUP, axis=0)
        raws = []
        for k in range(KV_HEADS):
            values = xb[k, rows, :].astype(F32)
            hidden = (values * inverse * gf[k, 0:1, :]).astype(BF16)
            hb[k, rows, :] = hidden
            keys = kb[window, pl.ds(k * HEAD_DIM, HEAD_DIM)]
            scores = dot_t(to_rows(hidden), keys)
            raws.append(jnp.exp2(scores * EXP_SCALE + bias_rows))
        last_k = KV_HEADS - 1
        new_vals = new_vals + dot(scaled[last_k], wb[last_k, :, vals_part])
        vb[own, :] = (new_vals * inverse).astype(BF16)
        for k in range(KV_HEADS):
            raw = raws[k]
            vals = vb[window, pl.ds(k * HEAD_DIM, HEAD_DIM)]
            share = 1.0 / jnp.sum(raw, -1, keepdims=True)
            mixed = dot(raw.astype(BF16), vals) * share
            xo[k, rows, :] = (xb[k, rows, :].astype(F32) + to_lanes(mixed)).astype(BF16)
            probs = raw * share
            pb[p, k] = probs
            pt[p, k] = probs.T

        @pl.when(p == 0)
        def _():
            pl.semaphore_wait(barrier, n_dp - 1 + before + after)

        @pl.when(sec < n_sec - 1)
        def _():
            for k in range(KV_HEADS):
                pltpu.make_async_remote_copy(
                    src_ref=xo.at[k, rows],
                    dst_ref=xb.at[k, rows],
                    send_sem=f_send,
                    recv_sem=f_recv.at[p, k],
                    device_id={"section": sec + 1},
                    device_id_type=MESH,
                ).start()

        return carry

    lax.fori_loop(0, pieces, forward, 0)

    def to_peer(dp, src, dst, send_sem, recv_sem):
        return pltpu.make_async_remote_copy(
            src_ref=src,
            dst_ref=dst,
            send_sem=send_sem,
            recv_sem=recv_sem,
            device_id={"dp": dp},
            device_id_type=MESH,
        )

    def wait_for(ref, sem):
        pltpu.make_async_copy(ref, ref, sem).wait()

    peers = []
    for jy in range(grid_y):
        for jx in range(KV_HEADS):
            peer_x, peer_y = (x + jx) % KV_HEADS, (y + jy) % grid_y
            peers.append((jy * KV_HEADS + jx, peer_x * grid_y + peer_y, peer_x, peer_y))
    others = pl.ds(1, n_dp - 1)

    upper, lower = x * grid_y + (y + 1) % grid_y, x * grid_y + (y + grid_y - 1) % grid_y
    half = seq_len // 2
    far = grid_y - 1

    own_hidden = pltpu.make_async_copy(hb.at[x], hg.at[0, 0], in_sem.at[0])
    own_hidden.start()
    for jx in range(1, KV_HEADS):
        peer_x = (x + jx) % KV_HEADS
        to_peer(peer_x * grid_y + y, hb.at[peer_x], hg.at[0, jx], hx_send, hx_recv).start()

    def spread_h():
        own_hidden.wait()
        wait_for(hg.at[0, pl.ds(1, KV_HEADS - 1)], hx_recv)
        if grid_y > 1:
            to_peer(upper, hg.at[0], hg.at[1], hy_send.at[0], hy_recv.at[0]).start()
            to_peer(lower, hg.at[0], hg.at[far], hy_send.at[1], hy_recv.at[1]).start()

    def relay_h():
        if grid_y > 1:
            wait_for(hg.at[1], hy_recv.at[0])
            wait_for(hg.at[far], hy_recv.at[1])
            for i, (dp, source) in enumerate(((upper, 1), (lower, far))):
                rows = pl.ds(i * half, half)
                to_peer(
                    dp, hg.at[source, :, rows], hg.at[2, :, rows], hr_send.at[i], hr_recv.at[i]
                ).start()

    def transpose_h():
        if grid_y > 1:
            for i in range(2):
                wait_for(hg.at[2, :, pl.ds(i * half, half)], hr_recv.at[i])

        def part(p, carry):
            rows = pl.ds(pl.multiple_of(p * span_rows, span_rows), span_rows)
            for c in range(CHUNK // 256):
                hidden = hg[:, :, rows, pl.ds(c * 256, 256)].reshape(n_dp * span_rows, 256)
                ht[p, pl.ds(c * 256, 256), :] = hidden.T
            return carry

        lax.fori_loop(0, pieces // SPAN, part, 0)

    late = jnp.logical_not(early) & (sec >= n_sec - 3)
    middle = jnp.logical_not(early | late)
    base = 3 * n_sec // 8
    relay_turn = 2 * (sec - base)
    late_turn = 2 * pieces // 3 - 3 * (n_sec - 1 - sec)

    @pl.when(early)
    def _():
        transpose_w()

    @pl.when(early | middle)
    def _():
        spread_h()

    @pl.when(early)
    def _():
        relay_h()
        transpose_h()

    def backward(step, carry):
        p = pieces - 1 - step
        start = pl.multiple_of(p * T, T)
        rows = pl.ds(start, T)
        window = pl.ds(start, WINDOW)
        own = pl.ds(pl.multiple_of(start + PAD, T), T)
        previous = pl.ds(start, PAD)
        own_keys, own_vals = [], []
        partial = [0.0] * KV_HEADS
        inner = jnp.zeros((T, 128), F32)
        for pair in range(KV_HEADS // 2):
            heads = (2 * pair, 2 * pair + 1)

            @pl.when(sec < n_sec - 1)
            def _():
                for i in heads:
                    pltpu.make_async_remote_copy(
                        src_ref=gb.at[i, rows],
                        dst_ref=gb.at[i, rows],
                        send_sem=g_send,
                        recv_sem=g_recv.at[p, i],
                        device_id={"section": sec},
                        device_id_type=MESH,
                    ).wait_recv()

            grads, d_vals = {}, {}
            for k in heads:
                grads[k] = to_rows(gb[k, rows, :])
                d_vals[k] = dot(pt[p, k].astype(BF16), grads[k])
                own_vals.append(dv_acc[k, own, :] + d_vals[k][PAD:])
            pair_vals = jnp.concatenate(own_vals[-2:], axis=1).astype(BF16)
            d_probs, d_probs_t = {}, {}
            for k in heads:
                vals = vb[window, pl.ds(k * HEAD_DIM, HEAD_DIM)]
                d_probs[k] = dot_t(grads[k], vals)
                d_probs_t[k] = dot_t(vals, grads[k])
            part = pl.ds(kv_width + pair * 2 * HEAD_DIM, 2 * HEAD_DIM)
            for c in range(KV_HEADS):
                partial[c] = partial[c] + dot(pair_vals, wt[c, part, :])
            for k in heads:
                hidden = hb[k, rows, :]
                query = to_rows(hidden)
                keys = kb[window, pl.ds(k * HEAD_DIM, HEAD_DIM)]
                probs = pb[p, k]
                product = probs * d_probs[k]
                total = jnp.sum(product, -1, keepdims=True)
                d_low = ((product - probs * total) * SCALE).astype(BF16)
                probs_t = pt[p, k]
                product_t = probs_t * d_probs_t[k]
                total_t = jnp.sum(product_t, 0, keepdims=True)
                d_low_t = ((product_t - probs_t * total_t) * SCALE).astype(BF16)
                d_keys = dot(d_low_t, query)
                own_keys.append(dk_acc[k, own, :] + d_keys[PAD:])
                d_query = to_lanes(dot(d_low, keys))
                dqb[k] = d_query
                inner = inner + fold_lanes(d_query * hidden.astype(F32))
                dk_acc[k, previous, :] += d_keys[:PAD]
                dv_acc[k, previous, :] += d_vals[k][:PAD]
        d_keys = jnp.concatenate(own_keys, axis=1).astype(BF16)
        d_vals = jnp.concatenate(own_vals, axis=1).astype(BF16)
        d_kv = jnp.concatenate([d_keys, d_vals], axis=1)
        for c in range(grid_y):
            do[p // SPAN, c, pl.ds(pl.multiple_of((p % SPAN) * T, T), T), :] = d_kv[
                :, c * cols : (c + 1) * cols
            ]
        inner = inner + fold_lanes(d_keys.astype(F32) * kb[own, :].astype(F32))
        inner = inner + fold_lanes(d_vals.astype(F32) * vb[own, :].astype(F32))
        mean = jnp.sum(inner, -1, keepdims=True) / width
        inverse = rb[rows, :][:, :1]

        def send_d_kv(part):
            q = p // SPAN
            dg[q, 0, part] = do[q, y, part]
            for j, dp, peer_x, peer_y in peers[1:]:
                to_peer(
                    dp, do.at[q, peer_y, part], dg.at[q, j, part], d_send, d_recv.at[q]
                ).start()

        def send_parts():
            near = sec < 2

            @pl.when((p % SPAN == 0) & jnp.logical_not(near & (p == 0)))
            def _():
                send_d_kv(pl.ds(0, span_rows))

            @pl.when(near & (p == 1))
            def _():
                send_d_kv(pl.ds(T, span_rows - T))

            @pl.when(near & (p == 0))
            def _():
                send_d_kv(pl.ds(0, T))

        def send_grads(chunks):
            @pl.when(sec > 0)
            def _():
                for k in chunks:
                    pltpu.make_async_remote_copy(
                        src_ref=go.at[k, rows],
                        dst_ref=gb.at[k, rows],
                        send_sem=g_send,
                        recv_sem=g_recv.at[p, k],
                        device_id={"section": sec - 1},
                        device_id_type=MESH,
                    ).start()

        for k in range(KV_HEADS):
            d_hidden = partial[k] + dqb[k] + dot(d_keys, wt[k, pl.ds(0, kv_width), :])
            normed = xb[k, rows, :].astype(F32) * inverse
            moment = d_hidden * normed
            gsum[k] += moment[0:8] + moment[8:16]
            d_inputs = inverse * (d_hidden * gf[k, 0:1, :] - normed * mean)
            go[k, rows, :] = (gb[k, rows, :].astype(F32) + d_inputs).astype(BF16)
            if k == 0:

                @pl.when(first)
                def _():
                    send_parts()

            if k < 2:
                send_grads([k])
            elif k == KV_HEADS - 1:
                send_grads([k - 1, k])

        @pl.when(sec > 0)
        def _():
            send_parts()

        @pl.when(late & (step == late_turn))
        def _():
            spread_h()

        @pl.when(
            middle
            & (
                (step == relay_turn)
                | ((step == 0) & (relay_turn < 0))
                | ((step == pieces - 1) & (relay_turn >= pieces))
            )
        )
        def _():
            relay_h()

        return carry

    lax.fori_loop(0, pieces, backward, 0)

    def gain_block(dp):
        column = dp * block
        return gs.at[
            column // CHUNK, :, pl.ds(pl.multiple_of(column % CHUNK, block), block)
        ]

    @pl.when(late)
    def _():
        relay_h()

    @pl.when(jnp.logical_not(early))
    def _():
        transpose_h()

    def multiply(step, carry):
        p = pieces // SPAN - 1 - step
        wait_for(dg.at[p, others], d_recv.at[p])
        d_kv = dg[p].reshape(n_dp * span_rows, cols)
        for c in range(CHUNK // 256):
            part = pl.ds(c * 256, 256)
            product = dot(ht[p, part, :], d_kv)
            wacc[part, :] = product + jnp.where(step > 0, wacc[part, :], 0.0)
        return carry

    lax.fori_loop(0, pieces // SPAN - 1, multiply, 0)
    wait_for(dg.at[0, others], d_recv.at[0])
    d_kv = dg[0].reshape(n_dp * span_rows, cols)
    for jy in list(range(1, grid_y)) + [0]:
        peer_y = (y + jy) % grid_y
        part = pl.ds(pl.multiple_of(peer_y * block, block), block)
        total = wacc[part, :] + dot(ht[0, part, :], d_kv)
        if jy == 0:
            out_w[:, pl.ds(pl.multiple_of(y * cols, cols), cols)] = total
        else:
            eo[jy] = total.astype(BF16)
            to_peer(
                x * grid_y + peer_y, eo.at[jy], eg.at[jy], e_send, e_recv.at[jy]
            ).start()

    for k in range(KV_HEADS):
        total = jnp.sum(gsum[k], 0, keepdims=True).astype(BF16).astype(F32)
        gs[k] = jnp.broadcast_to(total, (8, CHUNK))
    own_gain = pltpu.make_async_copy(gain_block(me), gg.at[0], in_sem.at[1])
    own_gain.start()
    for j, dp, peer_x, peer_y in peers[1:]:
        to_peer(dp, gain_block(dp), gg.at[j], s_send, s_recv).start()

    own_gain.wait()
    wait_for(gg.at[others], s_recv)
    gain_total = gg[0]
    for j in range(1, n_dp):
        gain_total = gain_total + gg[j]
    out_g[...] = gain_total[0:1]

    for jy in range(1, grid_y):
        wait_for(eg.at[jy], e_recv.at[jy])
        source_y = (y + grid_y - jy) % grid_y
        out_w[:, pl.ds(pl.multiple_of(source_y * cols, cols), cols)] = eg[jy].astype(F32)

    if grid_y > 1:
        wait_for(eo.at[pl.ds(1, grid_y - 1)], e_send)
        for i in range(2):
            wait_for(hg.at[0], hy_send.at[i])
            wait_for(hg.at[2, :, pl.ds(i * half, half)], hr_send.at[i])
    wait_for(hg.at[0, pl.ds(1, KV_HEADS - 1)], hx_send)
    wait_for(dg.at[:, others], d_send)
    wait_for(gg.at[others], s_send)

    @pl.when(sec < n_sec - 1)
    def _():
        wait_for(xo, f_send)

    @pl.when(sec > 0)
    def _():
        wait_for(go, g_send)


def local(n_sec, n_dp, tokens, upstream, gains, w_kv, doc_lengths, seg_lengths, block_mask):
    seq_len, width = tokens.shape[1:]
    pieces = seq_len // T
    kv2 = w_kv.shape[2]
    block = width // n_dp
    grid_y = n_dp // KV_HEADS
    cols = kv2 // grid_y
    any_spec = pl.BlockSpec(memory_space=pl.ANY)
    vmem = pl.BlockSpec(memory_space=pltpu.VMEM)
    smem = pl.BlockSpec(memory_space=pltpu.SMEM)
    features = (KV_HEADS, seq_len, CHUNK)
    dma = pltpu.SemaphoreType.DMA
    grad_weight, grad_gain = pl.pallas_call(
        functools.partial(kernel, n_sec, n_dp),
        out_shape=(
            jax.ShapeDtypeStruct((block, kv2), F32),
            jax.ShapeDtypeStruct((1, block), F32),
        ),
        in_specs=[any_spec, any_spec, vmem, any_spec, smem, smem, vmem],
        out_specs=(vmem, vmem),
        scratch_shapes=[
            pltpu.VMEM(features, BF16),
            pltpu.VMEM(features, BF16),
            pltpu.VMEM(features, BF16),
            pltpu.VMEM(features, BF16),
            pltpu.VMEM(features, BF16),
            pltpu.VMEM((KV_HEADS, CHUNK, kv2), BF16),
            pltpu.VMEM((KV_HEADS, kv2, CHUNK), BF16),
            pltpu.VMEM((PAD + seq_len, kv2 // 2), BF16),
            pltpu.VMEM((PAD + seq_len, kv2 // 2), BF16),
            pltpu.VMEM((KV_HEADS, PAD + seq_len, HEAD_DIM), F32),
            pltpu.VMEM((KV_HEADS, PAD + seq_len, HEAD_DIM), F32),
            pltpu.VMEM((pieces, KV_HEADS, GROUP * T, WINDOW), F32),
            pltpu.VMEM((pieces, KV_HEADS, WINDOW, GROUP * T), F32),
            pltpu.VMEM((KV_HEADS, T, CHUNK), F32),
            pltpu.VMEM((seq_len, 128), F32),
            pltpu.VMEM((pieces, T, WINDOW), F32),
            pltpu.VMEM((KV_HEADS, 8, CHUNK), F32),
            pltpu.VMEM((KV_HEADS, 8, CHUNK), F32),
            pltpu.VMEM((KV_HEADS, 8, CHUNK), F32),
            pltpu.VMEM((grid_y, KV_HEADS, seq_len, CHUNK), BF16),
            pltpu.VMEM((pieces // SPAN, CHUNK, n_dp * SPAN * T), BF16),
            pltpu.VMEM((pieces // SPAN, grid_y, SPAN * T, cols), BF16),
            pltpu.VMEM((pieces // SPAN, n_dp, SPAN * T, cols), BF16),
            pltpu.VMEM((CHUNK, cols), F32),
            pltpu.VMEM((grid_y, block, cols), BF16),
            pltpu.VMEM((grid_y, block, cols), BF16),
            pltpu.VMEM((n_dp, 8, block), F32),
            dma((KV_HEADS,)),
            dma((KV_HEADS,)),
            dma,
            dma((pieces, KV_HEADS)),
            dma,
            dma((pieces, KV_HEADS)),
            dma,
            dma,
            dma((2,)),
            dma((2,)),
            dma((2,)),
            dma((2,)),
            dma,
            dma((pieces // SPAN,)),
            dma,
            dma((grid_y,)),
            dma,
            dma,
        ],
        compiler_params=pltpu.CompilerParams(
            collective_id=0, has_side_effects=True, vmem_limit_bytes=60 * 1024 * 1024
        ),
        cost_estimate=pl.CostEstimate(
            flops=7 * 10**9, bytes_accessed=12 * 2**20, transcendentals=10**6
        ),
        name="relay",
    )(tokens, upstream, gains, w_kv, doc_lengths, seg_lengths, block_mask.transpose(1, 0, 2))
    return grad_weight[None], grad_gain


def solution(mesh):
    placed = (
        P("dp", None, None),
        P("dp", None, None),
        P("section", None),
        P("section", None, None),
        P("dp", None),
        P("dp", None),
        P("dp", None, None),
    )
    return jax.shard_map(
        functools.partial(local, mesh.shape["section"], mesh.shape["dp"]),
        mesh=mesh,
        in_specs=placed,
        out_specs=(P("section", "dp", None), P("section", "dp")),
        check_vma=False,
    )
```

```python
import functools
import math

import jax
import jax.numpy as jnp
from jax import lax
from jax.experimental import pallas as pl
from jax.experimental.pallas import tpu as pltpu
from jax.sharding import PartitionSpec as P

HEADS = 32
KV_HEADS = 4
GROUP = 8
HEAD_DIM = 128
SEGS = 4
BLK = 16
EPSILON = 1e-06

T = 16
SPAN = 4
WINDOW = 128
PAD = WINDOW - T
CHUNK = GROUP * HEAD_DIM
MESH = pl.DeviceIdType.MESH
F32 = jnp.float32
BF16 = jnp.bfloat16
EXP_SCALE = HEAD_DIM**-0.5 * math.log2(math.e)
SCALE = HEAD_DIM**-0.5


def to_rows(block):
    return jnp.concatenate(
        [block[:, HEAD_DIM * g : HEAD_DIM * (g + 1)] for g in range(GROUP)], axis=0
    )


def to_lanes(block):
    return jnp.concatenate([block[T * g : T * (g + 1)] for g in range(GROUP)], axis=1)


def fold_lanes(block):
    total = block[:, :128]
    for g in range(1, block.shape[1] // 128):
        total = total + block[:, 128 * g : 128 * (g + 1)]
    return total


def dot_t(a, b):
    return lax.dot_general(a, b, (((1,), (1,)), ((), ())), preferred_element_type=F32)


def t_dot(a, b):
    return lax.dot_general(a, b, (((0,), (0,)), ((), ())), preferred_element_type=F32)


def dot(a, b):
    return jnp.dot(a, b, preferred_element_type=F32)


def kernel(
    n_sec,
    n_dp,
    tok,
    ups,
    gain,
    w,
    docs,
    segs,
    table,
    out_w,
    out_g,
    xb,
    hb,
    gb,
    xo,
    go,
    wb,
    wt,
    kb,
    vb,
    dk_acc,
    dv_acc,
    pb,
    pt,
    dqb,
    rb,
    bias,
    gf,
    gsum,
    gs,
    hg,
    ht,
    do,
    dg,
    wacc,
    eo,
    eg,
    gg,
    w_sem,
    in_sem,
    f_send,
    f_recv,
    g_send,
    g_recv,
    hx_send,
    hx_recv,
    hy_send,
    hy_recv,
    hr_send,
    hr_recv,
    d_send,
    d_recv,
    e_send,
    e_recv,
    s_send,
    s_recv,
):
    sec = lax.axis_index("section")
    me = lax.axis_index("dp")
    seq_len = xb.shape[1]
    pieces = seq_len // T
    width = KV_HEADS * CHUNK
    kv_width = KV_HEADS * HEAD_DIM
    block = width // n_dp
    grid_y = n_dp // KV_HEADS
    cols = 2 * kv_width // grid_y
    x, y = me // grid_y, me % grid_y
    span_rows = SPAN * T
    first = sec == 0
    last = sec == n_sec - 1
    early = sec < (n_sec + 3) // 4

    w_copies = [
        pltpu.make_async_copy(w.at[0, pl.ds(k * CHUNK, CHUNK)], wb.at[k], w_sem.at[k])
        for k in range(KV_HEADS)
    ]
    tok_copies = [
        pltpu.make_async_copy(tok.at[0, :, pl.ds(k * CHUNK, CHUNK)], xb.at[k], in_sem.at[k])
        for k in range(KV_HEADS)
    ]
    ups_copies = [
        pltpu.make_async_copy(ups.at[0, :, pl.ds(k * CHUNK, CHUNK)], xo.at[k], in_sem.at[k])
        for k in range(KV_HEADS)
    ]

    @pl.when(first)
    def _():
        for copy in tok_copies:
            copy.start()

    for copy in w_copies:
        copy.start()

    @pl.when(last)
    def _():
        for copy in ups_copies:
            copy.start()

    barrier = pltpu.get_barrier_semaphore()

    @pl.when(sec > 0)
    def _():
        pl.semaphore_signal(barrier, inc=1, device_id={"section": sec - 1}, device_id_type=MESH)

    @pl.when(sec < n_sec - 1)
    def _():
        pl.semaphore_signal(barrier, inc=1, device_id={"section": sec + 1}, device_id_type=MESH)

    for j in range(1, n_dp):
        pl.semaphore_signal(
            barrier, inc=1, device_id={"dp": (me + j) % n_dp}, device_id_type=MESH
        )

    kb[pl.ds(0, PAD), :] = jnp.zeros((PAD, kv_width), BF16)
    vb[pl.ds(0, PAD), :] = jnp.zeros((PAD, kv_width), BF16)
    dk_acc[...] = jnp.zeros_like(dk_acc)
    dv_acc[...] = jnp.zeros_like(dv_acc)
    gsum[...] = jnp.zeros_like(gsum)
    for k in range(KV_HEADS):
        gf[k] = jnp.broadcast_to(
            gain[:, pl.ds(k * CHUNK, CHUNK)].astype(F32), (8, CHUNK)
        )

    doc_ends = [docs[0, 0]]
    for d in range(1, docs.shape[1] - 1):
        doc_ends.append(doc_ends[-1] + docs[0, d])

    def doc_of(positions):
        total = jnp.zeros_like(positions)
        for end in doc_ends:
            total = total + jnp.where(positions >= end, 1, 0)
        return total

    row = lax.broadcasted_iota(jnp.int32, (T, WINDOW), 0)
    column = lax.broadcasted_iota(jnp.int32, (T, WINDOW), 1)

    blocks = seq_len // BLK
    opened = table[:, 0, :].astype(BF16)
    block_row = lax.broadcasted_iota(jnp.int32, (blocks, WINDOW), 0)
    block_column = lax.broadcasted_iota(jnp.int32, (blocks, WINDOW), 1) // BLK
    for p in range(pieces):
        queries = row + p * T
        keys = column + (p * T - PAD)
        spread = (block_row == block_column + (p * T - PAD) // BLK).astype(BF16)
        line = dot(opened, spread)[p : p + 1]
        allowed = (
            (keys >= 0)
            & (keys <= queries)
            & (doc_of(keys) == doc_of(queries))
            & ((column // BLK == PAD // BLK) | (line > 0.5))
        )
        bias[p] = jnp.where(allowed, 0.0, -1e30)

    @pl.when(last)
    def _():
        for copy in ups_copies:
            copy.wait()
        sizes = [segs[0, i] for i in range(SEGS)]

        def scale_piece(p, carry):
            rows = pl.ds(pl.multiple_of(p * T, T), T)
            positions = row + p * T
            count = jnp.zeros((T, WINDOW), jnp.int32) + sizes[0]
            end = sizes[0]
            for i in range(1, SEGS):
                count = jnp.where(positions >= end, sizes[i], count)
                end = end + sizes[i]
            factor = seq_len / (SEGS * count.astype(F32))
            factor = jnp.concatenate([factor] * (CHUNK // WINDOW), axis=1)
            for k in range(KV_HEADS):
                gb[k, rows, :] = (xo[k, rows, :].astype(F32) * factor).astype(BF16)
            return carry

        lax.fori_loop(0, pieces, scale_piece, 0)

    @pl.when(first)
    def _():
        for copy in tok_copies:
            copy.wait()

    def transpose_w():
        def part(i, carry):
            k, c = i // 4, i % 4
            source = pl.ds(pl.multiple_of(c * 256, 256), 256)
            for n in range(2 * kv_width // 256):
                wt[k, pl.ds(n * 256, 256), source] = wb[k, source, pl.ds(n * 256, 256)].T
            return carry

        lax.fori_loop(0, KV_HEADS * (CHUNK // 256), part, 0)

    @pl.when(jnp.logical_not(early))
    def _():
        for copy in w_copies:
            copy.wait()
        transpose_w()

    before, after = (sec + n_sec - 1) // n_sec, (2 * n_sec - 2 - sec) // n_sec

    def forward(p, carry):
        start = pl.multiple_of(p * T, T)
        rows = pl.ds(start, T)
        keys_part, vals_part = pl.ds(0, kv_width), pl.ds(kv_width, kv_width)
        new_keys = jnp.zeros((T, kv_width), F32)
        new_vals = jnp.zeros((T, kv_width), F32)
        scaled = []
        squares = jnp.zeros((T, 128), F32)
        for k in range(KV_HEADS):
            if k % 2 == 0:
                arrival = pltpu.make_async_remote_copy(
                    src_ref=xb.at[pl.ds(k, 2), rows],
                    dst_ref=xb.at[pl.ds(k, 2), rows],
                    send_sem=f_send,
                    recv_sem=f_recv.at[p, k // 2],
                    device_id={"section": sec},
                    device_id_type=MESH,
                )

                @pl.when(sec > 0)
                def _():
                    arrival.wait_recv()

                @pl.when(early & (p == 0))
                def _():
                    w_copies[k].wait()
                    w_copies[k + 1].wait()

            values = xb[k, rows, :].astype(F32)
            squares = squares + fold_lanes(values * values)
            scaled.append((values * gf[k, 0:1, :]).astype(BF16))
            new_keys = new_keys + dot(scaled[k], wb[k, :, keys_part])
            if k > 0:
                new_vals = new_vals + dot(scaled[k - 1], wb[k - 1, :, vals_part])
        inverse = lax.rsqrt(jnp.sum(squares, -1, keepdims=True) / width + EPSILON)
        rb[rows, :] = jnp.broadcast_to(inverse, (T, 128))
        own = pl.ds(pl.multiple_of(start + PAD, T), T)
        window = pl.ds(start, WINDOW)
        kb[own, :] = (new_keys * inverse).astype(BF16)
        bias_rows = jnp.concatenate([bias[p]] * GROUP, axis=0)
        raws = []
        for k in range(KV_HEADS):
            values = xb[k, rows, :].astype(F32)
            hidden = (values * inverse * gf[k, 0:1, :]).astype(BF16)
            hb[k, rows, :] = hidden
            keys = kb[window, pl.ds(k * HEAD_DIM, HEAD_DIM)]
            scores = dot_t(to_rows(hidden), keys)
            raws.append(jnp.exp2(scores * EXP_SCALE + bias_rows))
        last_k = KV_HEADS - 1
        new_vals = new_vals + dot(scaled[last_k], wb[last_k, :, vals_part])
        vb[own, :] = (new_vals * inverse).astype(BF16)
        for k in range(KV_HEADS):
            raw = raws[k]
            vals = vb[window, pl.ds(k * HEAD_DIM, HEAD_DIM)]
            share = 1.0 / jnp.sum(raw, -1, keepdims=True)
            mixed = dot(raw.astype(BF16), vals) * share
            xo[k, rows, :] = (xb[k, rows, :].astype(F32) + to_lanes(mixed)).astype(BF16)
            probs = raw * share
            pb[p, k] = probs
            pt[p, k] = probs.T

        @pl.when(p == 0)
        def _():
            pl.semaphore_wait(barrier, n_dp - 1 + before + after)

        @pl.when(sec < n_sec - 1)
        def _():
            for i in range(KV_HEADS // 2):
                pltpu.make_async_remote_copy(
                    src_ref=xo.at[pl.ds(2 * i, 2), rows],
                    dst_ref=xb.at[pl.ds(2 * i, 2), rows],
                    send_sem=f_send,
                    recv_sem=f_recv.at[p, i],
                    device_id={"section": sec + 1},
                    device_id_type=MESH,
                ).start()

        return carry

    lax.fori_loop(0, pieces, forward, 0)

    def to_peer(dp, src, dst, send_sem, recv_sem):
        return pltpu.make_async_remote_copy(
            src_ref=src,
            dst_ref=dst,
            send_sem=send_sem,
            recv_sem=recv_sem,
            device_id={"dp": dp},
            device_id_type=MESH,
        )

    def wait_for(ref, sem):
        pltpu.make_async_copy(ref, ref, sem).wait()

    peers = []
    for jy in range(grid_y):
        for jx in range(KV_HEADS):
            peer_x, peer_y = (x + jx) % KV_HEADS, (y + jy) % grid_y
            peers.append((jy * KV_HEADS + jx, peer_x * grid_y + peer_y, peer_x, peer_y))
    others = pl.ds(1, n_dp - 1)

    upper, lower = x * grid_y + (y + 1) % grid_y, x * grid_y + (y + grid_y - 1) % grid_y
    half = seq_len // 2
    far = grid_y - 1

    own_hidden = pltpu.make_async_copy(hb.at[x], hg.at[0, 0], in_sem.at[0])
    own_hidden.start()
    for jx in range(1, KV_HEADS):
        peer_x = (x + jx) % KV_HEADS
        to_peer(peer_x * grid_y + y, hb.at[peer_x], hg.at[0, jx], hx_send, hx_recv).start()

    def spread_h():
        own_hidden.wait()
        wait_for(hg.at[0, pl.ds(1, KV_HEADS - 1)], hx_recv)
        if grid_y > 1:
            to_peer(upper, hg.at[0], hg.at[1], hy_send.at[0], hy_recv.at[0]).start()
            to_peer(lower, hg.at[0], hg.at[far], hy_send.at[1], hy_recv.at[1]).start()

    def relay_h():
        if grid_y > 1:
            wait_for(hg.at[1], hy_recv.at[0])
            wait_for(hg.at[far], hy_recv.at[1])
            for i, (dp, source) in enumerate(((upper, 1), (lower, far))):
                rows = pl.ds(i * half, half)
                to_peer(
                    dp, hg.at[source, :, rows], hg.at[2, :, rows], hr_send.at[i], hr_recv.at[i]
                ).start()

    def transpose_h():
        if grid_y > 1:
            for i in range(2):
                wait_for(hg.at[2, :, pl.ds(i * half, half)], hr_recv.at[i])

        def part(p, carry):
            rows = pl.ds(pl.multiple_of(p * span_rows, span_rows), span_rows)
            for c in range(CHUNK // 256):
                hidden = hg[:, :, rows, pl.ds(c * 256, 256)].reshape(n_dp * span_rows, 256)
                ht[p, pl.ds(c * 256, 256), :] = hidden.T
            return carry

        lax.fori_loop(0, pieces // SPAN, part, 0)

    late = jnp.logical_not(early) & (sec >= n_sec - 3)
    middle = jnp.logical_not(early | late)
    base = 3 * n_sec // 8
    relay_turn = 2 * (sec - base)
    late_turn = 2 * pieces // 3 - 3 * (n_sec - 1 - sec)

    @pl.when(early)
    def _():
        transpose_w()

    @pl.when(early | middle)
    def _():
        spread_h()

    @pl.when(early)
    def _():
        relay_h()
        transpose_h()

    def backward(step, carry):
        p = pieces - 1 - step
        start = pl.multiple_of(p * T, T)
        rows = pl.ds(start, T)
        window = pl.ds(start, WINDOW)
        own = pl.ds(pl.multiple_of(start + PAD, T), T)
        previous = pl.ds(start, PAD)
        own_keys, own_vals = [], []
        partial = [0.0] * KV_HEADS
        inner = jnp.zeros((T, 128), F32)
        for pair in range(KV_HEADS // 2):
            heads = (2 * pair, 2 * pair + 1)

            @pl.when(sec < n_sec - 1)
            def _():
                pltpu.make_async_remote_copy(
                    src_ref=gb.at[pl.ds(2 * pair, 2), rows],
                    dst_ref=gb.at[pl.ds(2 * pair, 2), rows],
                    send_sem=g_send,
                    recv_sem=g_recv.at[p, pair],
                    device_id={"section": sec},
                    device_id_type=MESH,
                ).wait_recv()

            grads, d_vals = {}, {}
            for k in heads:
                grads[k] = to_rows(gb[k, rows, :])
                d_vals[k] = dot(pt[p, k].astype(BF16), grads[k])
                own_vals.append(dv_acc[k, own, :] + d_vals[k][PAD:])
            pair_vals = jnp.concatenate(own_vals[-2:], axis=1).astype(BF16)
            d_probs, d_probs_t = {}, {}
            for k in heads:
                vals = vb[window, pl.ds(k * HEAD_DIM, HEAD_DIM)]
                d_probs[k] = dot_t(grads[k], vals)
                d_probs_t[k] = dot_t(vals, grads[k])
            part = pl.ds(kv_width + pair * 2 * HEAD_DIM, 2 * HEAD_DIM)
            for c in range(KV_HEADS):
                partial[c] = partial[c] + dot(pair_vals, wt[c, part, :])
            for k in heads:
                hidden = hb[k, rows, :]
                query = to_rows(hidden)
                keys = kb[window, pl.ds(k * HEAD_DIM, HEAD_DIM)]
                probs = pb[p, k]
                product = probs * d_probs[k]
                total = jnp.sum(product, -1, keepdims=True)
                d_low = ((product - probs * total) * SCALE).astype(BF16)
                probs_t = pt[p, k]
                product_t = probs_t * d_probs_t[k]
                total_t = jnp.sum(product_t, 0, keepdims=True)
                d_low_t = ((product_t - probs_t * total_t) * SCALE).astype(BF16)
                d_keys = dot(d_low_t, query)
                own_keys.append(dk_acc[k, own, :] + d_keys[PAD:])
                d_query = to_lanes(dot(d_low, keys))
                dqb[k] = d_query
                inner = inner + fold_lanes(d_query * hidden.astype(F32))
                dk_acc[k, previous, :] += d_keys[:PAD]
                dv_acc[k, previous, :] += d_vals[k][:PAD]
        d_keys = jnp.concatenate(own_keys, axis=1).astype(BF16)
        d_vals = jnp.concatenate(own_vals, axis=1).astype(BF16)
        d_kv = jnp.concatenate([d_keys, d_vals], axis=1)
        for c in range(grid_y):
            do[p // SPAN, c, pl.ds(pl.multiple_of((p % SPAN) * T, T), T), :] = d_kv[
                :, c * cols : (c + 1) * cols
            ]
        inner = inner + fold_lanes(d_keys.astype(F32) * kb[own, :].astype(F32))
        inner = inner + fold_lanes(d_vals.astype(F32) * vb[own, :].astype(F32))
        mean = jnp.sum(inner, -1, keepdims=True) / width
        inverse = rb[rows, :][:, :1]

        def send_d_kv(part):
            q = p // SPAN
            dg[q, 0, part] = do[q, y, part]
            for j, dp, peer_x, peer_y in peers[1:]:
                to_peer(
                    dp, do.at[q, peer_y, part], dg.at[q, j, part], d_send, d_recv.at[q]
                ).start()

        def send_parts():
            near = sec < 2

            @pl.when((p % SPAN == 0) & jnp.logical_not(near & (p == 0)))
            def _():
                send_d_kv(pl.ds(0, span_rows))

            @pl.when(near & (p == 1))
            def _():
                send_d_kv(pl.ds(T, span_rows - T))

            @pl.when(near & (p == 0))
            def _():
                send_d_kv(pl.ds(0, T))

        def send_grads(pair):
            @pl.when(sec > 0)
            def _():
                pltpu.make_async_remote_copy(
                    src_ref=go.at[pl.ds(2 * pair, 2), rows],
                    dst_ref=gb.at[pl.ds(2 * pair, 2), rows],
                    send_sem=g_send,
                    recv_sem=g_recv.at[p, pair],
                    device_id={"section": sec - 1},
                    device_id_type=MESH,
                ).start()

        for k in range(KV_HEADS):
            d_hidden = partial[k] + dqb[k] + dot(d_keys, wt[k, pl.ds(0, kv_width), :])
            normed = xb[k, rows, :].astype(F32) * inverse
            moment = d_hidden * normed
            gsum[k] += moment[0:8] + moment[8:16]
            d_inputs = inverse * (d_hidden * gf[k, 0:1, :] - normed * mean)
            go[k, rows, :] = (gb[k, rows, :].astype(F32) + d_inputs).astype(BF16)
            if k == 1:

                @pl.when(first)
                def _():
                    send_parts()

            if k % 2 == 1:
                send_grads(k // 2)

        @pl.when(sec > 0)
        def _():
            send_parts()

        @pl.when(late & (step == late_turn))
        def _():
            spread_h()

        @pl.when(
            middle
            & (
                (step == relay_turn)
                | ((step == 0) & (relay_turn < 0))
                | ((step == pieces - 1) & (relay_turn >= pieces))
            )
        )
        def _():
            relay_h()

        return carry

    lax.fori_loop(0, pieces, backward, 0)

    def gain_block(dp):
        column = dp * block
        return gs.at[
            column // CHUNK, :, pl.ds(pl.multiple_of(column % CHUNK, block), block)
        ]

    @pl.when(late)
    def _():
        relay_h()

    @pl.when(jnp.logical_not(early))
    def _():
        transpose_h()

    def multiply(step, carry):
        p = pieces // SPAN - 1 - step
        wait_for(dg.at[p, others], d_recv.at[p])
        d_kv = dg[p].reshape(n_dp * span_rows, cols)
        for c in range(CHUNK // 256):
            part = pl.ds(c * 256, 256)
            product = dot(ht[p, part, :], d_kv)
            wacc[part, :] = product + jnp.where(step > 0, wacc[part, :], 0.0)
        return carry

    lax.fori_loop(0, pieces // SPAN - 1, multiply, 0)
    wait_for(dg.at[0, others], d_recv.at[0])
    d_kv = dg[0].reshape(n_dp * span_rows, cols)
    for jy in list(range(1, grid_y)) + [0]:
        peer_y = (y + jy) % grid_y
        part = pl.ds(pl.multiple_of(peer_y * block, block), block)
        total = wacc[part, :] + dot(ht[0, part, :], d_kv)
        if jy == 0:
            out_w[:, pl.ds(pl.multiple_of(y * cols, cols), cols)] = total.astype(BF16)
        else:
            eo[jy] = total.astype(BF16)
            to_peer(
                x * grid_y + peer_y, eo.at[jy], eg.at[jy], e_send, e_recv.at[jy]
            ).start()

    for k in range(KV_HEADS):
        total = jnp.sum(gsum[k], 0, keepdims=True).astype(BF16).astype(F32)
        gs[k] = jnp.broadcast_to(total, (8, CHUNK))
    own_gain = pltpu.make_async_copy(gain_block(me), gg.at[0], in_sem.at[1])
    own_gain.start()
    for j, dp, peer_x, peer_y in peers[1:]:
        to_peer(dp, gain_block(dp), gg.at[j], s_send, s_recv).start()

    own_gain.wait()
    wait_for(gg.at[others], s_recv)
    gain_total = gg[0]
    for j in range(1, n_dp):
        gain_total = gain_total + gg[j]
    out_g[...] = gain_total[0:1]

    for jy in range(1, grid_y):
        wait_for(eg.at[jy], e_recv.at[jy])
        source_y = (y + grid_y - jy) % grid_y
        out_w[:, pl.ds(pl.multiple_of(source_y * cols, cols), cols)] = eg[jy]

    if grid_y > 1:
        wait_for(eo.at[pl.ds(1, grid_y - 1)], e_send)
        for i in range(2):
            wait_for(hg.at[0], hy_send.at[i])
            wait_for(hg.at[2, :, pl.ds(i * half, half)], hr_send.at[i])
    wait_for(hg.at[0, pl.ds(1, KV_HEADS - 1)], hx_send)
    wait_for(dg.at[:, others], d_send)
    wait_for(gg.at[others], s_send)

    @pl.when(sec < n_sec - 1)
    def _():
        wait_for(xo, f_send)

    @pl.when(sec > 0)
    def _():
        wait_for(go, g_send)


def local(n_sec, n_dp, tokens, upstream, gains, w_kv, doc_lengths, seg_lengths, block_mask):
    seq_len, width = tokens.shape[1:]
    pieces = seq_len // T
    kv2 = w_kv.shape[2]
    block = width // n_dp
    grid_y = n_dp // KV_HEADS
    cols = kv2 // grid_y
    any_spec = pl.BlockSpec(memory_space=pl.ANY)
    vmem = pl.BlockSpec(memory_space=pltpu.VMEM)
    smem = pl.BlockSpec(memory_space=pltpu.SMEM)
    features = (KV_HEADS, seq_len, CHUNK)
    dma = pltpu.SemaphoreType.DMA
    grad_weight, grad_gain = pl.pallas_call(
        functools.partial(kernel, n_sec, n_dp),
        out_shape=(
            jax.ShapeDtypeStruct((block, kv2), BF16),
            jax.ShapeDtypeStruct((1, block), F32),
        ),
        in_specs=[any_spec, any_spec, vmem, any_spec, smem, smem, vmem],
        out_specs=(vmem, vmem),
        scratch_shapes=[
            pltpu.VMEM(features, BF16),
            pltpu.VMEM(features, BF16),
            pltpu.VMEM(features, BF16),
            pltpu.VMEM(features, BF16),
            pltpu.VMEM(features, BF16),
            pltpu.VMEM((KV_HEADS, CHUNK, kv2), BF16),
            pltpu.VMEM((KV_HEADS, kv2, CHUNK), BF16),
            pltpu.VMEM((PAD + seq_len, kv2 // 2), BF16),
            pltpu.VMEM((PAD + seq_len, kv2 // 2), BF16),
            pltpu.VMEM((KV_HEADS, PAD + seq_len, HEAD_DIM), F32),
            pltpu.VMEM((KV_HEADS, PAD + seq_len, HEAD_DIM), F32),
            pltpu.VMEM((pieces, KV_HEADS, GROUP * T, WINDOW), F32),
            pltpu.VMEM((pieces, KV_HEADS, WINDOW, GROUP * T), F32),
            pltpu.VMEM((KV_HEADS, T, CHUNK), F32),
            pltpu.VMEM((seq_len, 128), F32),
            pltpu.VMEM((pieces, T, WINDOW), F32),
            pltpu.VMEM((KV_HEADS, 8, CHUNK), F32),
            pltpu.VMEM((KV_HEADS, 8, CHUNK), F32),
            pltpu.VMEM((KV_HEADS, 8, CHUNK), F32),
            pltpu.VMEM((grid_y, KV_HEADS, seq_len, CHUNK), BF16),
            pltpu.VMEM((pieces // SPAN, CHUNK, n_dp * SPAN * T), BF16),
            pltpu.VMEM((pieces // SPAN, grid_y, SPAN * T, cols), BF16),
            pltpu.VMEM((pieces // SPAN, n_dp, SPAN * T, cols), BF16),
            pltpu.VMEM((CHUNK, cols), F32),
            pltpu.VMEM((grid_y, block, cols), BF16),
            pltpu.VMEM((grid_y, block, cols), BF16),
            pltpu.VMEM((n_dp, 8, block), F32),
            dma((KV_HEADS,)),
            dma((KV_HEADS,)),
            dma,
            dma((pieces, KV_HEADS // 2)),
            dma,
            dma((pieces, KV_HEADS // 2)),
            dma,
            dma,
            dma((2,)),
            dma((2,)),
            dma((2,)),
            dma((2,)),
            dma,
            dma((pieces // SPAN,)),
            dma,
            dma((grid_y,)),
            dma,
            dma,
        ],
        compiler_params=pltpu.CompilerParams(
            collective_id=0, has_side_effects=True, vmem_limit_bytes=60 * 1024 * 1024
        ),
        cost_estimate=pl.CostEstimate(
            flops=7 * 10**9, bytes_accessed=12 * 2**20, transcendentals=10**6
        ),
        name="relay",
    )(tokens, upstream, gains, w_kv, doc_lengths, seg_lengths, block_mask.transpose(1, 0, 2))
    return grad_weight.astype(F32)[None], grad_gain


def solution(mesh):
    placed = (
        P("dp", None, None),
        P("dp", None, None),
        P("section", None),
        P("section", None, None),
        P("dp", None),
        P("dp", None),
        P("dp", None, None),
    )
    return jax.shard_map(
        functools.partial(local, mesh.shape["section"], mesh.shape["dp"]),
        mesh=mesh,
        in_specs=placed,
        out_specs=(P("section", "dp", None), P("section", "dp")),
        check_vma=False,
    )
```

```python
import functools
import math

import jax
import jax.numpy as jnp
from jax import lax
from jax.experimental import pallas as pl
from jax.experimental.pallas import tpu as pltpu
from jax.sharding import PartitionSpec as P

HEADS = 32
KV_HEADS = 4
GROUP = 8
HEAD_DIM = 128
SEGS = 4
BLK = 16
EPSILON = 1e-06

T = 16
GROUPS = ((6, 12), (1, 6), (0, 1))
WINDOW = 128
PAD = WINDOW - T
CHUNK = GROUP * HEAD_DIM
MESH = pl.DeviceIdType.MESH
F32 = jnp.float32
BF16 = jnp.bfloat16
EXP_SCALE = HEAD_DIM**-0.5 * math.log2(math.e)
SCALE = HEAD_DIM**-0.5


def to_rows(block):
    return jnp.concatenate(
        [block[:, HEAD_DIM * g : HEAD_DIM * (g + 1)] for g in range(GROUP)], axis=0
    )


def to_lanes(block):
    return jnp.concatenate([block[T * g : T * (g + 1)] for g in range(GROUP)], axis=1)


def fold_lanes(block):
    total = block[:, :128]
    for g in range(1, block.shape[1] // 128):
        total = total + block[:, 128 * g : 128 * (g + 1)]
    return total


def dot_t(a, b):
    return lax.dot_general(a, b, (((1,), (1,)), ((), ())), preferred_element_type=F32)


def t_dot(a, b):
    return lax.dot_general(a, b, (((0,), (0,)), ((), ())), preferred_element_type=F32)


def dot(a, b):
    return jnp.dot(a, b, preferred_element_type=F32)


def kernel(
    n_sec,
    n_dp,
    tok,
    ups,
    gain,
    w,
    docs,
    segs,
    table,
    out_w,
    out_g,
    xb,
    hb,
    gb,
    xo,
    go,
    wb,
    wt,
    kb,
    vb,
    dk_acc,
    dv_acc,
    pb,
    pt,
    dqb,
    rb,
    bias,
    gf,
    gsum,
    gs,
    hg,
    ht,
    do,
    dg,
    wacc,
    eo,
    eg,
    gg,
    w_sem,
    in_sem,
    f_send,
    f_recv,
    g_send,
    g_recv,
    hx_send,
    hx_recv,
    hy_send,
    hy_recv,
    hr_send,
    hr_recv,
    d_send,
    d_recv,
    e_send,
    e_recv,
    s_send,
    s_recv,
):
    sec = lax.axis_index("section")
    me = lax.axis_index("dp")
    seq_len = xb.shape[1]
    pieces = seq_len // T
    width = KV_HEADS * CHUNK
    kv_width = KV_HEADS * HEAD_DIM
    block = width // n_dp
    grid_y = n_dp // KV_HEADS
    cols = 2 * kv_width // grid_y
    x, y = me // grid_y, me % grid_y
    first = sec == 0
    last = sec == n_sec - 1
    early = sec < (n_sec + 3) // 4

    w_copies = [
        pltpu.make_async_copy(w.at[0, pl.ds(k * CHUNK, CHUNK)], wb.at[k], w_sem.at[k])
        for k in range(KV_HEADS)
    ]
    tok_copies = [
        pltpu.make_async_copy(tok.at[0, :, pl.ds(k * CHUNK, CHUNK)], xb.at[k], in_sem.at[k])
        for k in range(KV_HEADS)
    ]
    ups_copies = [
        pltpu.make_async_copy(ups.at[0, :, pl.ds(k * CHUNK, CHUNK)], xo.at[k], in_sem.at[k])
        for k in range(KV_HEADS)
    ]

    @pl.when(first)
    def _():
        for copy in tok_copies:
            copy.start()

    for copy in w_copies:
        copy.start()

    @pl.when(last)
    def _():
        for copy in ups_copies:
            copy.start()

    barrier = pltpu.get_barrier_semaphore()

    @pl.when(sec > 0)
    def _():
        pl.semaphore_signal(barrier, inc=1, device_id={"section": sec - 1}, device_id_type=MESH)

    @pl.when(sec < n_sec - 1)
    def _():
        pl.semaphore_signal(barrier, inc=1, device_id={"section": sec + 1}, device_id_type=MESH)

    for j in range(1, n_dp):
        pl.semaphore_signal(
            barrier, inc=1, device_id={"dp": (me + j) % n_dp}, device_id_type=MESH
        )

    kb[pl.ds(0, PAD), :] = jnp.zeros((PAD, kv_width), BF16)
    vb[pl.ds(0, PAD), :] = jnp.zeros((PAD, kv_width), BF16)
    dk_acc[...] = jnp.zeros_like(dk_acc)
    dv_acc[...] = jnp.zeros_like(dv_acc)
    gsum[...] = jnp.zeros_like(gsum)
    for k in range(KV_HEADS):
        gf[k] = jnp.broadcast_to(
            gain[:, pl.ds(k * CHUNK, CHUNK)].astype(F32), (8, CHUNK)
        )

    doc_ends = [docs[0, 0]]
    for d in range(1, docs.shape[1] - 1):
        doc_ends.append(doc_ends[-1] + docs[0, d])

    def doc_of(positions):
        total = jnp.zeros_like(positions)
        for end in doc_ends:
            total = total + jnp.where(positions >= end, 1, 0)
        return total

    row = lax.broadcasted_iota(jnp.int32, (T, WINDOW), 0)
    column = lax.broadcasted_iota(jnp.int32, (T, WINDOW), 1)

    blocks = seq_len // BLK
    opened = table[:, 0, :].astype(BF16)
    block_row = lax.broadcasted_iota(jnp.int32, (blocks, WINDOW), 0)
    block_column = lax.broadcasted_iota(jnp.int32, (blocks, WINDOW), 1) // BLK
    for p in range(pieces):
        queries = row + p * T
        keys = column + (p * T - PAD)
        spread = (block_row == block_column + (p * T - PAD) // BLK).astype(BF16)
        line = dot(opened, spread)[p : p + 1]
        allowed = (
            (keys >= 0)
            & (keys <= queries)
            & (doc_of(keys) == doc_of(queries))
            & ((column // BLK == PAD // BLK) | (line > 0.5))
        )
        bias[p] = jnp.where(allowed, 0.0, -1e30)

    @pl.when(last)
    def _():
        for copy in ups_copies:
            copy.wait()
        sizes = [segs[0, i] for i in range(SEGS)]

        def scale_piece(p, carry):
            rows = pl.ds(pl.multiple_of(p * T, T), T)
            positions = row + p * T
            count = jnp.zeros((T, WINDOW), jnp.int32) + sizes[0]
            end = sizes[0]
            for i in range(1, SEGS):
                count = jnp.where(positions >= end, sizes[i], count)
                end = end + sizes[i]
            factor = seq_len / (SEGS * count.astype(F32))
            factor = jnp.concatenate([factor] * (CHUNK // WINDOW), axis=1)
            for k in range(KV_HEADS):
                gb[k, rows, :] = (xo[k, rows, :].astype(F32) * factor).astype(BF16)
            return carry

        lax.fori_loop(0, pieces, scale_piece, 0)

    @pl.when(first)
    def _():
        for copy in tok_copies:
            copy.wait()

    def transpose_w():
        def part(i, carry):
            k, c = i // 4, i % 4
            source = pl.ds(pl.multiple_of(c * 256, 256), 256)
            for n in range(2 * kv_width // 256):
                wt[k, pl.ds(n * 256, 256), source] = wb[k, source, pl.ds(n * 256, 256)].T
            return carry

        lax.fori_loop(0, KV_HEADS * (CHUNK // 256), part, 0)

    @pl.when(jnp.logical_not(early))
    def _():
        for copy in w_copies:
            copy.wait()
        transpose_w()

    before, after = (sec + n_sec - 1) // n_sec, (2 * n_sec - 2 - sec) // n_sec

    def forward(p, carry):
        start = pl.multiple_of(p * T, T)
        rows = pl.ds(start, T)
        keys_part, vals_part = pl.ds(0, kv_width), pl.ds(kv_width, kv_width)
        new_keys = jnp.zeros((T, kv_width), F32)
        new_vals = jnp.zeros((T, kv_width), F32)
        scaled = []
        squares = jnp.zeros((T, 128), F32)
        for k in range(KV_HEADS):
            arrival = pltpu.make_async_remote_copy(
                src_ref=xb.at[k, rows],
                dst_ref=xb.at[k, rows],
                send_sem=f_send,
                recv_sem=f_recv.at[p, k],
                device_id={"section": sec},
                device_id_type=MESH,
            )

            @pl.when(sec > 0)
            def _():
                arrival.wait_recv()

            @pl.when(early & (p == 0))
            def _():
                w_copies[k].wait()

            values = xb[k, rows, :].astype(F32)
            squares = squares + fold_lanes(values * values)
            scaled.append((values * gf[k, 0:1, :]).astype(BF16))
            new_keys = new_keys + dot(scaled[k], wb[k, :, keys_part])
            if k > 0:
                new_vals = new_vals + dot(scaled[k - 1], wb[k - 1, :, vals_part])
        inverse = lax.rsqrt(jnp.sum(squares, -1, keepdims=True) / width + EPSILON)
        rb[rows, :] = jnp.broadcast_to(inverse, (T, 128))
        own = pl.ds(pl.multiple_of(start + PAD, T), T)
        window = pl.ds(start, WINDOW)
        kb[own, :] = (new_keys * inverse).astype(BF16)
        bias_rows = jnp.concatenate([bias[p]] * GROUP, axis=0)
        raws = []
        for k in range(KV_HEADS):
            values = xb[k, rows, :].astype(F32)
            hidden = (values * inverse * gf[k, 0:1, :]).astype(BF16)
            hb[k, rows, :] = hidden
            keys = kb[window, pl.ds(k * HEAD_DIM, HEAD_DIM)]
            scores = dot_t(to_rows(hidden), keys)
            raws.append(jnp.exp2(scores * EXP_SCALE + bias_rows))
        last_k = KV_HEADS - 1
        new_vals = new_vals + dot(scaled[last_k], wb[last_k, :, vals_part])
        vb[own, :] = (new_vals * inverse).astype(BF16)
        for k in range(KV_HEADS):
            raw = raws[k]
            vals = vb[window, pl.ds(k * HEAD_DIM, HEAD_DIM)]
            share = 1.0 / jnp.sum(raw, -1, keepdims=True)
            mixed = dot(raw.astype(BF16), vals) * share
            xo[k, rows, :] = (xb[k, rows, :].astype(F32) + to_lanes(mixed)).astype(BF16)
            probs = raw * share
            pb[p, k] = probs
            pt[p, k] = probs.T

        @pl.when(p == 0)
        def _():
            pl.semaphore_wait(barrier, n_dp - 1 + before + after)

        @pl.when(sec < n_sec - 1)
        def _():
            for k in range(KV_HEADS):
                pltpu.make_async_remote_copy(
                    src_ref=xo.at[k, rows],
                    dst_ref=xb.at[k, rows],
                    send_sem=f_send,
                    recv_sem=f_recv.at[p, k],
                    device_id={"section": sec + 1},
                    device_id_type=MESH,
                ).start()

        return carry

    lax.fori_loop(0, pieces, forward, 0)

    def to_peer(dp, src, dst, send_sem, recv_sem):
        return pltpu.make_async_remote_copy(
            src_ref=src,
            dst_ref=dst,
            send_sem=send_sem,
            recv_sem=recv_sem,
            device_id={"dp": dp},
            device_id_type=MESH,
        )

    def wait_for(ref, sem):
        pltpu.make_async_copy(ref, ref, sem).wait()

    peers = []
    for jy in range(grid_y):
        for jx in range(KV_HEADS):
            peer_x, peer_y = (x + jx) % KV_HEADS, (y + jy) % grid_y
            peers.append((jy * KV_HEADS + jx, peer_x * grid_y + peer_y, peer_x, peer_y))
    others = pl.ds(1, n_dp - 1)

    upper, lower = x * grid_y + (y + 1) % grid_y, x * grid_y + (y + grid_y - 1) % grid_y
    half = seq_len // 2
    far = grid_y - 1

    own_hidden = pltpu.make_async_copy(hb.at[x], hg.at[0, 0], in_sem.at[0])
    own_hidden.start()
    for jx in range(1, KV_HEADS):
        peer_x = (x + jx) % KV_HEADS
        to_peer(peer_x * grid_y + y, hb.at[peer_x], hg.at[0, jx], hx_send, hx_recv).start()

    def spread_h():
        own_hidden.wait()
        wait_for(hg.at[0, pl.ds(1, KV_HEADS - 1)], hx_recv)
        if grid_y > 1:
            to_peer(upper, hg.at[0], hg.at[1], hy_send.at[0], hy_recv.at[0]).start()
            to_peer(lower, hg.at[0], hg.at[far], hy_send.at[1], hy_recv.at[1]).start()

    def relay_h():
        if grid_y > 1:
            wait_for(hg.at[1], hy_recv.at[0])
            wait_for(hg.at[far], hy_recv.at[1])
            for i, (dp, source) in enumerate(((upper, 1), (lower, far))):
                rows = pl.ds(i * half, half)
                to_peer(
                    dp, hg.at[source, :, rows], hg.at[2, :, rows], hr_send.at[i], hr_recv.at[i]
                ).start()

    def transpose_h():
        if grid_y > 1:
            for i in range(2):
                wait_for(hg.at[2, :, pl.ds(i * half, half)], hr_recv.at[i])

        for low, high in GROUPS:
            tokens = (high - low) * T
            for c in range(CHUNK // 256):
                hidden = hg[:, :, pl.ds(low * T, tokens), pl.ds(c * 256, 256)]
                ht[pl.ds(c * 256, 256), pl.ds(n_dp * low * T, n_dp * tokens)] = hidden.reshape(
                    n_dp * tokens, 256
                ).T

    late = jnp.logical_not(early) & (sec >= n_sec - 3)
    middle = jnp.logical_not(early | late)
    base = 3 * n_sec // 8
    relay_turn = 2 * (sec - base)
    late_turn = 2 * pieces // 3 - 3 * (n_sec - 1 - sec)

    @pl.when(early)
    def _():
        transpose_w()

    @pl.when(early | middle)
    def _():
        spread_h()

    @pl.when(early)
    def _():
        relay_h()
        transpose_h()

    def backward(step, carry):
        p = pieces - 1 - step
        start = pl.multiple_of(p * T, T)
        rows = pl.ds(start, T)
        window = pl.ds(start, WINDOW)
        own = pl.ds(pl.multiple_of(start + PAD, T), T)
        previous = pl.ds(start, PAD)
        own_keys, own_vals = [], []
        partial = [0.0] * KV_HEADS
        inner = jnp.zeros((T, 128), F32)
        for pair in range(KV_HEADS // 2):
            heads = (2 * pair, 2 * pair + 1)

            @pl.when(sec < n_sec - 1)
            def _():
                pltpu.make_async_remote_copy(
                    src_ref=gb.at[pl.ds(2 * pair, 2), rows],
                    dst_ref=gb.at[pl.ds(2 * pair, 2), rows],
                    send_sem=g_send,
                    recv_sem=g_recv.at[p, pair],
                    device_id={"section": sec},
                    device_id_type=MESH,
                ).wait_recv()

            grads, d_vals = {}, {}
            for k in heads:
                grads[k] = to_rows(gb[k, rows, :])
                d_vals[k] = dot(pt[p, k].astype(BF16), grads[k])
                own_vals.append(dv_acc[k, own, :] + d_vals[k][PAD:])
            pair_vals = jnp.concatenate(own_vals[-2:], axis=1).astype(BF16)
            d_probs, d_probs_t = {}, {}
            for k in heads:
                vals = vb[window, pl.ds(k * HEAD_DIM, HEAD_DIM)]
                d_probs[k] = dot_t(grads[k], vals)
                d_probs_t[k] = dot_t(vals, grads[k])
            part = pl.ds(kv_width + pair * 2 * HEAD_DIM, 2 * HEAD_DIM)
            for c in range(KV_HEADS):
                partial[c] = partial[c] + dot(pair_vals, wt[c, part, :])
            for k in heads:
                hidden = hb[k, rows, :]
                query = to_rows(hidden)
                keys = kb[window, pl.ds(k * HEAD_DIM, HEAD_DIM)]
                probs = pb[p, k]
                product = probs * d_probs[k]
                total = jnp.sum(product, -1, keepdims=True)
                d_low = ((product - probs * total) * SCALE).astype(BF16)
                probs_t = pt[p, k]
                product_t = probs_t * d_probs_t[k]
                total_t = jnp.sum(product_t, 0, keepdims=True)
                d_low_t = ((product_t - probs_t * total_t) * SCALE).astype(BF16)
                d_keys = dot(d_low_t, query)
                own_keys.append(dk_acc[k, own, :] + d_keys[PAD:])
                d_query = to_lanes(dot(d_low, keys))
                dqb[k] = d_query
                inner = inner + fold_lanes(d_query * hidden.astype(F32))
                dk_acc[k, previous, :] += d_keys[:PAD]
                dv_acc[k, previous, :] += d_vals[k][:PAD]
        d_keys = jnp.concatenate(own_keys, axis=1).astype(BF16)
        d_vals = jnp.concatenate(own_vals, axis=1).astype(BF16)
        d_kv = jnp.concatenate([d_keys, d_vals], axis=1)
        for c in range(grid_y):
            do[c, rows, :] = d_kv[:, c * cols : (c + 1) * cols]
        inner = inner + fold_lanes(d_keys.astype(F32) * kb[own, :].astype(F32))
        inner = inner + fold_lanes(d_vals.astype(F32) * vb[own, :].astype(F32))
        mean = jnp.sum(inner, -1, keepdims=True) / width
        inverse = rb[rows, :][:, :1]

        def send_parts():
            for g, (low, high) in enumerate(GROUPS):
                part = pl.ds(low * T, (high - low) * T)

                @pl.when(p == low)
                def _():
                    dg[0, part] = do[y, part]
                    for j, dp, peer_x, peer_y in peers[1:]:
                        to_peer(
                            dp, do.at[peer_y, part], dg.at[j, part], d_send, d_recv.at[g]
                        ).start()

        def send_grads(pair):
            @pl.when(sec > 0)
            def _():
                pltpu.make_async_remote_copy(
                    src_ref=go.at[pl.ds(2 * pair, 2), rows],
                    dst_ref=gb.at[pl.ds(2 * pair, 2), rows],
                    send_sem=g_send,
                    recv_sem=g_recv.at[p, pair],
                    device_id={"section": sec - 1},
                    device_id_type=MESH,
                ).start()

        for k in range(KV_HEADS):
            d_hidden = partial[k] + dqb[k] + dot(d_keys, wt[k, pl.ds(0, kv_width), :])
            normed = xb[k, rows, :].astype(F32) * inverse
            moment = d_hidden * normed
            gsum[k] += moment[0:8] + moment[8:16]
            d_inputs = inverse * (d_hidden * gf[k, 0:1, :] - normed * mean)
            go[k, rows, :] = (gb[k, rows, :].astype(F32) + d_inputs).astype(BF16)
            if k == 1:

                @pl.when(first)
                def _():
                    send_parts()

            if k % 2 == 1:
                send_grads(k // 2)

        @pl.when(sec > 0)
        def _():
            send_parts()

        @pl.when(late & (step == late_turn))
        def _():
            spread_h()

        @pl.when(
            middle
            & (
                (step == relay_turn)
                | ((step == 0) & (relay_turn < 0))
                | ((step == pieces - 1) & (relay_turn >= pieces))
            )
        )
        def _():
            relay_h()

        return carry

    lax.fori_loop(0, pieces, backward, 0)

    def gain_block(dp):
        column = dp * block
        return gs.at[
            column // CHUNK, :, pl.ds(pl.multiple_of(column % CHUNK, block), block)
        ]

    @pl.when(late)
    def _():
        relay_h()

    @pl.when(jnp.logical_not(early))
    def _():
        transpose_h()

    def product(g, part):
        low, high = GROUPS[g]
        tokens = (high - low) * T
        d_kv = dg[:, pl.ds(low * T, tokens), :].reshape(n_dp * tokens, cols)
        return dot(ht[part, pl.ds(n_dp * low * T, n_dp * tokens)], d_kv)

    final = len(GROUPS) - 1
    for g, (low, high) in enumerate(GROUPS):
        wait_for(dg.at[others, pl.ds(low * T, (high - low) * T)], d_recv.at[g])
        if g < final:
            for c in range(CHUNK // 256):
                part = pl.ds(c * 256, 256)
                wacc[part, :] = product(g, part) + (wacc[part, :] if g > 0 else 0.0)
    for jy in (2, 1, 3, 0) if grid_y == 4 else (0,):
        peer_y = (y + jy) % grid_y
        part = pl.ds(pl.multiple_of(peer_y * block, block), block)
        total = wacc[part, :] + product(final, part)
        if jy == 0:
            out_w[:, pl.ds(pl.multiple_of(y * cols, cols), cols)] = total.astype(BF16)
        else:
            eo[jy] = total.astype(BF16)
            to_peer(
                x * grid_y + peer_y, eo.at[jy], eg.at[jy], e_send, e_recv.at[jy]
            ).start()

    for k in range(KV_HEADS):
        total = jnp.sum(gsum[k], 0, keepdims=True).astype(BF16).astype(F32)
        gs[k] = jnp.broadcast_to(total, (8, CHUNK))
    own_gain = pltpu.make_async_copy(gain_block(me), gg.at[0], in_sem.at[1])
    own_gain.start()
    for j, dp, peer_x, peer_y in peers[1:]:
        to_peer(dp, gain_block(dp), gg.at[j], s_send, s_recv).start()

    own_gain.wait()
    wait_for(gg.at[others], s_recv)
    gain_total = gg[0]
    for j in range(1, n_dp):
        gain_total = gain_total + gg[j]
    out_g[...] = gain_total[0:1]

    for jy in range(1, grid_y):
        wait_for(eg.at[jy], e_recv.at[jy])
        source_y = (y + grid_y - jy) % grid_y
        out_w[:, pl.ds(pl.multiple_of(source_y * cols, cols), cols)] = eg[jy]

    if grid_y > 1:
        wait_for(eo.at[pl.ds(1, grid_y - 1)], e_send)
        for i in range(2):
            wait_for(hg.at[0], hy_send.at[i])
            wait_for(hg.at[2, :, pl.ds(i * half, half)], hr_send.at[i])
    wait_for(hg.at[0, pl.ds(1, KV_HEADS - 1)], hx_send)
    wait_for(dg.at[others], d_send)
    wait_for(gg.at[others], s_send)

    @pl.when(sec < n_sec - 1)
    def _():
        wait_for(xo, f_send)

    @pl.when(sec > 0)
    def _():
        wait_for(go, g_send)


def local(n_sec, n_dp, tokens, upstream, gains, w_kv, doc_lengths, seg_lengths, block_mask):
    seq_len, width = tokens.shape[1:]
    pieces = seq_len // T
    kv2 = w_kv.shape[2]
    block = width // n_dp
    grid_y = n_dp // KV_HEADS
    cols = kv2 // grid_y
    any_spec = pl.BlockSpec(memory_space=pl.ANY)
    vmem = pl.BlockSpec(memory_space=pltpu.VMEM)
    smem = pl.BlockSpec(memory_space=pltpu.SMEM)
    features = (KV_HEADS, seq_len, CHUNK)
    dma = pltpu.SemaphoreType.DMA
    grad_weight, grad_gain = pl.pallas_call(
        functools.partial(kernel, n_sec, n_dp),
        out_shape=(
            jax.ShapeDtypeStruct((block, kv2), BF16),
            jax.ShapeDtypeStruct((1, block), F32),
        ),
        in_specs=[any_spec, any_spec, vmem, any_spec, smem, smem, vmem],
        out_specs=(vmem, vmem),
        scratch_shapes=[
            pltpu.VMEM(features, BF16),
            pltpu.VMEM(features, BF16),
            pltpu.VMEM(features, BF16),
            pltpu.VMEM(features, BF16),
            pltpu.VMEM(features, BF16),
            pltpu.VMEM((KV_HEADS, CHUNK, kv2), BF16),
            pltpu.VMEM((KV_HEADS, kv2, CHUNK), BF16),
            pltpu.VMEM((PAD + seq_len, kv2 // 2), BF16),
            pltpu.VMEM((PAD + seq_len, kv2 // 2), BF16),
            pltpu.VMEM((KV_HEADS, PAD + seq_len, HEAD_DIM), F32),
            pltpu.VMEM((KV_HEADS, PAD + seq_len, HEAD_DIM), F32),
            pltpu.VMEM((pieces, KV_HEADS, GROUP * T, WINDOW), F32),
            pltpu.VMEM((pieces, KV_HEADS, WINDOW, GROUP * T), F32),
            pltpu.VMEM((KV_HEADS, T, CHUNK), F32),
            pltpu.VMEM((seq_len, 128), F32),
            pltpu.VMEM((pieces, T, WINDOW), F32),
            pltpu.VMEM((KV_HEADS, 8, CHUNK), F32),
            pltpu.VMEM((KV_HEADS, 8, CHUNK), F32),
            pltpu.VMEM((KV_HEADS, 8, CHUNK), F32),
            pltpu.VMEM((grid_y, KV_HEADS, seq_len, CHUNK), BF16),
            pltpu.VMEM((CHUNK, n_dp * seq_len), BF16),
            pltpu.VMEM((grid_y, seq_len, cols), BF16),
            pltpu.VMEM((n_dp, seq_len, cols), BF16),
            pltpu.VMEM((CHUNK, cols), F32),
            pltpu.VMEM((grid_y, block, cols), BF16),
            pltpu.VMEM((grid_y, block, cols), BF16),
            pltpu.VMEM((n_dp, 8, block), F32),
            dma((KV_HEADS,)),
            dma((KV_HEADS,)),
            dma,
            dma((pieces, KV_HEADS)),
            dma,
            dma((pieces, KV_HEADS // 2)),
            dma,
            dma,
            dma((2,)),
            dma((2,)),
            dma((2,)),
            dma((2,)),
            dma,
            dma((len(GROUPS),)),
            dma,
            dma((grid_y,)),
            dma,
            dma,
        ],
        compiler_params=pltpu.CompilerParams(
            collective_id=0, has_side_effects=True, vmem_limit_bytes=60 * 1024 * 1024
        ),
        cost_estimate=pl.CostEstimate(
            flops=7 * 10**9, bytes_accessed=12 * 2**20, transcendentals=10**6
        ),
        name="relay",
    )(tokens, upstream, gains, w_kv, doc_lengths, seg_lengths, block_mask.transpose(1, 0, 2))
    return grad_weight.astype(F32)[None], grad_gain


def solution(mesh):
    placed = (
        P("dp", None, None),
        P("dp", None, None),
        P("section", None),
        P("section", None, None),
        P("dp", None),
        P("dp", None),
        P("dp", None, None),
    )
    return jax.shard_map(
        functools.partial(local, mesh.shape["section"], mesh.shape["dp"]),
        mesh=mesh,
        in_specs=placed,
        out_specs=(P("section", "dp", None), P("section", "dp")),
        check_vma=False,
    )
```

```python
import functools
import math

import jax
import jax.numpy as jnp
from jax import lax
from jax.experimental import pallas as pl
from jax.experimental.pallas import tpu as pltpu
from jax.sharding import PartitionSpec as P

HEADS = 32
KV_HEADS = 4
GROUP = 8
HEAD_DIM = 128
SEGS = 4
BLK = 16
EPSILON = 1e-06

T = 16
GROUPS = ((6, 12), (3, 6), (0, 3))
WINDOW = 128
PAD = WINDOW - T
CHUNK = GROUP * HEAD_DIM
MESH = pl.DeviceIdType.MESH
F32 = jnp.float32
BF16 = jnp.bfloat16
EXP_SCALE = HEAD_DIM**-0.5 * math.log2(math.e)
SCALE = HEAD_DIM**-0.5


def to_rows(block):
    return jnp.concatenate(
        [block[:, HEAD_DIM * g : HEAD_DIM * (g + 1)] for g in range(GROUP)], axis=0
    )


def to_lanes(block):
    return jnp.concatenate([block[T * g : T * (g + 1)] for g in range(GROUP)], axis=1)


def fold_lanes(block):
    total = block[:, :128]
    for g in range(1, block.shape[1] // 128):
        total = total + block[:, 128 * g : 128 * (g + 1)]
    return total


def dot_t(a, b):
    return lax.dot_general(a, b, (((1,), (1,)), ((), ())), preferred_element_type=F32)


def t_dot(a, b):
    return lax.dot_general(a, b, (((0,), (0,)), ((), ())), preferred_element_type=F32)


def dot(a, b):
    return jnp.dot(a, b, preferred_element_type=F32)


def kernel(
    n_sec,
    n_dp,
    tok,
    ups,
    gain,
    w,
    docs,
    segs,
    table,
    out_w,
    out_g,
    xb,
    hb,
    gb,
    xo,
    go,
    wb,
    wt,
    kb,
    vb,
    dk_acc,
    dv_acc,
    pb,
    pt,
    dqb,
    rb,
    bias,
    gf,
    gsum,
    gs,
    hg,
    ht,
    do,
    dg,
    wacc,
    eo,
    eg,
    gg,
    w_sem,
    in_sem,
    f_send,
    f_recv,
    g_send,
    g_recv,
    hx_send,
    hx_recv,
    hy_send,
    hy_recv,
    hr_send,
    hr_recv,
    d_send,
    d_recv,
    e_send,
    e_recv,
    s_send,
    s_recv,
):
    sec = lax.axis_index("section")
    me = lax.axis_index("dp")
    seq_len = xb.shape[1]
    pieces = seq_len // T
    width = KV_HEADS * CHUNK
    kv_width = KV_HEADS * HEAD_DIM
    block = width // n_dp
    grid_y = n_dp // KV_HEADS
    cols = 2 * kv_width // grid_y
    x, y = me // grid_y, me % grid_y
    first = sec == 0
    last = sec == n_sec - 1
    early = sec < (n_sec + 3) // 4

    w_copies = [
        pltpu.make_async_copy(w.at[0, pl.ds(k * CHUNK, CHUNK)], wb.at[k], w_sem.at[k])
        for k in range(KV_HEADS)
    ]
    tok_copies = [
        pltpu.make_async_copy(tok.at[0, :, pl.ds(k * CHUNK, CHUNK)], xb.at[k], in_sem.at[k])
        for k in range(KV_HEADS)
    ]
    ups_copies = [
        pltpu.make_async_copy(ups.at[0, :, pl.ds(k * CHUNK, CHUNK)], xo.at[k], in_sem.at[k])
        for k in range(KV_HEADS)
    ]

    @pl.when(first)
    def _():
        for copy in tok_copies:
            copy.start()

    for copy in w_copies:
        copy.start()

    @pl.when(last)
    def _():
        for copy in ups_copies:
            copy.start()

    barrier = pltpu.get_barrier_semaphore()

    @pl.when(sec > 0)
    def _():
        pl.semaphore_signal(barrier, inc=1, device_id={"section": sec - 1}, device_id_type=MESH)

    @pl.when(sec < n_sec - 1)
    def _():
        pl.semaphore_signal(barrier, inc=1, device_id={"section": sec + 1}, device_id_type=MESH)

    for j in range(1, n_dp):
        pl.semaphore_signal(
            barrier, inc=1, device_id={"dp": (me + j) % n_dp}, device_id_type=MESH
        )

    kb[pl.ds(0, PAD), :] = jnp.zeros((PAD, kv_width), BF16)
    vb[pl.ds(0, PAD), :] = jnp.zeros((PAD, kv_width), BF16)
    dk_acc[...] = jnp.zeros_like(dk_acc)
    dv_acc[...] = jnp.zeros_like(dv_acc)
    gsum[...] = jnp.zeros_like(gsum)
    for k in range(KV_HEADS):
        gf[k] = jnp.broadcast_to(
            gain[:, pl.ds(k * CHUNK, CHUNK)].astype(F32), (8, CHUNK)
        )

    doc_ends = [docs[0, 0]]
    for d in range(1, docs.shape[1] - 1):
        doc_ends.append(doc_ends[-1] + docs[0, d])

    def doc_of(positions):
        total = jnp.zeros_like(positions)
        for end in doc_ends:
            total = total + jnp.where(positions >= end, 1, 0)
        return total

    row = lax.broadcasted_iota(jnp.int32, (T, WINDOW), 0)
    column = lax.broadcasted_iota(jnp.int32, (T, WINDOW), 1)

    blocks = seq_len // BLK
    opened = table[:, 0, :].astype(BF16)
    block_row = lax.broadcasted_iota(jnp.int32, (blocks, WINDOW), 0)
    block_column = lax.broadcasted_iota(jnp.int32, (blocks, WINDOW), 1) // BLK
    for p in range(pieces):
        queries = row + p * T
        keys = column + (p * T - PAD)
        spread = (block_row == block_column + (p * T - PAD) // BLK).astype(BF16)
        line = dot(opened, spread)[p : p + 1]
        allowed = (
            (keys >= 0)
            & (keys <= queries)
            & (doc_of(keys) == doc_of(queries))
            & ((column // BLK == PAD // BLK) | (line > 0.5))
        )
        bias[p] = jnp.where(allowed, 0.0, -1e30)

    @pl.when(last)
    def _():
        for copy in ups_copies:
            copy.wait()
        sizes = [segs[0, i] for i in range(SEGS)]

        def scale_piece(p, carry):
            rows = pl.ds(pl.multiple_of(p * T, T), T)
            positions = row + p * T
            count = jnp.zeros((T, WINDOW), jnp.int32) + sizes[0]
            end = sizes[0]
            for i in range(1, SEGS):
                count = jnp.where(positions >= end, sizes[i], count)
                end = end + sizes[i]
            factor = seq_len / (SEGS * count.astype(F32))
            factor = jnp.concatenate([factor] * (CHUNK // WINDOW), axis=1)
            for k in range(KV_HEADS):
                gb[k, rows, :] = (xo[k, rows, :].astype(F32) * factor).astype(BF16)
            return carry

        lax.fori_loop(0, pieces, scale_piece, 0)

    @pl.when(first)
    def _():
        for copy in tok_copies:
            copy.wait()

    def transpose_w():
        def part(i, carry):
            k, c = i // 4, i % 4
            source = pl.ds(pl.multiple_of(c * 256, 256), 256)
            for n in range(2 * kv_width // 256):
                wt[k, pl.ds(n * 256, 256), source] = wb[k, source, pl.ds(n * 256, 256)].T
            return carry

        lax.fori_loop(0, KV_HEADS * (CHUNK // 256), part, 0)

    @pl.when(jnp.logical_not(early))
    def _():
        for copy in w_copies:
            copy.wait()
        transpose_w()

    before, after = (sec + n_sec - 1) // n_sec, (2 * n_sec - 2 - sec) // n_sec

    def forward(p, carry):
        start = pl.multiple_of(p * T, T)
        rows = pl.ds(start, T)
        keys_part, vals_part = pl.ds(0, kv_width), pl.ds(kv_width, kv_width)
        new_keys = jnp.zeros((T, kv_width), F32)
        new_vals = jnp.zeros((T, kv_width), F32)
        scaled = []
        squares = jnp.zeros((T, 128), F32)
        for k in range(KV_HEADS):
            arrival = pltpu.make_async_remote_copy(
                src_ref=xb.at[k, rows],
                dst_ref=xb.at[k, rows],
                send_sem=f_send,
                recv_sem=f_recv.at[p, k],
                device_id={"section": sec},
                device_id_type=MESH,
            )

            @pl.when(sec > 0)
            def _():
                arrival.wait_recv()

            @pl.when(early & (p == 0))
            def _():
                w_copies[k].wait()

            values = xb[k, rows, :].astype(F32)
            squares = squares + fold_lanes(values * values)
            scaled.append((values * gf[k, 0:1, :]).astype(BF16))
            new_keys = new_keys + dot(scaled[k], wb[k, :, keys_part])
            if k > 0:
                new_vals = new_vals + dot(scaled[k - 1], wb[k - 1, :, vals_part])
        inverse = lax.rsqrt(jnp.sum(squares, -1, keepdims=True) / width + EPSILON)
        rb[rows, :] = jnp.broadcast_to(inverse, (T, 128))
        own = pl.ds(pl.multiple_of(start + PAD, T), T)
        window = pl.ds(start, WINDOW)
        kb[own, :] = (new_keys * inverse).astype(BF16)
        bias_rows = jnp.concatenate([bias[p]] * GROUP, axis=0)
        raws = []
        for k in range(KV_HEADS):
            values = xb[k, rows, :].astype(F32)
            hidden = (values * inverse * gf[k, 0:1, :]).astype(BF16)
            hb[k, rows, :] = hidden
            keys = kb[window, pl.ds(k * HEAD_DIM, HEAD_DIM)]
            scores = dot_t(to_rows(hidden), keys)
            raws.append(jnp.exp2(scores * EXP_SCALE + bias_rows))
        last_k = KV_HEADS - 1
        new_vals = new_vals + dot(scaled[last_k], wb[last_k, :, vals_part])
        vb[own, :] = (new_vals * inverse).astype(BF16)
        for k in range(KV_HEADS):
            raw = raws[k]
            vals = vb[window, pl.ds(k * HEAD_DIM, HEAD_DIM)]
            share = 1.0 / jnp.sum(raw, -1, keepdims=True)
            mixed = dot(raw.astype(BF16), vals) * share
            xo[k, rows, :] = (xb[k, rows, :].astype(F32) + to_lanes(mixed)).astype(BF16)
            probs = raw * share
            pb[p, k] = probs
            pt[p, k] = probs.T

        @pl.when(p == 0)
        def _():
            pl.semaphore_wait(barrier, n_dp - 1 + before + after)

        @pl.when(sec < n_sec - 1)
        def _():
            for k in range(KV_HEADS):
                pltpu.make_async_remote_copy(
                    src_ref=xo.at[k, rows],
                    dst_ref=xb.at[k, rows],
                    send_sem=f_send,
                    recv_sem=f_recv.at[p, k],
                    device_id={"section": sec + 1},
                    device_id_type=MESH,
                ).start()

        return carry

    lax.fori_loop(0, pieces, forward, 0)

    def to_peer(dp, src, dst, send_sem, recv_sem):
        return pltpu.make_async_remote_copy(
            src_ref=src,
            dst_ref=dst,
            send_sem=send_sem,
            recv_sem=recv_sem,
            device_id={"dp": dp},
            device_id_type=MESH,
        )

    def wait_for(ref, sem):
        pltpu.make_async_copy(ref, ref, sem).wait()

    peers = []
    for jy in range(grid_y):
        for jx in range(KV_HEADS):
            peer_x, peer_y = (x + jx) % KV_HEADS, (y + jy) % grid_y
            peers.append((jy * KV_HEADS + jx, peer_x * grid_y + peer_y, peer_x, peer_y))
    others = pl.ds(1, n_dp - 1)

    upper, lower = x * grid_y + (y + 1) % grid_y, x * grid_y + (y + grid_y - 1) % grid_y
    half = seq_len // 2
    far = grid_y - 1

    own_hidden = pltpu.make_async_copy(hb.at[x], hg.at[0, 0], in_sem.at[0])
    own_hidden.start()
    for jx in range(1, KV_HEADS):
        peer_x = (x + jx) % KV_HEADS
        to_peer(peer_x * grid_y + y, hb.at[peer_x], hg.at[0, jx], hx_send, hx_recv).start()

    def spread_h():
        own_hidden.wait()
        wait_for(hg.at[0, pl.ds(1, KV_HEADS - 1)], hx_recv)
        if grid_y > 1:
            to_peer(upper, hg.at[0], hg.at[1], hy_send.at[0], hy_recv.at[0]).start()
            to_peer(lower, hg.at[0], hg.at[far], hy_send.at[1], hy_recv.at[1]).start()

    def relay_h():
        if grid_y > 1:
            wait_for(hg.at[1], hy_recv.at[0])
            wait_for(hg.at[far], hy_recv.at[1])
            for i, (dp, source) in enumerate(((upper, 1), (lower, far))):
                rows = pl.ds(i * half, half)
                to_peer(
                    dp, hg.at[source, :, rows], hg.at[2, :, rows], hr_send.at[i], hr_recv.at[i]
                ).start()

    def transpose_h():
        if grid_y > 1:
            for i in range(2):
                wait_for(hg.at[2, :, pl.ds(i * half, half)], hr_recv.at[i])

        for low, high in GROUPS:
            tokens = (high - low) * T
            for c in range(CHUNK // 256):
                hidden = hg[:, :, pl.ds(low * T, tokens), pl.ds(c * 256, 256)]
                ht[pl.ds(c * 256, 256), pl.ds(n_dp * low * T, n_dp * tokens)] = hidden.reshape(
                    n_dp * tokens, 256
                ).T

    late = jnp.logical_not(early) & (sec >= n_sec - 3)
    middle = jnp.logical_not(early | late)
    base = 3 * n_sec // 8
    relay_turn = 2 * (sec - base)
    late_turn = 2 * pieces // 3 - 3 * (n_sec - 1 - sec)

    @pl.when(early)
    def _():
        transpose_w()

    @pl.when(early | middle)
    def _():
        spread_h()

    @pl.when(early)
    def _():
        relay_h()
        transpose_h()

    def backward(step, carry):
        p = pieces - 1 - step
        start = pl.multiple_of(p * T, T)
        rows = pl.ds(start, T)
        window = pl.ds(start, WINDOW)
        own = pl.ds(pl.multiple_of(start + PAD, T), T)
        previous = pl.ds(start, PAD)
        own_keys, own_vals = [], []
        partial = [0.0] * KV_HEADS
        inner = jnp.zeros((T, 128), F32)
        for pair in range(KV_HEADS // 2):
            heads = (2 * pair, 2 * pair + 1)

            @pl.when(sec < n_sec - 1)
            def _():
                pltpu.make_async_remote_copy(
                    src_ref=gb.at[pl.ds(2 * pair, 2), rows],
                    dst_ref=gb.at[pl.ds(2 * pair, 2), rows],
                    send_sem=g_send,
                    recv_sem=g_recv.at[p, pair],
                    device_id={"section": sec},
                    device_id_type=MESH,
                ).wait_recv()

            grads, d_vals = {}, {}
            for k in heads:
                grads[k] = to_rows(gb[k, rows, :])
                d_vals[k] = dot(pt[p, k].astype(BF16), grads[k])
                own_vals.append(dv_acc[k, own, :] + d_vals[k][PAD:])
            pair_vals = jnp.concatenate(own_vals[-2:], axis=1).astype(BF16)
            d_probs, d_probs_t = {}, {}
            for k in heads:
                vals = vb[window, pl.ds(k * HEAD_DIM, HEAD_DIM)]
                d_probs[k] = dot_t(grads[k], vals)
                d_probs_t[k] = dot_t(vals, grads[k])
            part = pl.ds(kv_width + pair * 2 * HEAD_DIM, 2 * HEAD_DIM)
            for c in range(KV_HEADS):
                partial[c] = partial[c] + dot(pair_vals, wt[c, part, :])
            for k in heads:
                hidden = hb[k, rows, :]
                query = to_rows(hidden)
                keys = kb[window, pl.ds(k * HEAD_DIM, HEAD_DIM)]
                probs = pb[p, k]
                product = probs * d_probs[k]
                total = jnp.sum(product, -1, keepdims=True)
                d_low = ((product - probs * total) * SCALE).astype(BF16)
                probs_t = pt[p, k]
                product_t = probs_t * d_probs_t[k]
                total_t = jnp.sum(product_t, 0, keepdims=True)
                d_low_t = ((product_t - probs_t * total_t) * SCALE).astype(BF16)
                d_keys = dot(d_low_t, query)
                own_keys.append(dk_acc[k, own, :] + d_keys[PAD:])
                d_query = to_lanes(dot(d_low, keys))
                dqb[k] = d_query
                inner = inner + fold_lanes(d_query * hidden.astype(F32))
                dk_acc[k, previous, :] += d_keys[:PAD]
                dv_acc[k, previous, :] += d_vals[k][:PAD]
        d_keys = jnp.concatenate(own_keys, axis=1).astype(BF16)
        d_vals = jnp.concatenate(own_vals, axis=1).astype(BF16)
        d_kv = jnp.concatenate([d_keys, d_vals], axis=1)
        for c in range(grid_y):
            do[c, rows, :] = d_kv[:, c * cols : (c + 1) * cols]
        inner = inner + fold_lanes(d_keys.astype(F32) * kb[own, :].astype(F32))
        inner = inner + fold_lanes(d_vals.astype(F32) * vb[own, :].astype(F32))
        mean = jnp.sum(inner, -1, keepdims=True) / width
        inverse = rb[rows, :][:, :1]

        def send_parts():
            near = sec < 2
            whole = [(g, low, high, p == low) for g, (low, high) in enumerate(GROUPS)]
            g, low, high, here = whole.pop()
            sends = whole + [
                (g, low, high, here & jnp.logical_not(near)),
                (g, low + 1, high, near & (p == low + 1)),
                (g, low, low + 1, near & here),
            ]
            for g, low, high, here in sends:
                part = pl.ds(low * T, (high - low) * T)

                @pl.when(here)
                def _():
                    dg[0, part] = do[y, part]
                    for j, dp, peer_x, peer_y in peers[1:]:
                        to_peer(
                            dp, do.at[peer_y, part], dg.at[j, part], d_send, d_recv.at[g]
                        ).start()

        def send_grads(pair):
            @pl.when(sec > 0)
            def _():
                pltpu.make_async_remote_copy(
                    src_ref=go.at[pl.ds(2 * pair, 2), rows],
                    dst_ref=gb.at[pl.ds(2 * pair, 2), rows],
                    send_sem=g_send,
                    recv_sem=g_recv.at[p, pair],
                    device_id={"section": sec - 1},
                    device_id_type=MESH,
                ).start()

        for k in range(KV_HEADS):
            d_hidden = partial[k] + dqb[k] + dot(d_keys, wt[k, pl.ds(0, kv_width), :])
            normed = xb[k, rows, :].astype(F32) * inverse
            moment = d_hidden * normed
            gsum[k] += moment[0:8] + moment[8:16]
            d_inputs = inverse * (d_hidden * gf[k, 0:1, :] - normed * mean)
            go[k, rows, :] = (gb[k, rows, :].astype(F32) + d_inputs).astype(BF16)
            if k == 1:

                @pl.when(first)
                def _():
                    send_parts()

            if k % 2 == 1:
                send_grads(k // 2)

        @pl.when(sec > 0)
        def _():
            send_parts()

        @pl.when(late & (step == late_turn))
        def _():
            spread_h()

        @pl.when(
            middle
            & (
                (step == relay_turn)
                | ((step == 0) & (relay_turn < 0))
                | ((step == pieces - 1) & (relay_turn >= pieces))
            )
        )
        def _():
            relay_h()

        return carry

    lax.fori_loop(0, pieces, backward, 0)

    def gain_block(dp):
        column = dp * block
        return gs.at[
            column // CHUNK, :, pl.ds(pl.multiple_of(column % CHUNK, block), block)
        ]

    @pl.when(late)
    def _():
        relay_h()

    @pl.when(jnp.logical_not(early))
    def _():
        transpose_h()

    def product(g, part):
        low, high = GROUPS[g]
        tokens = (high - low) * T
        d_kv = dg[:, pl.ds(low * T, tokens), :].reshape(n_dp * tokens, cols)
        return dot(ht[part, pl.ds(n_dp * low * T, n_dp * tokens)], d_kv)

    final = len(GROUPS) - 1
    for g, (low, high) in enumerate(GROUPS):
        wait_for(dg.at[others, pl.ds(low * T, (high - low) * T)], d_recv.at[g])
        if g < final:
            for c in range(CHUNK // 256):
                part = pl.ds(c * 256, 256)
                wacc[part, :] = product(g, part) + (wacc[part, :] if g > 0 else 0.0)
    for jy in (2, 1, 3, 0) if grid_y == 4 else (0,):
        peer_y = (y + jy) % grid_y
        part = pl.ds(pl.multiple_of(peer_y * block, block), block)
        total = wacc[part, :] + product(final, part)
        if jy == 0:
            out_w[:, pl.ds(pl.multiple_of(y * cols, cols), cols)] = total.astype(BF16)
        else:
            eo[jy] = total.astype(BF16)
            to_peer(
                x * grid_y + peer_y, eo.at[jy], eg.at[jy], e_send, e_recv.at[jy]
            ).start()

    for k in range(KV_HEADS):
        total = jnp.sum(gsum[k], 0, keepdims=True).astype(BF16).astype(F32)
        gs[k] = jnp.broadcast_to(total, (8, CHUNK))
    own_gain = pltpu.make_async_copy(gain_block(me), gg.at[0], in_sem.at[1])
    own_gain.start()
    for j, dp, peer_x, peer_y in peers[1:]:
        to_peer(dp, gain_block(dp), gg.at[j], s_send, s_recv).start()

    own_gain.wait()
    wait_for(gg.at[others], s_recv)
    gain_total = gg[0]
    for j in range(1, n_dp):
        gain_total = gain_total + gg[j]
    out_g[...] = gain_total[0:1]

    for jy in range(1, grid_y):
        wait_for(eg.at[jy], e_recv.at[jy])
        source_y = (y + grid_y - jy) % grid_y
        out_w[:, pl.ds(pl.multiple_of(source_y * cols, cols), cols)] = eg[jy]

    if grid_y > 1:
        wait_for(eo.at[pl.ds(1, grid_y - 1)], e_send)
        for i in range(2):
            wait_for(hg.at[0], hy_send.at[i])
            wait_for(hg.at[2, :, pl.ds(i * half, half)], hr_send.at[i])
    wait_for(hg.at[0, pl.ds(1, KV_HEADS - 1)], hx_send)
    wait_for(dg.at[others], d_send)
    wait_for(gg.at[others], s_send)

    @pl.when(sec < n_sec - 1)
    def _():
        wait_for(xo, f_send)

    @pl.when(sec > 0)
    def _():
        wait_for(go, g_send)


def local(n_sec, n_dp, tokens, upstream, gains, w_kv, doc_lengths, seg_lengths, block_mask):
    seq_len, width = tokens.shape[1:]
    pieces = seq_len // T
    kv2 = w_kv.shape[2]
    block = width // n_dp
    grid_y = n_dp // KV_HEADS
    cols = kv2 // grid_y
    any_spec = pl.BlockSpec(memory_space=pl.ANY)
    vmem = pl.BlockSpec(memory_space=pltpu.VMEM)
    smem = pl.BlockSpec(memory_space=pltpu.SMEM)
    features = (KV_HEADS, seq_len, CHUNK)
    dma = pltpu.SemaphoreType.DMA
    grad_weight, grad_gain = pl.pallas_call(
        functools.partial(kernel, n_sec, n_dp),
        out_shape=(
            jax.ShapeDtypeStruct((block, kv2), BF16),
            jax.ShapeDtypeStruct((1, block), F32),
        ),
        in_specs=[any_spec, any_spec, vmem, any_spec, smem, smem, vmem],
        out_specs=(vmem, vmem),
        scratch_shapes=[
            pltpu.VMEM(features, BF16),
            pltpu.VMEM(features, BF16),
            pltpu.VMEM(features, BF16),
            pltpu.VMEM(features, BF16),
            pltpu.VMEM(features, BF16),
            pltpu.VMEM((KV_HEADS, CHUNK, kv2), BF16),
            pltpu.VMEM((KV_HEADS, kv2, CHUNK), BF16),
            pltpu.VMEM((PAD + seq_len, kv2 // 2), BF16),
            pltpu.VMEM((PAD + seq_len, kv2 // 2), BF16),
            pltpu.VMEM((KV_HEADS, PAD + seq_len, HEAD_DIM), F32),
            pltpu.VMEM((KV_HEADS, PAD + seq_len, HEAD_DIM), F32),
            pltpu.VMEM((pieces, KV_HEADS, GROUP * T, WINDOW), F32),
            pltpu.VMEM((pieces, KV_HEADS, WINDOW, GROUP * T), F32),
            pltpu.VMEM((KV_HEADS, T, CHUNK), F32),
            pltpu.VMEM((seq_len, 128), F32),
            pltpu.VMEM((pieces, T, WINDOW), F32),
            pltpu.VMEM((KV_HEADS, 8, CHUNK), F32),
            pltpu.VMEM((KV_HEADS, 8, CHUNK), F32),
            pltpu.VMEM((KV_HEADS, 8, CHUNK), F32),
            pltpu.VMEM((grid_y, KV_HEADS, seq_len, CHUNK), BF16),
            pltpu.VMEM((CHUNK, n_dp * seq_len), BF16),
            pltpu.VMEM((grid_y, seq_len, cols), BF16),
            pltpu.VMEM((n_dp, seq_len, cols), BF16),
            pltpu.VMEM((CHUNK, cols), F32),
            pltpu.VMEM((grid_y, block, cols), BF16),
            pltpu.VMEM((grid_y, block, cols), BF16),
            pltpu.VMEM((n_dp, 8, block), F32),
            dma((KV_HEADS,)),
            dma((KV_HEADS,)),
            dma,
            dma((pieces, KV_HEADS)),
            dma,
            dma((pieces, KV_HEADS // 2)),
            dma,
            dma,
            dma((2,)),
            dma((2,)),
            dma((2,)),
            dma((2,)),
            dma,
            dma((len(GROUPS),)),
            dma,
            dma((grid_y,)),
            dma,
            dma,
        ],
        compiler_params=pltpu.CompilerParams(
            collective_id=0, has_side_effects=True, vmem_limit_bytes=60 * 1024 * 1024
        ),
        cost_estimate=pl.CostEstimate(
            flops=7 * 10**9, bytes_accessed=12 * 2**20, transcendentals=10**6
        ),
        name="relay",
    )(tokens, upstream, gains, w_kv, doc_lengths, seg_lengths, block_mask.transpose(1, 0, 2))
    return grad_weight.astype(F32)[None], grad_gain


def solution(mesh):
    placed = (
        P("dp", None, None),
        P("dp", None, None),
        P("section", None),
        P("section", None, None),
        P("dp", None),
        P("dp", None),
        P("dp", None, None),
    )
    return jax.shard_map(
        functools.partial(local, mesh.shape["section"], mesh.shape["dp"]),
        mesh=mesh,
        in_specs=placed,
        out_specs=(P("section", "dp", None), P("section", "dp")),
        check_vma=False,
    )
```

```python
import functools
import math

import jax
import jax.numpy as jnp
from jax import lax
from jax.experimental import pallas as pl
from jax.experimental.pallas import tpu as pltpu
from jax.sharding import PartitionSpec as P

HEADS = 32
KV_HEADS = 4
GROUP = 8
HEAD_DIM = 128
SEGS = 4
BLK = 16
EPSILON = 1e-06

T = 16
GROUPS = ((6, 12), (3, 6), (0, 3))
WINDOW = 128
PAD = WINDOW - T
CHUNK = GROUP * HEAD_DIM
MESH = pl.DeviceIdType.MESH
F32 = jnp.float32
BF16 = jnp.bfloat16
EXP_SCALE = HEAD_DIM**-0.5 * math.log2(math.e)
SCALE = HEAD_DIM**-0.5


def to_rows(block):
    return jnp.concatenate(
        [block[:, HEAD_DIM * g : HEAD_DIM * (g + 1)] for g in range(GROUP)], axis=0
    )


def to_lanes(block):
    return jnp.concatenate([block[T * g : T * (g + 1)] for g in range(GROUP)], axis=1)


def fold_lanes(block):
    total = block[:, :128]
    for g in range(1, block.shape[1] // 128):
        total = total + block[:, 128 * g : 128 * (g + 1)]
    return total


def dot_t(a, b):
    return lax.dot_general(a, b, (((1,), (1,)), ((), ())), preferred_element_type=F32)


def t_dot(a, b):
    return lax.dot_general(a, b, (((0,), (0,)), ((), ())), preferred_element_type=F32)


def dot(a, b):
    return jnp.dot(a, b, preferred_element_type=F32)


def kernel(
    n_sec,
    n_dp,
    tok,
    ups,
    gain,
    w,
    docs,
    segs,
    table,
    out_w,
    out_g,
    xb,
    hb,
    gb,
    xo,
    go,
    wb,
    wt,
    kb,
    vb,
    dk_acc,
    dv_acc,
    pb,
    pt,
    dqb,
    rb,
    bias,
    gf,
    gsum,
    gs,
    hg,
    ht,
    do,
    dg,
    wacc,
    eo,
    eg,
    gg,
    w_sem,
    in_sem,
    f_send,
    f_recv,
    g_send,
    g_recv,
    hx_send,
    hx_recv,
    hy_send,
    hy_recv,
    hr_send,
    hr_recv,
    d_send,
    d_recv,
    e_send,
    e_recv,
    s_send,
    s_recv,
):
    sec = lax.axis_index("section")
    me = lax.axis_index("dp")
    seq_len = xb.shape[1]
    pieces = seq_len // T
    width = KV_HEADS * CHUNK
    kv_width = KV_HEADS * HEAD_DIM
    block = width // n_dp
    grid_y = n_dp // KV_HEADS
    cols = 2 * kv_width // grid_y
    x, y = me // grid_y, me % grid_y
    first = sec == 0
    last = sec == n_sec - 1
    early = sec < (n_sec + 3) // 4

    w_copies = [
        pltpu.make_async_copy(w.at[0, pl.ds(k * CHUNK, CHUNK)], wb.at[k], w_sem.at[k])
        for k in range(KV_HEADS)
    ]
    tok_copies = [
        pltpu.make_async_copy(tok.at[0, :, pl.ds(k * CHUNK, CHUNK)], xb.at[k], in_sem.at[k])
        for k in range(KV_HEADS)
    ]
    ups_copies = [
        pltpu.make_async_copy(ups.at[0, :, pl.ds(k * CHUNK, CHUNK)], xo.at[k], in_sem.at[k])
        for k in range(KV_HEADS)
    ]

    @pl.when(first)
    def _():
        for copy in tok_copies:
            copy.start()

    for copy in w_copies:
        copy.start()

    @pl.when(last)
    def _():
        for copy in ups_copies:
            copy.start()

    barrier = pltpu.get_barrier_semaphore()

    @pl.when(sec > 0)
    def _():
        pl.semaphore_signal(barrier, inc=1, device_id={"section": sec - 1}, device_id_type=MESH)

    @pl.when(sec < n_sec - 1)
    def _():
        pl.semaphore_signal(barrier, inc=1, device_id={"section": sec + 1}, device_id_type=MESH)

    for j in range(1, n_dp):
        pl.semaphore_signal(
            barrier, inc=1, device_id={"dp": (me + j) % n_dp}, device_id_type=MESH
        )

    kb[pl.ds(0, PAD), :] = jnp.zeros((PAD, kv_width), BF16)
    vb[pl.ds(0, PAD), :] = jnp.zeros((PAD, kv_width), BF16)
    dk_acc[...] = jnp.zeros_like(dk_acc)
    dv_acc[...] = jnp.zeros_like(dv_acc)
    gsum[...] = jnp.zeros_like(gsum)
    for k in range(KV_HEADS):
        gf[k] = jnp.broadcast_to(
            gain[:, pl.ds(k * CHUNK, CHUNK)].astype(F32), (8, CHUNK)
        )

    doc_ends = [docs[0, 0]]
    for d in range(1, docs.shape[1] - 1):
        doc_ends.append(doc_ends[-1] + docs[0, d])

    def doc_of(positions):
        total = jnp.zeros_like(positions)
        for end in doc_ends:
            total = total + jnp.where(positions >= end, 1, 0)
        return total

    row = lax.broadcasted_iota(jnp.int32, (T, WINDOW), 0)
    column = lax.broadcasted_iota(jnp.int32, (T, WINDOW), 1)

    blocks = seq_len // BLK
    opened = table[:, 0, :].astype(BF16)
    block_row = lax.broadcasted_iota(jnp.int32, (blocks, WINDOW), 0)
    block_column = lax.broadcasted_iota(jnp.int32, (blocks, WINDOW), 1) // BLK
    for p in range(pieces):
        queries = row + p * T
        keys = column + (p * T - PAD)
        spread = (block_row == block_column + (p * T - PAD) // BLK).astype(BF16)
        line = dot(opened, spread)[p : p + 1]
        allowed = (
            (keys >= 0)
            & (keys <= queries)
            & (doc_of(keys) == doc_of(queries))
            & ((column // BLK == PAD // BLK) | (line > 0.5))
        )
        bias[p] = jnp.where(allowed, 0.0, -1e30)

    @pl.when(last)
    def _():
        for copy in ups_copies:
            copy.wait()
        sizes = [segs[0, i] for i in range(SEGS)]

        def scale_piece(p, carry):
            rows = pl.ds(pl.multiple_of(p * T, T), T)
            positions = row + p * T
            count = jnp.zeros((T, WINDOW), jnp.int32) + sizes[0]
            end = sizes[0]
            for i in range(1, SEGS):
                count = jnp.where(positions >= end, sizes[i], count)
                end = end + sizes[i]
            factor = seq_len / (SEGS * count.astype(F32))
            factor = jnp.concatenate([factor] * (CHUNK // WINDOW), axis=1)
            for k in range(KV_HEADS):
                gb[k, rows, :] = (xo[k, rows, :].astype(F32) * factor).astype(BF16)
            return carry

        lax.fori_loop(0, pieces, scale_piece, 0)

    @pl.when(first)
    def _():
        for copy in tok_copies:
            copy.wait()

    def transpose_w():
        def part(i, carry):
            k, c = i // 4, i % 4
            source = pl.ds(pl.multiple_of(c * 256, 256), 256)
            for n in range(2 * kv_width // 256):
                wt[k, pl.ds(n * 256, 256), source] = wb[k, source, pl.ds(n * 256, 256)].T
            return carry

        lax.fori_loop(0, KV_HEADS * (CHUNK // 256), part, 0)

    @pl.when(jnp.logical_not(early))
    def _():
        for copy in w_copies:
            copy.wait()
        transpose_w()

    before, after = (sec + n_sec - 1) // n_sec, (2 * n_sec - 2 - sec) // n_sec

    def forward(p, carry):
        start = pl.multiple_of(p * T, T)
        rows = pl.ds(start, T)
        keys_part, vals_part = pl.ds(0, kv_width), pl.ds(kv_width, kv_width)
        new_keys = jnp.zeros((T, kv_width), F32)
        new_vals = jnp.zeros((T, kv_width), F32)
        scaled = []
        squares = jnp.zeros((T, 128), F32)
        for k in range(KV_HEADS):
            arrival = pltpu.make_async_remote_copy(
                src_ref=xb.at[k, rows],
                dst_ref=xb.at[k, rows],
                send_sem=f_send,
                recv_sem=f_recv.at[p, k],
                device_id={"section": sec},
                device_id_type=MESH,
            )

            @pl.when(sec > 0)
            def _():
                arrival.wait_recv()

            @pl.when(early & (p == 0))
            def _():
                w_copies[k].wait()

            values = xb[k, rows, :].astype(F32)
            squares = squares + fold_lanes(values * values)
            scaled.append((values * gf[k, 0:1, :]).astype(BF16))
            new_keys = new_keys + dot(scaled[k], wb[k, :, keys_part])
            if k > 0:
                new_vals = new_vals + dot(scaled[k - 1], wb[k - 1, :, vals_part])
        inverse = lax.rsqrt(jnp.sum(squares, -1, keepdims=True) / width + EPSILON)
        rb[rows, :] = jnp.broadcast_to(inverse, (T, 128))
        own = pl.ds(pl.multiple_of(start + PAD, T), T)
        window = pl.ds(start, WINDOW)
        kb[own, :] = (new_keys * inverse).astype(BF16)
        bias_rows = jnp.concatenate([bias[p]] * GROUP, axis=0)
        raws = []
        for k in range(KV_HEADS):
            values = xb[k, rows, :].astype(F32)
            hidden = (values * inverse * gf[k, 0:1, :]).astype(BF16)
            hb[k, rows, :] = hidden
            keys = kb[window, pl.ds(k * HEAD_DIM, HEAD_DIM)]
            scores = dot_t(to_rows(hidden), keys)
            raws.append(jnp.exp2(scores * EXP_SCALE + bias_rows))
        last_k = KV_HEADS - 1
        new_vals = new_vals + dot(scaled[last_k], wb[last_k, :, vals_part])
        vb[own, :] = (new_vals * inverse).astype(BF16)
        for k in range(KV_HEADS):
            raw = raws[k]
            vals = vb[window, pl.ds(k * HEAD_DIM, HEAD_DIM)]
            share = 1.0 / jnp.sum(raw, -1, keepdims=True)
            mixed = dot(raw.astype(BF16), vals) * share
            xo[k, rows, :] = (xb[k, rows, :].astype(F32) + to_lanes(mixed)).astype(BF16)
            probs = raw * share
            pb[p, k] = probs
            pt[p, k] = probs.T

        @pl.when(p == 0)
        def _():
            pl.semaphore_wait(barrier, n_dp - 1 + before + after)

        @pl.when(sec < n_sec - 1)
        def _():
            for k in range(KV_HEADS):
                pltpu.make_async_remote_copy(
                    src_ref=xo.at[k, rows],
                    dst_ref=xb.at[k, rows],
                    send_sem=f_send,
                    recv_sem=f_recv.at[p, k],
                    device_id={"section": sec + 1},
                    device_id_type=MESH,
                ).start()

        return carry

    lax.fori_loop(0, pieces, forward, 0)

    def to_peer(dp, src, dst, send_sem, recv_sem):
        return pltpu.make_async_remote_copy(
            src_ref=src,
            dst_ref=dst,
            send_sem=send_sem,
            recv_sem=recv_sem,
            device_id={"dp": dp},
            device_id_type=MESH,
        )

    def wait_for(ref, sem):
        pltpu.make_async_copy(ref, ref, sem).wait()

    peers = []
    for jy in range(grid_y):
        for jx in range(KV_HEADS):
            peer_x, peer_y = (x + jx) % KV_HEADS, (y + jy) % grid_y
            peers.append((jy * KV_HEADS + jx, peer_x * grid_y + peer_y, peer_x, peer_y))
    others = pl.ds(1, n_dp - 1)

    def hops(peer):
        jx, jy = peer[0] % KV_HEADS, peer[0] // KV_HEADS
        return min(jx, KV_HEADS - jx) + min(jy, grid_y - jy)

    far_first = sorted(peers[1:], key=hops, reverse=True)

    upper, lower = x * grid_y + (y + 1) % grid_y, x * grid_y + (y + grid_y - 1) % grid_y
    half = seq_len // 2
    far = grid_y - 1

    own_hidden = pltpu.make_async_copy(hb.at[x], hg.at[0, 0], in_sem.at[0])
    own_hidden.start()
    for jx in range(1, KV_HEADS):
        peer_x = (x + jx) % KV_HEADS
        to_peer(peer_x * grid_y + y, hb.at[peer_x], hg.at[0, jx], hx_send, hx_recv).start()

    def spread_h():
        own_hidden.wait()
        wait_for(hg.at[0, pl.ds(1, KV_HEADS - 1)], hx_recv)
        if grid_y > 1:
            to_peer(upper, hg.at[0], hg.at[1], hy_send.at[0], hy_recv.at[0]).start()
            to_peer(lower, hg.at[0], hg.at[far], hy_send.at[1], hy_recv.at[1]).start()

    def relay_h():
        if grid_y > 1:
            wait_for(hg.at[1], hy_recv.at[0])
            wait_for(hg.at[far], hy_recv.at[1])
            for i, (dp, source) in enumerate(((upper, 1), (lower, far))):
                rows = pl.ds(i * half, half)
                to_peer(
                    dp, hg.at[source, :, rows], hg.at[2, :, rows], hr_send.at[i], hr_recv.at[i]
                ).start()

    def transpose_h():
        if grid_y > 1:
            for i in range(2):
                wait_for(hg.at[2, :, pl.ds(i * half, half)], hr_recv.at[i])

        for low, high in GROUPS:
            tokens = (high - low) * T
            for c in range(CHUNK // 256):
                hidden = hg[:, :, pl.ds(low * T, tokens), pl.ds(c * 256, 256)]
                ht[pl.ds(c * 256, 256), pl.ds(n_dp * low * T, n_dp * tokens)] = hidden.reshape(
                    n_dp * tokens, 256
                ).T

    late = jnp.logical_not(early) & (sec >= n_sec - 3)
    middle = jnp.logical_not(early | late)
    base = 3 * n_sec // 8
    relay_turn = 2 * (sec - base)
    late_turn = 2 * pieces // 3 - 3 * (n_sec - 1 - sec)

    @pl.when(early)
    def _():
        transpose_w()

    @pl.when(early | middle)
    def _():
        spread_h()

    @pl.when(early)
    def _():
        relay_h()
        transpose_h()

    def backward(step, carry):
        p = pieces - 1 - step
        start = pl.multiple_of(p * T, T)
        rows = pl.ds(start, T)
        window = pl.ds(start, WINDOW)
        own = pl.ds(pl.multiple_of(start + PAD, T), T)
        previous = pl.ds(start, PAD)
        own_keys, own_vals = [], []
        partial = [0.0] * KV_HEADS
        inner = jnp.zeros((T, 128), F32)
        for pair in range(KV_HEADS // 2):
            heads = (2 * pair, 2 * pair + 1)

            @pl.when(sec < n_sec - 1)
            def _():
                pltpu.make_async_remote_copy(
                    src_ref=gb.at[pl.ds(2 * pair, 2), rows],
                    dst_ref=gb.at[pl.ds(2 * pair, 2), rows],
                    send_sem=g_send,
                    recv_sem=g_recv.at[p, pair],
                    device_id={"section": sec},
                    device_id_type=MESH,
                ).wait_recv()

            grads, d_vals = {}, {}
            for k in heads:
                grads[k] = to_rows(gb[k, rows, :])
                d_vals[k] = dot(pt[p, k].astype(BF16), grads[k])
                own_vals.append(dv_acc[k, own, :] + d_vals[k][PAD:])
            pair_vals = jnp.concatenate(own_vals[-2:], axis=1).astype(BF16)
            d_probs, d_probs_t = {}, {}
            for k in heads:
                vals = vb[window, pl.ds(k * HEAD_DIM, HEAD_DIM)]
                d_probs[k] = dot_t(grads[k], vals)
                d_probs_t[k] = dot_t(vals, grads[k])
            part = pl.ds(kv_width + pair * 2 * HEAD_DIM, 2 * HEAD_DIM)
            for c in range(KV_HEADS):
                partial[c] = partial[c] + dot(pair_vals, wt[c, part, :])
            for k in heads:
                hidden = hb[k, rows, :]
                query = to_rows(hidden)
                keys = kb[window, pl.ds(k * HEAD_DIM, HEAD_DIM)]
                probs = pb[p, k]
                product = probs * d_probs[k]
                total = jnp.sum(product, -1, keepdims=True)
                d_low = ((product - probs * total) * SCALE).astype(BF16)
                probs_t = pt[p, k]
                product_t = probs_t * d_probs_t[k]
                total_t = jnp.sum(product_t, 0, keepdims=True)
                d_low_t = ((product_t - probs_t * total_t) * SCALE).astype(BF16)
                d_keys = dot(d_low_t, query)
                own_keys.append(dk_acc[k, own, :] + d_keys[PAD:])
                d_query = to_lanes(dot(d_low, keys))
                dqb[k] = d_query
                inner = inner + fold_lanes(d_query * hidden.astype(F32))
                dk_acc[k, previous, :] += d_keys[:PAD]
                dv_acc[k, previous, :] += d_vals[k][:PAD]
        d_keys = jnp.concatenate(own_keys, axis=1).astype(BF16)
        d_vals = jnp.concatenate(own_vals, axis=1).astype(BF16)
        d_kv = jnp.concatenate([d_keys, d_vals], axis=1)
        for c in range(grid_y):
            do[c, rows, :] = d_kv[:, c * cols : (c + 1) * cols]
        inner = inner + fold_lanes(d_keys.astype(F32) * kb[own, :].astype(F32))
        inner = inner + fold_lanes(d_vals.astype(F32) * vb[own, :].astype(F32))
        mean = jnp.sum(inner, -1, keepdims=True) / width
        inverse = rb[rows, :][:, :1]

        def send_parts():
            near = sec < 2
            whole = [(g, low, high, p == low) for g, (low, high) in enumerate(GROUPS)]
            g, low, high, here = whole.pop()
            sends = whole + [
                (g, low, high, here & jnp.logical_not(near)),
                (g, low + 1, high, near & (p == low + 1)),
                (g, low, low + 1, near & here),
            ]
            for g, low, high, here in sends:
                part = pl.ds(low * T, (high - low) * T)

                @pl.when(here)
                def _():
                    dg[0, part] = do[y, part]
                    for j, dp, peer_x, peer_y in far_first:
                        to_peer(
                            dp, do.at[peer_y, part], dg.at[j, part], d_send, d_recv.at[g]
                        ).start()

        def send_grads(pair):
            @pl.when(sec > 0)
            def _():
                pltpu.make_async_remote_copy(
                    src_ref=go.at[pl.ds(2 * pair, 2), rows],
                    dst_ref=gb.at[pl.ds(2 * pair, 2), rows],
                    send_sem=g_send,
                    recv_sem=g_recv.at[p, pair],
                    device_id={"section": sec - 1},
                    device_id_type=MESH,
                ).start()

        for k in range(KV_HEADS):
            d_hidden = partial[k] + dqb[k] + dot(d_keys, wt[k, pl.ds(0, kv_width), :])
            normed = xb[k, rows, :].astype(F32) * inverse
            moment = d_hidden * normed
            gsum[k] += moment[0:8] + moment[8:16]
            d_inputs = inverse * (d_hidden * gf[k, 0:1, :] - normed * mean)
            go[k, rows, :] = (gb[k, rows, :].astype(F32) + d_inputs).astype(BF16)
            if k == 1:

                @pl.when(first)
                def _():
                    send_parts()

            if k % 2 == 1:
                send_grads(k // 2)

        @pl.when(sec > 0)
        def _():
            send_parts()

        @pl.when(late & (step == late_turn))
        def _():
            spread_h()

        @pl.when(
            middle
            & (
                (step == relay_turn)
                | ((step == 0) & (relay_turn < 0))
                | ((step == pieces - 1) & (relay_turn >= pieces))
            )
        )
        def _():
            relay_h()

        return carry

    lax.fori_loop(0, pieces, backward, 0)

    def gain_block(dp):
        column = dp * block
        return gs.at[
            column // CHUNK, :, pl.ds(pl.multiple_of(column % CHUNK, block), block)
        ]

    @pl.when(late)
    def _():
        relay_h()

    @pl.when(jnp.logical_not(early))
    def _():
        transpose_h()

    def product(g, part):
        low, high = GROUPS[g]
        tokens = (high - low) * T
        d_kv = dg[:, pl.ds(low * T, tokens), :].reshape(n_dp * tokens, cols)
        return dot(ht[part, pl.ds(n_dp * low * T, n_dp * tokens)], d_kv)

    final = len(GROUPS) - 1
    for g, (low, high) in enumerate(GROUPS):
        wait_for(dg.at[others, pl.ds(low * T, (high - low) * T)], d_recv.at[g])
        if g < final:
            for c in range(CHUNK // 256):
                part = pl.ds(c * 256, 256)
                wacc[part, :] = product(g, part) + (wacc[part, :] if g > 0 else 0.0)
    for jy in (2, 1, 3, 0) if grid_y == 4 else (0,):
        peer_y = (y + jy) % grid_y
        part = pl.ds(pl.multiple_of(peer_y * block, block), block)
        total = wacc[part, :] + product(final, part)
        if jy == 0:
            out_w[:, pl.ds(pl.multiple_of(y * cols, cols), cols)] = total.astype(BF16)
        else:
            eo[jy] = total.astype(BF16)
            to_peer(
                x * grid_y + peer_y, eo.at[jy], eg.at[jy], e_send, e_recv.at[jy]
            ).start()

    for k in range(KV_HEADS):
        total = jnp.sum(gsum[k], 0, keepdims=True).astype(BF16).astype(F32)
        gs[k] = jnp.broadcast_to(total, (8, CHUNK))
    own_gain = pltpu.make_async_copy(gain_block(me), gg.at[0], in_sem.at[1])
    own_gain.start()
    for j, dp, peer_x, peer_y in peers[1:]:
        to_peer(dp, gain_block(dp), gg.at[j], s_send, s_recv).start()

    own_gain.wait()
    wait_for(gg.at[others], s_recv)
    gain_total = gg[0]
    for j in range(1, n_dp):
        gain_total = gain_total + gg[j]
    out_g[...] = gain_total[0:1]

    for jy in range(1, grid_y):
        wait_for(eg.at[jy], e_recv.at[jy])
        source_y = (y + grid_y - jy) % grid_y
        out_w[:, pl.ds(pl.multiple_of(source_y * cols, cols), cols)] = eg[jy]

    if grid_y > 1:
        wait_for(eo.at[pl.ds(1, grid_y - 1)], e_send)
        for i in range(2):
            wait_for(hg.at[0], hy_send.at[i])
            wait_for(hg.at[2, :, pl.ds(i * half, half)], hr_send.at[i])
    wait_for(hg.at[0, pl.ds(1, KV_HEADS - 1)], hx_send)
    wait_for(dg.at[others], d_send)
    wait_for(gg.at[others], s_send)

    @pl.when(sec < n_sec - 1)
    def _():
        wait_for(xo, f_send)

    @pl.when(sec > 0)
    def _():
        wait_for(go, g_send)


def local(n_sec, n_dp, tokens, upstream, gains, w_kv, doc_lengths, seg_lengths, block_mask):
    seq_len, width = tokens.shape[1:]
    pieces = seq_len // T
    kv2 = w_kv.shape[2]
    block = width // n_dp
    grid_y = n_dp // KV_HEADS
    cols = kv2 // grid_y
    any_spec = pl.BlockSpec(memory_space=pl.ANY)
    vmem = pl.BlockSpec(memory_space=pltpu.VMEM)
    smem = pl.BlockSpec(memory_space=pltpu.SMEM)
    features = (KV_HEADS, seq_len, CHUNK)
    dma = pltpu.SemaphoreType.DMA
    grad_weight, grad_gain = pl.pallas_call(
        functools.partial(kernel, n_sec, n_dp),
        out_shape=(
            jax.ShapeDtypeStruct((block, kv2), BF16),
            jax.ShapeDtypeStruct((1, block), F32),
        ),
        in_specs=[any_spec, any_spec, vmem, any_spec, smem, smem, vmem],
        out_specs=(vmem, vmem),
        scratch_shapes=[
            pltpu.VMEM(features, BF16),
            pltpu.VMEM(features, BF16),
            pltpu.VMEM(features, BF16),
            pltpu.VMEM(features, BF16),
            pltpu.VMEM(features, BF16),
            pltpu.VMEM((KV_HEADS, CHUNK, kv2), BF16),
            pltpu.VMEM((KV_HEADS, kv2, CHUNK), BF16),
            pltpu.VMEM((PAD + seq_len, kv2 // 2), BF16),
            pltpu.VMEM((PAD + seq_len, kv2 // 2), BF16),
            pltpu.VMEM((KV_HEADS, PAD + seq_len, HEAD_DIM), F32),
            pltpu.VMEM((KV_HEADS, PAD + seq_len, HEAD_DIM), F32),
            pltpu.VMEM((pieces, KV_HEADS, GROUP * T, WINDOW), F32),
            pltpu.VMEM((pieces, KV_HEADS, WINDOW, GROUP * T), F32),
            pltpu.VMEM((KV_HEADS, T, CHUNK), F32),
            pltpu.VMEM((seq_len, 128), F32),
            pltpu.VMEM((pieces, T, WINDOW), F32),
            pltpu.VMEM((KV_HEADS, 8, CHUNK), F32),
            pltpu.VMEM((KV_HEADS, 8, CHUNK), F32),
            pltpu.VMEM((KV_HEADS, 8, CHUNK), F32),
            pltpu.VMEM((grid_y, KV_HEADS, seq_len, CHUNK), BF16),
            pltpu.VMEM((CHUNK, n_dp * seq_len), BF16),
            pltpu.VMEM((grid_y, seq_len, cols), BF16),
            pltpu.VMEM((n_dp, seq_len, cols), BF16),
            pltpu.VMEM((CHUNK, cols), F32),
            pltpu.VMEM((grid_y, block, cols), BF16),
            pltpu.VMEM((grid_y, block, cols), BF16),
            pltpu.VMEM((n_dp, 8, block), F32),
            dma((KV_HEADS,)),
            dma((KV_HEADS,)),
            dma,
            dma((pieces, KV_HEADS)),
            dma,
            dma((pieces, KV_HEADS // 2)),
            dma,
            dma,
            dma((2,)),
            dma((2,)),
            dma((2,)),
            dma((2,)),
            dma,
            dma((len(GROUPS),)),
            dma,
            dma((grid_y,)),
            dma,
            dma,
        ],
        compiler_params=pltpu.CompilerParams(
            collective_id=0, has_side_effects=True, vmem_limit_bytes=60 * 1024 * 1024
        ),
        cost_estimate=pl.CostEstimate(
            flops=7 * 10**9, bytes_accessed=12 * 2**20, transcendentals=10**6
        ),
        name="relay",
    )(tokens, upstream, gains, w_kv, doc_lengths, seg_lengths, block_mask.transpose(1, 0, 2))
    return grad_weight.astype(F32)[None], grad_gain


def solution(mesh):
    placed = (
        P("dp", None, None),
        P("dp", None, None),
        P("section", None),
        P("section", None, None),
        P("dp", None),
        P("dp", None),
        P("dp", None, None),
    )
    return jax.shard_map(
        functools.partial(local, mesh.shape["section"], mesh.shape["dp"]),
        mesh=mesh,
        in_specs=placed,
        out_specs=(P("section", "dp", None), P("section", "dp")),
        check_vma=False,
    )
```
